32 devices in a mesh: bx: 4 (over z), by: 2 (over y), bz: 4 (over x, core).
Axes of the slice: x: 2, y: 2, z: 4, core: 2. Of those that a mesh axis runs over, the one named last changes fastest.
Arguments:
- positions: float32 [3, 131072], P(None, ('bx', 'by', 'bz')), may hold values from -15 to 55, as said below
- velocities: float32 [3, 131072], P(None, ('bx', 'by', 'bz')), may hold values from -6 to 6
- species: int32 [131072], P(('bx', 'by', 'bz')), may hold values 0 or 1
- corner_slot: int32 [2, 8, 131072], P(None, None, ('bx', 'by', 'bz')), may hold values from 0 to 255, as said below
- corner_weight: float32 [8, 131072], P(None, ('bx', 'by', 'bz')), may hold values from 0 to 1, as said below
- slot_cell: int32 [3, 256, 256], P(None, ('bx', 'by', 'bz')), may hold values from 0 to 63, as said below
- bond_pairs: int32 [2, 122880], P(None, ('bx', 'by', 'bz')), may hold values from 0 to 4095, as said below
Outputs:
- new_positions: float32 [3, 131072], P(None, ('bx', 'by', 'bz'))
- new_velocities: float32 [3, 131072], P(None, ('bx', 'by', 'bz'))
- smoothed: float32 [2, 64, 128, 256], P(None, 'bx', 'by', 'bz')
The draws below stay inside these ranges and needn't reach their ends.
Inputs may be any that keep to these rules, and one draw needn't show every extreme that they name: `corner_slot`: row 0 is below 8 and row 1 below 256. For every owner and destination brick the named slots are those below a count of at least 32; the count is 256 for some destination of every owner, and for some brick of every z plane from all owners of that plane. `corner_weight`: for each bead the eight weights are the trilinear weights of a point inside a cell, corner c taking the upper side along x, y, z by bits 4, 2, 1 of c; they sum to one. `slot_cell`: row 0 is below 16, row 1 below 64, row 2 below 64. `bond_pairs`: bonds join beads of one device into chains of 16 beads; each bead lies in at most two bonds. `positions`: bonded beads stand at distance 1.
All inputs are finite; a program needn't handle non-finite values. No bound on the sum of `species` on one device may be relied on, other than what follows from the above.
Results may differ from the reference program's by a relative error of at most 0.0003.
Values sent between devices are 32-bit elements; how exact they have to be, the bound alone decides.
No kernel may reach another device: no remote copies, remote signals or barrier semaphores. Data moves between devices by JAX's collectives and lax.ppermute only.
A program may use at most 128 MiB of HBM per device.

```python
import math
import jax
import jax.numpy as jnp

CX = 16
CY = 64
CZ = 64
BEADS_DEV = 4096
MOL = 16
REACH = 3
SWEEPS = 4
SLOTS = 256
PLANE = 8
NX = 64
NY = 128
NZ = 256
BEADS = 131072
BONDS_DEV = 3840
BONDS = 122880
N_BY = 2
N_BZ = 4
DEVICES = 32


def chain_layout(key, device):
    return jax.random.permutation(jax.random.fold_in(jax.random.fold_in(key, 4242), device), BEADS_DEV).astype(jnp.int32)


def draw_bond_pairs(key, part):

    def one_device(device):
        order = chain_layout(key, device).reshape(BEADS_DEV // MOL, MOL)
        return jnp.stack([order[:, :-1].reshape(-1), order[:, 1:].reshape(-1)])
    blocks = jax.vmap(one_device)(jnp.arange(DEVICES, dtype=jnp.int32))
    return jnp.transpose(blocks, (1, 0, 2)).reshape(2, -1).astype(jnp.int32)


def draw_positions(key, part):

    def one_device(device):
        branch_key = jax.random.fold_in(jax.random.fold_in(key, 5151), device)
        key_steps, key_starts = jax.random.split(branch_key, 2)
        chains = BEADS_DEV // MOL
        steps = jax.random.normal(key_steps, (chains, MOL, 3), jnp.float32)
        steps = steps / jnp.sqrt(jnp.sum(steps * steps, axis=-1, keepdims=True) + 1e-12)
        first_mask = (jnp.arange(MOL) > 0).astype(jnp.float32)[None, :, None]
        steps = steps * first_mask
        starts = jax.random.uniform(key_starts, (chains, 1, 3), jnp.float32, 0.0, 40.0)
        coords = starts + jnp.cumsum(steps, axis=1)
        order = chain_layout(key, device)
        return jnp.zeros((3, BEADS_DEV), jnp.float32).at[:, order].set(coords.reshape(-1, 3).T)
    blocks = jax.vmap(one_device)(jnp.arange(DEVICES, dtype=jnp.int32))
    return jnp.transpose(blocks, (1, 0, 2)).reshape(3, -1)


def draw_corner_weight(key, part):
    fraction = jax.random.uniform(key, (3, BEADS_DEV * DEVICES), jnp.float32)
    corners = []
    for corner in range(8):
        weight_x = fraction[0] if corner >> 2 & 1 else 1.0 - fraction[0]
        weight_y = fraction[1] if corner >> 1 & 1 else 1.0 - fraction[1]
        weight_z = fraction[2] if corner & 1 else 1.0 - fraction[2]
        corners.append(weight_x * weight_y * weight_z)
    return jnp.stack(corners)


def draw_slot_cell(key, part):
    rows = DEVICES * PLANE
    local_x = jax.random.randint(jax.random.fold_in(key, 7070), (rows, SLOTS), 0, CX)
    local_y = jax.random.randint(jax.random.fold_in(key, 7171), (rows, SLOTS), 0, CY)
    local_z = jax.random.randint(jax.random.fold_in(key, 7272), (rows, SLOTS), 0, CZ)
    return jnp.stack([local_x, local_y, local_z]).astype(jnp.int32)


def draw_corner_slot(key, part):

    def one_device(device):
        device_key = jax.random.fold_in(jax.random.fold_in(key, 6060), device)
        key_counts, key_picks = jax.random.split(device_key)
        plane_z = device % N_BZ
        home = device // N_BZ
        crowded = jax.random.randint(jax.random.fold_in(jax.random.fold_in(key, 6161), plane_z), (), 0, PLANE)
        counts = jax.random.randint(key_counts, (PLANE,), SLOTS // 8, SLOTS // 2 + 1)
        brick_index = jnp.arange(PLANE, dtype=jnp.int32)
        counts = jnp.where((brick_index == home) | (brick_index == crowded), SLOTS, counts).astype(jnp.int32)
        running = jnp.cumsum(counts).astype(jnp.int32)
        picks = jax.random.randint(key_picks, (8, BEADS_DEV), 0, running[-1])
        target = jnp.searchsorted(running, picks, side='right').astype(jnp.int32)
        within = picks - (running[target] - counts[target])
        return jnp.stack([target, within]).astype(jnp.int32)
    blocks = jax.vmap(one_device)(jnp.arange(DEVICES, dtype=jnp.int32))
    return jnp.transpose(blocks, (1, 2, 0, 3)).reshape(2, 8, -1).astype(jnp.int32)


def set_ends(entries, own_key, smallest, largest):
    extent = entries.shape
    index_at = [jax.random.randint(jax.random.fold_in(own_key, axis), (), 0, extent[axis]) for axis in range(len(extent))]
    entries = entries.at[tuple(index_at)].set(smallest)
    longest = extent.index(max(extent))
    index_at[longest] = (index_at[longest] + 1) % extent[longest]
    return entries.at[tuple(index_at)].set(largest)


def steps_of(rng, shape, cuts, least, top_value):
    def one(dim, shards_of):
        draws = jax.random.uniform(jax.random.fold_in(jax.random.fold_in(rng, 6), dim), (shards_of,), jnp.float32, least / len(cuts), top_value / len(cuts))
        return jnp.repeat(jnp.exp(draws), shape[dim] // shards_of).reshape((-1,) + (1,) * (len(shape) - dim - 1))

    loudness = one(*cuts[0])
    for cut in cuts[1:]:
        loudness = loudness * one(*cut)
    return loudness


def scatter_about(rng, shape, spread, reach, cuts=(), kind=jnp.bfloat16):
    array = spread * jax.random.normal(rng, shape, jnp.float32)
    if cuts:
        array = array * steps_of(rng, shape, cuts, -0.22, 0.18)
    return jnp.clip(array, -reach, reach).astype(kind)


def setup_inputs(seed: int = 0) -> dict:
    splits = jax.random.split(jax.random.key(seed), 8)
    return {
        "positions": draw_positions(jax.random.fold_in(splits[7], 71), 0),
        "velocities": scatter_about(splits[1], (3, BEADS), 1.0, 6.0, ((1, 32),), jnp.float32),
        "species": set_ends((jax.random.randint(splits[2], (BEADS,), 0, 2) < 1).astype(jnp.int32), jax.random.fold_in(splits[2], 1), 0, 1),
        "corner_slot": draw_corner_slot(jax.random.fold_in(splits[7], 71), 0),
        "corner_weight": draw_corner_weight(jax.random.fold_in(splits[7], 71), 0),
        "slot_cell": draw_slot_cell(jax.random.fold_in(splits[7], 71), 0),
        "bond_pairs": draw_bond_pairs(jax.random.fold_in(splits[7], 71), 0),
    }


spread_cells = 1.0
mixing = 10.0
stiffness = 5.0
time_step = 0.1
bond_length = 1.0


def gauss_taps():
    raw_list = [math.exp(-0.5 * (offset - REACH) ** 2 / spread_cells ** 2) for offset in range(2 * REACH + 1)]
    tap_total = sum(raw_list)
    return [entry / tap_total for entry in raw_list]


def smooth_periodic(field, axis):
    taps = gauss_taps()
    result = jnp.zeros_like(field)
    for offset in range(2 * REACH + 1):
        result = result + taps[offset] * jnp.roll(field, REACH - offset, axis=axis)
    return result


def constrain(anchor, moved, first, second):
    separation = anchor[:, first] - anchor[:, second]
    for repeat in range(SWEEPS):
        stretch = moved[:, first] - moved[:, second]
        excess = jnp.sum(stretch * stretch, axis=0) - bond_length * bond_length
        intersection = jnp.maximum(jnp.sum(stretch * separation, axis=0), 0.5 * bond_length * bond_length)
        factor = excess / (4.0 * intersection)
        shifted = factor * separation
        moved = moved.at[:, first].add(-shifted).at[:, second].add(shifted)
    return moved


def reference(positions, velocities, species, corner_slot, corner_weight, slot_cell, bond_pairs):
    bead_index = jnp.arange(BEADS, dtype=jnp.int32)
    owner = bead_index // BEADS_DEV
    plane_src = owner // N_BZ
    plane_z = owner % N_BZ
    target = corner_slot[0]
    within = corner_slot[1]
    row_index = ((target * N_BZ + plane_z[None, :]) * PLANE + plane_src[None, :]).astype(jnp.int32)
    local_x = slot_cell[0][row_index, within]
    local_y = slot_cell[1][row_index, within]
    local_z = slot_cell[2][row_index, within]
    cell_x = (target // N_BY) * CX + local_x
    cell_y = (target % N_BY) * CY + local_y
    cell_z = plane_z[None, :] * CZ + local_z
    global_cell = ((cell_x * NY + cell_y) * NZ + cell_z).astype(jnp.int32)
    is_lipid = (species == 0)[None, :]
    weight_a = jnp.where(is_lipid, corner_weight, 0.0)
    weight_b = jnp.where(is_lipid, 0.0, corner_weight)
    density = jnp.zeros((2, NX * NY * NZ), jnp.float32)
    density = density.at[0, global_cell.reshape(-1)].add(weight_a.reshape(-1))
    density = density.at[1, global_cell.reshape(-1)].add(weight_b.reshape(-1))
    density = density * (CX * CY * CZ / BEADS_DEV)
    filtered = density.reshape(2, NX, NY, NZ)
    for axis in (1, 2, 3):
        filtered = smooth_periodic(filtered, axis)
    combined = filtered[0] + filtered[1]
    potential = jnp.stack([mixing * filtered[1] + stiffness * combined, mixing * filtered[0] + stiffness * combined])
    components = []
    for axis in (1, 2, 3):
        slope = (jnp.roll(potential, -1, axis=axis) - jnp.roll(potential, 1, axis=axis)) * 0.5
        table = slope.reshape(2, -1)
        picked = jnp.where(is_lipid, table[0][global_cell], table[1][global_cell])
        components.append(-jnp.sum(corner_weight * picked, axis=0))
    force = jnp.stack(components)
    half = velocities + 0.5 * time_step * force
    moved = positions + time_step * half
    bond_owner = jnp.arange(BONDS, dtype=jnp.int32) // BONDS_DEV
    first = (bond_pairs[0] + bond_owner * BEADS_DEV).astype(jnp.int32)
    second = (bond_pairs[1] + bond_owner * BEADS_DEV).astype(jnp.int32)
    moved = constrain(positions, moved, first, second)
    new_velocities = (moved - positions) / time_step
    return moved, new_velocities, filtered
```

```python
import math

import jax
import jax.numpy as jnp
from jax import lax
from jax.experimental import pallas as pl
from jax.experimental.pallas import tpu as pltpu
from jax.sharding import PartitionSpec as P

CX = 16
CY = 64
CZ = 64
BEADS_DEV = 4096
REACH = 3
SWEEPS = 4


spread_cells = 1.0
mixing = 10.0
stiffness = 5.0
time_step = 0.1
bond_length = 1.0


def extended_2(cells, sides, width):
    for axis, dim in sides:
        count = lax.axis_size(axis)
        head = lax.slice_in_dim(cells, 0, width, axis=dim)
        tail = lax.slice_in_dim(cells, cells.shape[dim] - width, cells.shape[dim], axis=dim)
        cells = jnp.concatenate(
            [
                lax.ppermute(tail, axis, [(i, (i + 1) % count) for i in range(count)]),
                cells,
                lax.ppermute(head, axis, [((i + 1) % count, i) for i in range(count)]),
            ],
            axis=dim,
        )
    return cells


def gauss_taps():
    raw_list = [
        math.exp(-0.5 * (offset - REACH) ** 2 / spread_cells**2) for offset in range(2 * REACH + 1)
    ]
    tap_total = sum(raw_list)
    return [entry / tap_total for entry in raw_list]


def smooth_along(extended, axis):
    taps = gauss_taps()
    length = extended.shape[axis] - 2 * REACH
    result = jnp.zeros_like(lax.slice_in_dim(extended, 0, length, axis=axis))
    for offset in range(2 * REACH + 1):
        result = result + taps[offset] * lax.slice_in_dim(
            extended, offset, offset + length, axis=axis
        )
    return result


def smooth_brick(density, margin):
    width = REACH + margin
    field = smooth_along(extended_2(density, (("bx", 1),), width), 1)
    field = smooth_along(extended_2(field, (("by", 2),), width), 2)
    return smooth_along(extended_2(field, (("bz", 3),), width), 3)


LANES = 128
VMEM_LIMIT = 56 * 1024 * 1024
f32 = jnp.float32
bf16 = jnp.bfloat16


def parts_of(values, count):
    parts = []
    for _ in range(count):
        part = values.astype(bf16)
        parts.append(part)
        values = values - part.astype(f32)
    return parts


def one_hot(index, size):
    rows = lax.broadcasted_iota(jnp.int32, (size, index.shape[1]), 0)
    return jnp.where(rows == index, 1.0, 0.0).astype(bf16)


def dot_nn(left, right):
    return lax.dot_general(left, right, (((1,), (0,)), ((), ())), preferred_element_type=f32)


def dot_nt(left, right):
    return lax.dot_general(left, right, (((1,), (1,)), ((), ())), preferred_element_type=f32)


def chunk_of(length, most):
    tiles = length // LANES
    best = max(t for t in range(1, most + 1) if tiles % t == 0)
    return best * LANES


def corner_keys(species, corner_slot, corner, where, plane, blocks):
    brick = corner_slot[0, pl.ds(corner, 1), where]
    slot = corner_slot[1, pl.ds(corner, 1), where]
    block = slot // LANES
    high = (species * blocks + block) * plane + brick
    return high, slot - block * LANES


def deposit_kernel(species, corner_slot, corner_weight, packets):
    plane, slots = packets.shape[1:]
    blocks = slots // LANES
    highs = 2 * blocks * plane
    beads = corner_weight.shape[1]
    step = chunk_of(beads, 4)

    def body(j, total):
        where = pl.ds(pl.multiple_of(j * step, step), step)
        kind = species[:, where]
        for corner in range(8):
            high, low = corner_keys(kind, corner_slot, corner, where, plane, blocks)
            weight = corner_weight[pl.ds(corner, 1), where]
            rows = lax.broadcasted_iota(jnp.int32, (highs, step), 0) == high
            left = [jnp.where(rows, p.astype(f32), 0.0).astype(bf16) for p in parts_of(weight, 2)]
            total = total + dot_nt(jnp.concatenate(left, axis=0), one_hot(low, LANES))
        return total

    total = lax.fori_loop(0, beads // step, body, jnp.zeros((2 * highs, LANES), f32))
    total = total[:highs] + total[highs:]
    for kind in range(2):
        for block in range(blocks):
            start = (kind * blocks + block) * plane
            packets[kind, :, block * LANES : (block + 1) * LANES] = total[start : start + plane]


def deposit(species, corner_slot, corner_weight, plane, slots):
    return pl.pallas_call(
        deposit_kernel,
        out_shape=jax.ShapeDtypeStruct((2, plane, slots), f32),
        compiler_params=pltpu.CompilerParams(vmem_limit_bytes=VMEM_LIMIT),
    )(species, corner_slot, corner_weight)


def to_rows(store, base, row):
    for tile in range(row.shape[1] // LANES):
        store[pl.ds(base + tile, 1), :] = row[:, tile * LANES : (tile + 1) * LANES]


def finish_kernel(
    species,
    corner_slot,
    corner_weight,
    slopes,
    positions,
    velocities,
    bonds,
    new_positions,
    new_velocities,
    table,
    shift,
    anchor,
    hot,
    separation,
):
    plane, slots = slopes.shape[1:]
    blocks = slots // LANES
    highs = 2 * blocks * plane
    beads = corner_weight.shape[1]
    bead_rows = beads // LANES
    count = bonds.shape[1]

    for axis in range(3):
        for kind in range(2):
            for block in range(blocks):
                start = (axis * 2 * blocks + kind * blocks + block) * plane
                for at, part in enumerate(
                    parts_of(slopes[kind * 3 + axis, :, block * LANES : (block + 1) * LANES], 2)
                ):
                    table[start : start + plane, at * LANES : (at + 1) * LANES] = part.astype(f32)
    slope_table = table[...].astype(bf16)

    step = chunk_of(beads, 4)

    def force_body(j, carry):
        where = pl.ds(pl.multiple_of(j * step, step), step)
        kind = species[:, where]
        total = jnp.zeros((3 * highs, step), f32)
        for corner in range(8):
            high, low = corner_keys(kind, corner_slot, corner, where, plane, blocks)
            weight = corner_weight[pl.ds(corner, 1), where]
            rows = lax.broadcasted_iota(jnp.int32, (highs, step), 0) == high
            weights = jnp.where(rows, weight, 0.0)
            hot_low = one_hot(low, LANES)
            picked = dot_nn(slope_table, jnp.concatenate([hot_low, hot_low], axis=0))
            total = total + picked * jnp.concatenate([weights] * 3, axis=0)
        for axis in range(3):
            force = -jnp.sum(total[axis * highs : (axis + 1) * highs], axis=0, keepdims=True)
            half = velocities[pl.ds(axis, 1), where] + 0.5 * time_step * force
            to_rows(shift, axis * bead_rows + j * (step // LANES), time_step * half)
            to_rows(anchor, axis * bead_rows + j * (step // LANES), positions[pl.ds(axis, 1), where])
        return carry

    lax.fori_loop(0, beads // step, force_body, 0)

    bond_step = chunk_of(count, 6)
    bond_rows = 3 * bead_rows
    anchor_parts = parts_of(anchor[...], 3)
    anchor_table = jnp.concatenate(anchor_parts, axis=1)

    def ends(side, where):
        index = bonds[pl.ds(side, 1), where]
        high = index // LANES
        return lax.broadcasted_iota(jnp.int32, (bead_rows, bond_step), 0) == high, index - high * LANES

    def select(rows, picked):
        return [
            jnp.sum(
                jnp.where(rows, picked[axis * bead_rows : (axis + 1) * bead_rows], 0.0),
                axis=0,
                keepdims=True,
            )
            for axis in range(3)
        ]

    for j in range(count // bond_step):
        where = slice(j * bond_step, (j + 1) * bond_step)
        found = []
        for side in range(2):
            rows, low = ends(side, where)
            hot_low = one_hot(low, LANES)
            hot[side, :, where] = hot_low
            found.append(select(rows, dot_nn(anchor_table, jnp.concatenate([hot_low] * 3, axis=0))))
        for axis in range(3):
            separation[axis : axis + 1, where] = found[0][axis] - found[1][axis]

    def sweep(repeat, carry):
        shift_table = jnp.concatenate(parts_of(shift[...], 2), axis=1)
        total = jnp.zeros((2 * bond_rows, LANES), f32)
        for j in range(count // bond_step):
            where = slice(j * bond_step, (j + 1) * bond_step)
            hots = [hot[side, :, where] for side in range(2)]
            rows = [ends(side, where)[0] for side in range(2)]
            found = [
                select(rows[side], dot_nn(shift_table, jnp.concatenate([hots[side]] * 2, axis=0)))
                for side in range(2)
            ]
            apart = [separation[axis : axis + 1, where] for axis in range(3)]
            stretch = [apart[axis] + (found[0][axis] - found[1][axis]) for axis in range(3)]
            excess = sum(s * s for s in stretch) - bond_length * bond_length
            along = sum(s * a for s, a in zip(stretch, apart))
            factor = excess / (4.0 * jnp.maximum(along, 0.5 * bond_length * bond_length))
            moves = [parts_of(factor * apart[axis], 2) for axis in range(3)]
            for side in range(2):
                sign = 1.0 if side else -1.0
                left = jnp.concatenate(
                    [
                        jnp.where(rows[side], sign * moves[axis][part].astype(f32), 0.0).astype(bf16)
                        for part in range(2)
                        for axis in range(3)
                    ],
                    axis=0,
                )
                total = total + dot_nt(left, hots[side])
        shift[...] = shift[...] + total[:bond_rows] + total[bond_rows:]
        return carry

    lax.fori_loop(0, SWEEPS, sweep, 0)

    for axis in range(3):
        for tile in range(bead_rows):
            row = slice(axis * bead_rows + tile, axis * bead_rows + tile + 1)
            where = slice(tile * LANES, (tile + 1) * LANES)
            move = shift[row, :]
            new_positions[axis : axis + 1, where] = anchor[row, :] + move
            new_velocities[axis : axis + 1, where] = move / time_step


def finish(species, corner_slot, corner_weight, slopes, positions, velocities, bonds):
    beads = positions.shape[1]
    count = bonds.shape[1]
    plane, slots = slopes.shape[1:]
    highs = 2 * (slots // LANES) * plane
    return pl.pallas_call(
        finish_kernel,
        out_shape=[jax.ShapeDtypeStruct((3, beads), f32)] * 2,
        scratch_shapes=[
            pltpu.VMEM((3 * highs, 2 * LANES), f32),
            pltpu.VMEM((3 * beads // LANES, LANES), f32),
            pltpu.VMEM((3 * beads // LANES, LANES), f32),
            pltpu.VMEM((2, LANES, count), bf16),
            pltpu.VMEM((3, count), f32),
        ],
        compiler_params=pltpu.CompilerParams(vmem_limit_bytes=VMEM_LIMIT),
    )(species, corner_slot, corner_weight, slopes, positions, velocities, bonds)

def on_device(positions, velocities, species, corner_slot, corner_weight, slot_cell, bond_pairs):
    plane = slot_cell.shape[1]
    slots = slot_cell.shape[2]
    cells = CX * CY * CZ
    species = species.reshape(1, -1)
    packets = deposit(species, corner_slot, corner_weight, plane, slots)
    received = lax.all_to_all(
        packets, ("bx", "by"), split_axis=1, concat_axis=1, tiled=True
    )
    flat_cells = ((slot_cell[0] * CY + slot_cell[1]) * CZ + slot_cell[2]).reshape(-1)
    density = jnp.zeros((2, cells), jnp.float32).at[:, flat_cells].add(received.reshape(2, -1))
    density = density * (CX * CY * CZ / BEADS_DEV)
    density = density.reshape(2, CX, CY, CZ)
    margin = 1
    filtered = smooth_brick(density, margin)
    smoothed = filtered[:, margin : margin + CX, margin : margin + CY, margin : margin + CZ]
    combined = filtered[0] + filtered[1]
    potential = jnp.stack(
        [mixing * filtered[1] + stiffness * combined, mixing * filtered[0] + stiffness * combined]
    )
    slope_x = (potential[:, 2:, 1:-1, 1:-1] - potential[:, :-2, 1:-1, 1:-1]) * 0.5
    slope_y = (potential[:, 1:-1, 2:, 1:-1] - potential[:, 1:-1, :-2, 1:-1]) * 0.5
    slope_z = (potential[:, 1:-1, 1:-1, 2:] - potential[:, 1:-1, 1:-1, :-2]) * 0.5
    slopes = jnp.stack([slope_x, slope_y, slope_z], axis=1).reshape(6, cells)
    outgoing = slopes[:, flat_cells]
    returned = lax.all_to_all(
        outgoing.reshape(6, plane, slots), ("bx", "by"), split_axis=1, concat_axis=1, tiled=True
    )
    moved, new_velocities = finish(
        species, corner_slot, corner_weight, returned, positions, velocities, bond_pairs
    )
    return (moved, new_velocities, smoothed)


def solution(mesh):
    in_specs = (
        P(None, ("bx", "by", "bz")),
        P(None, ("bx", "by", "bz")),
        P(("bx", "by", "bz")),
        P(None, None, ("bx", "by", "bz")),
        P(None, ("bx", "by", "bz")),
        P(None, ("bx", "by", "bz"), None),
        P(None, ("bx", "by", "bz")),
    )
    out_specs = (
        P(None, ("bx", "by", "bz")),
        P(None, ("bx", "by", "bz")),
        P(None, "bx", "by", "bz"),
    )
    return jax.shard_map(
        on_device, mesh=mesh, in_specs=in_specs, out_specs=out_specs, check_vma=False
    )
```

```python
import functools
import math

import jax
import jax.numpy as jnp
from jax import lax
from jax.experimental import pallas as pl
from jax.experimental.pallas import tpu as pltpu
from jax.sharding import PartitionSpec as P

CX = 16
CY = 64
CZ = 64
BEADS_DEV = 4096
REACH = 3
SWEEPS = 4


spread_cells = 1.0
mixing = 10.0
stiffness = 5.0
time_step = 0.1
bond_length = 1.0


def gauss_taps():
    raw_list = [
        math.exp(-0.5 * (offset - REACH) ** 2 / spread_cells**2) for offset in range(2 * REACH + 1)
    ]
    tap_total = sum(raw_list)
    return [entry / tap_total for entry in raw_list]


LANES = 128
VMEM_LIMIT = 56 * 1024 * 1024
f32 = jnp.float32
bf16 = jnp.bfloat16


def parts_of(values, count):
    parts = []
    for _ in range(count):
        part = values.astype(bf16)
        parts.append(part)
        values = values - part.astype(f32)
    return parts


def one_hot(index, size):
    rows = lax.broadcasted_iota(jnp.int32, (size, index.shape[1]), 0)
    return jnp.where(rows == index, 1.0, 0.0).astype(bf16)


def dot_nn(left, right):
    return lax.dot_general(left, right, (((1,), (0,)), ((), ())), preferred_element_type=f32)


def dot_nt(left, right):
    return lax.dot_general(left, right, (((1,), (1,)), ((), ())), preferred_element_type=f32)


def chunk_of(length, most):
    tiles = length // LANES
    best = max(t for t in range(1, most + 1) if tiles % t == 0)
    return best * LANES


def corner_keys(species, corner_slot, corner, where, plane, blocks):
    brick = corner_slot[0, pl.ds(corner, 1), where]
    slot = corner_slot[1, pl.ds(corner, 1), where]
    block = slot // LANES
    high = (species * blocks + block) * plane + brick
    return high, slot - block * LANES


def deposit_kernel(bricks, species, corner_slot, corner_weight, packets, sums):
    plane, _, slots = packets.shape
    blocks = slots // LANES
    highs = 2 * blocks * plane
    beads = corner_weight.shape[1]
    step = chunk_of(beads, 4)
    count_x, count_y = bricks.counts

    def body(j, total):
        where = pl.ds(pl.multiple_of(j * step, step), step)
        kind = species[:, where]
        for corner in range(8):
            high, low = corner_keys(kind, corner_slot, corner, where, plane, blocks)
            weight = corner_weight[pl.ds(corner, 1), where]
            rows = lax.broadcasted_iota(jnp.int32, (highs, step), 0) == high
            left = [jnp.where(rows, p.astype(f32), 0.0).astype(bf16) for p in parts_of(weight, 2)]
            total = total + dot_nt(jnp.concatenate(left, axis=0), one_hot(low, LANES))
        return total

    total = lax.fori_loop(0, beads // step, body, jnp.zeros((2 * highs, LANES), f32))
    sums[...] = total[:highs] + total[highs:]

    def hand_out(target, carry):
        for near, (step_x, step_y) in enumerate(bricks.offsets):
            brick = lax.rem(target // count_y + step_x, count_x) * count_y + lax.rem(
                lax.rem(target, count_y) + step_y, count_y
            )
            for kind in range(2):
                for block in range(blocks):
                    packets[target, near * 2 + kind : near * 2 + kind + 1, block * LANES : (block + 1) * LANES] = sums[
                        pl.ds((kind * blocks + block) * plane + brick, 1), :
                    ]
        return carry

    lax.fori_loop(0, plane, hand_out, 0, unroll=plane <= 8)


def deposit(bricks, species, corner_slot, corner_weight, plane, slots):
    return pl.pallas_call(
        functools.partial(deposit_kernel, bricks),
        out_shape=jax.ShapeDtypeStruct((plane, 2 * len(bricks.offsets), slots), f32),
        scratch_shapes=[pltpu.VMEM((2 * slots // LANES * plane, LANES), f32)],
        compiler_params=pltpu.CompilerParams(vmem_limit_bytes=VMEM_LIMIT),
    )(species, corner_slot, corner_weight)


HALO = REACH + 1
PAD = 8


class Bricks:
    def __init__(self, count_x, count_y):
        self.counts = (count_x, count_y)
        self.sides_x = self.sides(count_x)
        self.sides_y = self.sides(count_y)
        self.offsets = [(x, y) for y in self.sides_y for x in self.sides_x]

    @staticmethod
    def sides(count):
        found = {}
        for side in (0, 1, -1):
            found.setdefault(side % count, []).append(side)
        return found


def tap_of(distance):
    taps = gauss_taps()
    result = jnp.zeros(distance.shape, f32)
    for far in range(REACH, -1, -1):
        result = jnp.where(distance == far, taps[REACH + far], result)
    return result


def filter_rows(load):
    taps = gauss_taps()
    result = taps[REACH] * load(REACH)
    for far in range(1, REACH + 1):
        result = result + taps[REACH + far] * (load(REACH - far) + load(REACH + far))
    return result


def fill_kernel(bricks, group, received, *refs):
    places = refs[: len(bricks.offsets)]
    field, below, above, columns, edge_columns, edges = refs[len(bricks.offsets) :]
    plane, _, slots = received.shape
    scale = CX * CY * CZ / BEADS_DEV
    edges[...] = jnp.zeros_like(edges)
    if plane > group:
        field[...] = jnp.zeros_like(field)

    def put(ref, index, value):
        if plane > group:
            value = value + ref[index]
        ref[index] = value

    def sources(g, carry):
        for near, (step_x, step_y) in enumerate(bricks.offsets):
            place = places[near]
            cells_xy = []
            for p in range(group):
                row = pl.ds(g * group + p, 1)
                cells_xy.append((place[0, row, :], place[1, row, :]))
                z = place[2, row, :]
                amounts = [scale * received[g * group + p, near * 2 + k : near * 2 + k + 1, :] for k in range(2)]
                tap = tap_of(jnp.abs(lax.broadcasted_iota(jnp.int32, (CZ, slots), 0) - z))
                lane = slice(p * slots, (p + 1) * slots)
                for k in range(2):
                    for at, part in enumerate(parts_of(tap * amounts[k], 2)):
                        columns[at * 2 * CZ + k * CZ : at * 2 * CZ + (k + 1) * CZ, lane] = part
                row_of = lax.broadcasted_iota(jnp.int32, (4 * HALO, slots), 0)
                layer = row_of % HALO
                layer = jnp.where(row_of < 2 * HALO, layer - REACH, layer + (CZ - 1))
                amount = jnp.where((row_of // HALO) % 2 == 0, amounts[0], amounts[1])
                edge = tap_of(jnp.abs(layer - z)) * amount
                for at, part in enumerate(parts_of(edge, 2)):
                    edge_columns[at * 4 * HALO : (at + 1) * 4 * HALO, lane] = part
            for side_x in bricks.sides_x[step_x]:
                first_x, width_x, from_x = {
                    0: (HALO, CX, 0),
                    1: (HALO + CX, HALO, 0),
                    -1: (0, HALO, CX - HALO),
                }[side_x]
                for side_y in bricks.sides_y[step_y]:
                    first_y, width_y, from_y, lane_y = {
                        0: (PAD, CY, 0, 0),
                        1: (PAD + CY, PAD, 0, CY),
                        -1: (0, PAD, CY - PAD, LANES - PAD),
                    }[side_y]
                    keys = [
                        jnp.where(
                            (y >= from_y) & (y < from_y + width_y), (x - from_x) * width_y + (y - from_y), -1
                        )
                        for x, y in cells_xy
                    ]
                    layers = min(width_x, 256 // width_y)
                    rows = layers * width_y
                    for start in range(0, width_x, layers):
                        hot = jnp.concatenate(
                            [one_hot(key - start * width_y, rows) for key in keys], axis=1
                        )
                        sums = dot_nt(hot, columns[...])
                        sums = sums[:, : 2 * CZ] + sums[:, 2 * CZ :]
                        outer = dot_nt(edge_columns[...], hot)
                        outer = outer[: 4 * HALO] + outer[4 * HALO :]
                        for layer in range(layers):
                            at = first_x + start + layer
                            piece = slice(layer * width_y, (layer + 1) * width_y)
                            put(field, (at, slice(first_y, first_y + width_y), slice(None)), sums[piece])
                            put(edges, (at, slice(None), slice(lane_y, lane_y + width_y)), outer[:, piece])
        return carry

    lax.fori_loop(0, plane // group, sources, 0)

    for layer in range(CX + 2):
        along_x = filter_rows(lambda j: edges[layer + j])
        both = filter_rows(lambda j: pltpu.roll(along_x, (REACH - j) % LANES, 1))
        below[layer] = both[: 2 * HALO]
        above[layer] = both[2 * HALO :]


def fill(bricks, received, places):
    plane, _, slots = received.shape
    group = 8 if plane % 8 == 0 else plane
    return pl.pallas_call(
        functools.partial(fill_kernel, bricks, group),
        out_shape=[
            jax.ShapeDtypeStruct((CX + 2 * HALO, CY + 2 * PAD, 2 * CZ), f32),
            jax.ShapeDtypeStruct((CX + 2, 2 * HALO, LANES), f32),
            jax.ShapeDtypeStruct((CX + 2, 2 * HALO, LANES), f32),
        ],
        scratch_shapes=[
            pltpu.VMEM((4 * CZ, group * slots), bf16),
            pltpu.VMEM((8 * HALO, group * slots), bf16),
            pltpu.VMEM((CX + 2 * HALO, 4 * HALO, LANES), f32),
        ],
        compiler_params=pltpu.CompilerParams(vmem_limit_bytes=VMEM_LIMIT),
    )(received, *places)


def smooth_kernel(field, below, above, turned, line):
    line[...] = jnp.zeros_like(line)
    wide = CY + PAD
    for layer in range(CX + 2):
        line[PAD : PAD + CY + 2 * PAD, :] = filter_rows(lambda j: field[layer + j])
        main = filter_rows(lambda j: line[2 * PAD + j - REACH : 2 * PAD + j - REACH + wide, :])
        before = filter_rows(lambda j: line[PAD + j - REACH : 2 * PAD + j - REACH, :])
        rest = jnp.zeros((LANES - wide - PAD, 2 * CZ), f32)
        flipped = jnp.concatenate([main, rest, before], axis=0).T
        for k in range(2):
            turned[layer, k, PAD : PAD + CZ, :] = flipped[k * CZ : (k + 1) * CZ]
            turned[layer, k, PAD - 1 : PAD, :] = below[layer, k * HALO + REACH - 1 : k * HALO + REACH, :]
            turned[layer, k, PAD + CZ : PAD + CZ + 1, :] = above[layer, k * HALO + 1 : k * HALO + 2, :]


def smooth(field, below, above):
    return pl.pallas_call(
        smooth_kernel,
        out_shape=jax.ShapeDtypeStruct((CX + 2, 2, CZ + 2 * PAD, LANES), f32),
        scratch_shapes=[pltpu.VMEM((CY + 5 * PAD, 2 * CZ), f32)],
        compiler_params=pltpu.CompilerParams(vmem_limit_bytes=VMEM_LIMIT),
    )(field, below, above)


def slope_kernel(turned, from_below, from_above, place, slopes, whole, table):
    plane, _, slots = slopes.shape
    lanes = lax.broadcasted_iota(jnp.int32, (CZ, LANES), 1)
    for layer in range(CX + 2):
        for k in range(2):
            whole[layer, k] = turned[layer, k]
            at = slice(PAD - 1, PAD - 1 + HALO)
            whole[layer, k, at, :] = whole[layer, k, at, :] + from_below[layer, k * HALO : (k + 1) * HALO, :]
            at = slice(PAD + CZ - REACH, PAD + CZ - REACH + HALO)
            whole[layer, k, at, :] = whole[layer, k, at, :] + from_above[layer, k * HALO : (k + 1) * HALO, :]
    for pair in range(CX // 2):
        for k in range(2):
            halves = []
            for layer in (1 + 2 * pair, 2 + 2 * pair):
                inner = slice(PAD, PAD + CZ)
                here = whole[layer, k, inner, :]
                halves.append(
                    (
                        whole[layer + 1, k, inner, :] - whole[layer - 1, k, inner, :],
                        pltpu.roll(here, LANES - 1, 1) - pltpu.roll(here, 1, 1),
                        whole[layer, k, PAD + 1 : PAD + 1 + CZ, :] - whole[layer, k, PAD - 1 : PAD - 1 + CZ, :],
                    )
                )
            for axis in range(3):
                both = 0.5 * jnp.where(lanes < CY, halves[0][axis], pltpu.roll(halves[1][axis], CY, 1))
                for at, part in enumerate(parts_of(both, 2)):
                    start = at * CX * CY + pair * LANES
                    table[(axis * 2 + k) * CZ : (axis * 2 + k + 1) * CZ, start : start + LANES] = part

    def source(p, carry):
        row = pl.ds(p, 1)
        hot = one_hot(place[0, row, :] * CY + place[1, row, :], CX * CY)
        picked = dot_nn(table[:, : CX * CY], hot) + dot_nn(table[:, CX * CY :], hot)
        depth = lax.broadcasted_iota(jnp.int32, (CZ, slots), 0) == place[2, row, :]
        for axis in range(3):
            steep = [
                jnp.sum(
                    jnp.where(depth, picked[(axis * 2 + k) * CZ : (axis * 2 + k + 1) * CZ], 0.0),
                    axis=0,
                    keepdims=True,
                )
                for k in range(2)
            ]
            joint = stiffness * (steep[0] + steep[1])
            for k in range(2):
                slopes[p, k * 3 + axis : k * 3 + axis + 1, :] = mixing * steep[1 - k] + joint
        return carry

    lax.fori_loop(0, plane, source, 0)


def pick_slopes(turned, from_below, from_above, place):
    plane, slots = place.shape[1:]
    return pl.pallas_call(
        slope_kernel,
        out_shape=[
            jax.ShapeDtypeStruct((plane, 6, slots), f32),
            jax.ShapeDtypeStruct(turned.shape, f32),
        ],
        scratch_shapes=[pltpu.VMEM((6 * CZ, 2 * CX * CY), bf16)],
        compiler_params=pltpu.CompilerParams(vmem_limit_bytes=VMEM_LIMIT),
    )(turned, from_below, from_above, place)


def smoothed_kernel(whole, smoothed):
    for layer in range(CX):
        for k in range(2):
            smoothed[k, layer] = whole[layer + 1, k, PAD : PAD + CZ, :].T[:CY]


def smoothed_of(whole):
    return pl.pallas_call(
        smoothed_kernel,
        out_shape=jax.ShapeDtypeStruct((2, CX, CY, CZ), f32),
        compiler_params=pltpu.CompilerParams(vmem_limit_bytes=VMEM_LIMIT),
    )(whole)


def shifted(values, axis, step):
    count = lax.axis_size(axis)
    return lax.ppermute(values, axis, [((i + step) % count, i) for i in range(count)])


def near_places(slot_cell, bricks):
    found = {}
    for step_y in bricks.sides_y:
        for step_x in bricks.sides_x:
            values = slot_cell if step_x == 0 else found[step_x, 0] if step_y else shifted(slot_cell, "bx", step_x)
            found[step_x, step_y] = values
        if step_y:
            across = [found[step_x, 0] for step_x in bricks.sides_x]
            moved = shifted(jnp.concatenate(across, axis=0), "by", step_y)
            for at, step_x in enumerate(bricks.sides_x):
                found[step_x, step_y] = moved[3 * at : 3 * at + 3]
    return [found[offset] for offset in bricks.offsets]


def to_rows(store, base, row):
    for tile in range(row.shape[1] // LANES):
        store[pl.ds(base + tile, 1), :] = row[:, tile * LANES : (tile + 1) * LANES]


def finish_kernel(
    species,
    corner_slot,
    corner_weight,
    slopes,
    positions,
    velocities,
    bonds,
    new_positions,
    new_velocities,
    table,
    shift,
    anchor,
    hot,
    separation,
):
    plane, _, slots = slopes.shape
    blocks = slots // LANES
    highs = 2 * blocks * plane
    beads = corner_weight.shape[1]
    bead_rows = beads // LANES
    count = bonds.shape[1]

    def collect(brick, carry):
        for axis in range(3):
            for kind in range(2):
                for block in range(blocks):
                    row = pl.ds((axis * 2 * blocks + kind * blocks + block) * plane + brick, 1)
                    at = kind * 3 + axis
                    table[row, :] = slopes[brick, at : at + 1, block * LANES : (block + 1) * LANES]
        return carry

    lax.fori_loop(0, plane, collect, 0, unroll=plane <= 8)
    slope_table = jnp.concatenate(parts_of(table[...], 2), axis=1)

    step = chunk_of(beads, 4)

    def force_body(j, carry):
        where = pl.ds(pl.multiple_of(j * step, step), step)
        kind = species[:, where]
        total = jnp.zeros((3 * highs, step), f32)
        for corner in range(8):
            high, low = corner_keys(kind, corner_slot, corner, where, plane, blocks)
            weight = corner_weight[pl.ds(corner, 1), where]
            rows = lax.broadcasted_iota(jnp.int32, (highs, step), 0) == high
            weights = jnp.where(rows, weight, 0.0)
            hot_low = one_hot(low, LANES)
            picked = dot_nn(slope_table, jnp.concatenate([hot_low, hot_low], axis=0))
            total = total + picked * jnp.concatenate([weights] * 3, axis=0)
        for axis in range(3):
            force = -jnp.sum(total[axis * highs : (axis + 1) * highs], axis=0, keepdims=True)
            half = velocities[pl.ds(axis, 1), where] + 0.5 * time_step * force
            to_rows(shift, axis * bead_rows + j * (step // LANES), time_step * half)
            to_rows(anchor, axis * bead_rows + j * (step // LANES), positions[pl.ds(axis, 1), where])
        return carry

    lax.fori_loop(0, beads // step, force_body, 0)

    bond_step = chunk_of(count, 6)
    bond_rows = 3 * bead_rows
    anchor_parts = parts_of(anchor[...], 3)
    anchor_table = jnp.concatenate(anchor_parts, axis=1)

    def ends(side, where):
        index = bonds[pl.ds(side, 1), where]
        high = index // LANES
        return lax.broadcasted_iota(jnp.int32, (bead_rows, bond_step), 0) == high, index - high * LANES

    def select(rows, picked):
        return [
            jnp.sum(
                jnp.where(rows, picked[axis * bead_rows : (axis + 1) * bead_rows], 0.0),
                axis=0,
                keepdims=True,
            )
            for axis in range(3)
        ]

    for j in range(count // bond_step):
        where = slice(j * bond_step, (j + 1) * bond_step)
        found = []
        for side in range(2):
            rows, low = ends(side, where)
            hot_low = one_hot(low, LANES)
            hot[side, :, where] = hot_low
            found.append(select(rows, dot_nn(anchor_table, jnp.concatenate([hot_low] * 3, axis=0))))
        for axis in range(3):
            separation[axis : axis + 1, where] = found[0][axis] - found[1][axis]

    def sweep(repeat, carry):
        shift_table = jnp.concatenate(parts_of(shift[...], 2), axis=1)
        total = jnp.zeros((2 * bond_rows, LANES), f32)
        for j in range(count // bond_step):
            where = slice(j * bond_step, (j + 1) * bond_step)
            hots = [hot[side, :, where] for side in range(2)]
            rows = [ends(side, where)[0] for side in range(2)]
            found = [
                select(rows[side], dot_nn(shift_table, jnp.concatenate([hots[side]] * 2, axis=0)))
                for side in range(2)
            ]
            apart = [separation[axis : axis + 1, where] for axis in range(3)]
            stretch = [apart[axis] + (found[0][axis] - found[1][axis]) for axis in range(3)]
            excess = sum(s * s for s in stretch) - bond_length * bond_length
            along = sum(s * a for s, a in zip(stretch, apart))
            factor = excess / (4.0 * jnp.maximum(along, 0.5 * bond_length * bond_length))
            moves = [parts_of(factor * apart[axis], 2) for axis in range(3)]
            for side in range(2):
                sign = 1.0 if side else -1.0
                left = jnp.concatenate(
                    [
                        jnp.where(rows[side], sign * moves[axis][part].astype(f32), 0.0).astype(bf16)
                        for part in range(2)
                        for axis in range(3)
                    ],
                    axis=0,
                )
                total = total + dot_nt(left, hots[side])
        shift[...] = shift[...] + total[:bond_rows] + total[bond_rows:]
        return carry

    lax.fori_loop(0, SWEEPS, sweep, 0)

    for axis in range(3):
        for tile in range(bead_rows):
            row = slice(axis * bead_rows + tile, axis * bead_rows + tile + 1)
            where = slice(tile * LANES, (tile + 1) * LANES)
            move = shift[row, :]
            new_positions[axis : axis + 1, where] = anchor[row, :] + move
            new_velocities[axis : axis + 1, where] = move / time_step


def finish(species, corner_slot, corner_weight, slopes, positions, velocities, bonds):
    beads = positions.shape[1]
    count = bonds.shape[1]
    plane, _, slots = slopes.shape
    highs = 2 * (slots // LANES) * plane
    return pl.pallas_call(
        finish_kernel,
        out_shape=[jax.ShapeDtypeStruct((3, beads), f32)] * 2,
        scratch_shapes=[
            pltpu.VMEM((3 * highs, LANES), f32),
            pltpu.VMEM((3 * beads // LANES, LANES), f32),
            pltpu.VMEM((3 * beads // LANES, LANES), f32),
            pltpu.VMEM((2, LANES, count), bf16),
            pltpu.VMEM((3, count), f32),
        ],
        compiler_params=pltpu.CompilerParams(vmem_limit_bytes=VMEM_LIMIT),
    )(species, corner_slot, corner_weight, slopes, positions, velocities, bonds)

def on_device(positions, velocities, species, corner_slot, corner_weight, slot_cell, bond_pairs):
    plane, slots = slot_cell.shape[1:]
    bricks = Bricks(lax.axis_size("bx"), lax.axis_size("by"))
    places = near_places(slot_cell, bricks)
    species = species.reshape(1, -1)
    packets = deposit(bricks, species, corner_slot, corner_weight, plane, slots)
    received = lax.all_to_all(packets, ("bx", "by"), split_axis=0, concat_axis=0, tiled=True)
    field, below, above = fill(bricks, received, places)
    from_above = shifted(below, "bz", 1)
    from_below = shifted(above, "bz", -1)
    turned = smooth(field, below, above)
    slopes, whole = pick_slopes(turned, from_below, from_above, slot_cell)
    returned = lax.all_to_all(slopes, ("bx", "by"), split_axis=0, concat_axis=0, tiled=True)
    smoothed = smoothed_of(whole)
    moved, new_velocities = finish(
        species, corner_slot, corner_weight, returned, positions, velocities, bond_pairs
    )
    return (moved, new_velocities, smoothed)


def solution(mesh):
    in_specs = (
        P(None, ("bx", "by", "bz")),
        P(None, ("bx", "by", "bz")),
        P(("bx", "by", "bz")),
        P(None, None, ("bx", "by", "bz")),
        P(None, ("bx", "by", "bz")),
        P(None, ("bx", "by", "bz"), None),
        P(None, ("bx", "by", "bz")),
    )
    out_specs = (
        P(None, ("bx", "by", "bz")),
        P(None, ("bx", "by", "bz")),
        P(None, "bx", "by", "bz"),
    )
    return jax.shard_map(
        on_device, mesh=mesh, in_specs=in_specs, out_specs=out_specs, check_vma=False
    )
```

```python
import functools
import math

import jax
import jax.numpy as jnp
from jax import lax
from jax.experimental import pallas as pl
from jax.experimental.pallas import tpu as pltpu
from jax.sharding import PartitionSpec as P

CX = 16
CY = 64
CZ = 64
BEADS_DEV = 4096
REACH = 3
SWEEPS = 4


spread_cells = 1.0
mixing = 10.0
stiffness = 5.0
time_step = 0.1
bond_length = 1.0


def gauss_taps():
    raw_list = [
        math.exp(-0.5 * (offset - REACH) ** 2 / spread_cells**2) for offset in range(2 * REACH + 1)
    ]
    tap_total = sum(raw_list)
    return [entry / tap_total for entry in raw_list]


LANES = 128
VMEM_LIMIT = 20 * 1024 * 1024
VMEM_WIDE = 60 * 1024 * 1024
HBM = pl.BlockSpec(memory_space=pltpu.HBM)
f32 = jnp.float32
bf16 = jnp.bfloat16


def parts_of(values, count):
    parts = []
    for _ in range(count):
        part = values.astype(bf16)
        parts.append(part)
        values = values - part.astype(f32)
    return parts


def one_hot(index, size):
    rows = lax.broadcasted_iota(jnp.int16, (size, index.shape[1]), 0)
    return jnp.where(rows == index.astype(jnp.int16), jnp.array(1, bf16), jnp.array(0, bf16))


def dot_nn(left, right):
    return lax.dot_general(left, right, (((1,), (0,)), ((), ())), preferred_element_type=f32)


def dot_nt(left, right):
    return lax.dot_general(left, right, (((1,), (1,)), ((), ())), preferred_element_type=f32)


def chunk_of(length, most):
    tiles = length // LANES
    best = max(t for t in range(1, most + 1) if tiles % t == 0)
    return best * LANES


def chunk_copies(pairs, sems, step, count):
    def copies(j):
        where = pl.ds(pl.multiple_of(j * step, step), step)
        for at, (source, target) in enumerate(pairs):
            lead = (slice(None),) * (len(source.shape) - 1)
            yield pltpu.make_async_copy(source.at[lead + (where,)], target.at[lead + (where,)], sems.at[at, j])

    def start(j, carry):
        for copy in copies(j):
            copy.start()
        return carry

    lax.fori_loop(0, count, start, 0, unroll=True)

    def wait(j):
        for copy in copies(j):
            copy.wait()

    return wait


def corner_keys(species, corner_slot, corner, where, plane, blocks):
    brick = corner_slot[0, pl.ds(corner, 1), where]
    slot = corner_slot[1, pl.ds(corner, 1), where]
    block = slot // LANES
    high = (species * blocks + block) * plane + brick
    return high, slot - block * LANES


def deposit_kernel(
    bricks,
    species_far,
    corner_slot_far,
    corner_weight_far,
    slot_cell_far,
    packets,
    sums,
    species,
    corner_slot,
    corner_weight,
    slot_cell,
    sems,
    cell_sem,
):
    plane, slots = slot_cell.shape[1:]
    blocks = slots // LANES
    highs = 2 * blocks * plane
    beads = corner_weight.shape[1]
    step = chunk_of(beads, 8)
    count_x, count_y = bricks.counts
    wait = chunk_copies(
        [(species_far, species), (corner_slot_far, corner_slot), (corner_weight_far, corner_weight)],
        sems,
        step,
        beads // step,
    )
    cell_copy = pltpu.make_async_copy(slot_cell_far, slot_cell, cell_sem)
    cell_copy.start()

    def body(j, total):
        wait(j)
        where = pl.ds(pl.multiple_of(j * step, step), step)
        kind = species[:, where]
        for corner in range(8):
            high, low = corner_keys(kind, corner_slot, corner, where, plane, blocks)
            weight = corner_weight[pl.ds(corner, 1), where]
            rows = lax.broadcasted_iota(jnp.int32, (highs, step), 0) == high
            left = [jnp.where(rows, p.astype(f32), 0.0).astype(bf16) for p in parts_of(weight, 2)]
            total = total + dot_nt(jnp.concatenate(left, axis=0), one_hot(low, LANES))
        return total

    total = lax.fori_loop(0, beads // step, body, jnp.zeros((2 * highs, LANES), f32))
    sums[...] = total[:highs] + total[highs:]
    cell_copy.wait()
    cells = (slot_cell[0] * CY + slot_cell[1]) * CZ + slot_cell[2]
    first = 2 * blocks * len(bricks.offsets)

    def hand_out(target, carry):
        for near, (step_x, step_y) in enumerate(bricks.offsets):
            brick = lax.rem(target // count_y + step_x, count_x) * count_y + lax.rem(
                lax.rem(target, count_y) + step_y, count_y
            )
            for kind in range(2):
                for block in range(blocks):
                    row = (near * 2 + kind) * blocks + block
                    packets[target, row : row + 1, :] = sums[
                        pl.ds((kind * blocks + block) * plane + brick, 1), :
                    ]
        for block in range(blocks):
            rows = slice(first + block * plane, first + (block + 1) * plane)
            packets[target, rows, :] = cells[:, block * LANES : (block + 1) * LANES].astype(f32)
        return carry

    lax.fori_loop(0, plane, hand_out, 0, unroll=plane <= 8)


def deposit(bricks, species, corner_slot, corner_weight, slot_cell):
    plane, slots = slot_cell.shape[1:]
    blocks = slots // LANES
    rows = blocks * (2 * len(bricks.offsets) + plane)
    return pl.pallas_call(
        functools.partial(deposit_kernel, bricks),
        out_shape=jax.ShapeDtypeStruct((plane, rows, LANES), f32),
        in_specs=[HBM] * 4,
        scratch_shapes=[
            pltpu.VMEM((2 * blocks * plane, LANES), f32),
            pltpu.VMEM(species.shape, species.dtype),
            pltpu.VMEM(corner_slot.shape, corner_slot.dtype),
            pltpu.VMEM(corner_weight.shape, corner_weight.dtype),
            pltpu.VMEM(slot_cell.shape, slot_cell.dtype),
            pltpu.SemaphoreType.DMA((3, species.shape[1] // chunk_of(species.shape[1], 8))),
            pltpu.SemaphoreType.DMA(()),
        ],
        compiler_params=pltpu.CompilerParams(vmem_limit_bytes=VMEM_WIDE),
    )(species, corner_slot, corner_weight, slot_cell)


HALO = REACH + 1
PAD = 8


class Bricks:
    def __init__(self, count_x, count_y):
        self.counts = (count_x, count_y)
        self.sides_x = self.sides(count_x)
        self.sides_y = self.sides(count_y)
        self.offsets = [(x, y) for y in self.sides_y for x in self.sides_x]

    @staticmethod
    def sides(count):
        found = {}
        for side in (0, 1, -1):
            found.setdefault(side % count, []).append(side)
        return found


def tap_of(distance):
    taps = gauss_taps()
    result = jnp.zeros(distance.shape, f32)
    for far in range(REACH, -1, -1):
        result = jnp.where(distance == far, taps[REACH + far], result)
    return result


def filter_rows(load):
    taps = gauss_taps()
    result = taps[REACH] * load(REACH)
    for far in range(1, REACH + 1):
        result = result + taps[REACH + far] * (load(REACH - far) + load(REACH + far))
    return result


def fill_kernel(bricks, group, slots, received, after, field, below, above, columns, edge_columns, edges):
    plane = received.shape[0]
    blocks = slots // LANES
    first_cell = 2 * blocks * len(bricks.offsets)
    count_x, count_y = bricks.counts
    mine = (lax.axis_index("bx"), lax.axis_index("by"))
    scale = CX * CY * CZ / BEADS_DEV
    edges[...] = jnp.zeros_like(edges)
    if plane > group:
        field[...] = jnp.zeros_like(field)

    def put(ref, index, value):
        if plane > group:
            value = value + ref[index]
        ref[index] = value

    def sources(g, carry):
        for near, (step_x, step_y) in enumerate(bricks.offsets):
            brick = lax.rem(mine[0] + step_x, count_x) * count_y + lax.rem(mine[1] + step_y, count_y)
            cells_xy = []
            for p in range(group):
                source = g * group + p
                cell = jnp.concatenate(
                    [received[brick, pl.ds(first_cell + block * plane + source, 1), :] for block in range(blocks)],
                    axis=1,
                ).astype(jnp.int32)
                cells_xy.append((cell // (CY * CZ), cell // CZ % CY))
                z = cell % CZ
                amounts = []
                for k in range(2):
                    row = (near * 2 + k) * blocks
                    amounts.append(
                        scale
                        * jnp.concatenate(
                            [received[source, row + block : row + block + 1, :] for block in range(blocks)], axis=1
                        )
                    )
                tap = tap_of(jnp.abs(lax.broadcasted_iota(jnp.int32, (CZ, slots), 0) - z))
                lane = slice(p * slots, (p + 1) * slots)
                for k in range(2):
                    for at, part in enumerate(parts_of(tap * amounts[k], 2)):
                        columns[at * 2 * CZ + k * CZ : at * 2 * CZ + (k + 1) * CZ, lane] = part
                row_of = lax.broadcasted_iota(jnp.int32, (4 * HALO, slots), 0)
                layer = row_of % HALO
                layer = jnp.where(row_of < 2 * HALO, layer - REACH, layer + (CZ - 1))
                amount = jnp.where((row_of // HALO) % 2 == 0, amounts[0], amounts[1])
                edge = tap_of(jnp.abs(layer - z)) * amount
                for at, part in enumerate(parts_of(edge, 2)):
                    edge_columns[at * 4 * HALO : (at + 1) * 4 * HALO, lane] = part
            for side_x in bricks.sides_x[step_x]:
                first_x, width_x, from_x = {
                    0: (HALO, CX, 0),
                    1: (HALO + CX, HALO, 0),
                    -1: (0, HALO, CX - HALO),
                }[side_x]
                for side_y in bricks.sides_y[step_y]:
                    first_y, width_y, from_y, lane_y = {
                        0: (PAD, CY, 0, 0),
                        1: (PAD + CY, PAD, 0, CY),
                        -1: (0, PAD, CY - PAD, LANES - PAD),
                    }[side_y]
                    keys = [
                        jnp.where(
                            (y >= from_y) & (y < from_y + width_y), (x - from_x) * width_y + (y - from_y), -1
                        )
                        for x, y in cells_xy
                    ]
                    layers = min(width_x, 256 // width_y)
                    rows = layers * width_y
                    for start in range(0, width_x, layers):
                        hot = jnp.concatenate(
                            [one_hot(key - start * width_y, rows) for key in keys], axis=1
                        )
                        sums = dot_nt(hot, columns[...])
                        sums = sums[:, : 2 * CZ] + sums[:, 2 * CZ :]
                        outer = dot_nt(edge_columns[...], hot)
                        outer = outer[: 4 * HALO] + outer[4 * HALO :]
                        for layer in range(layers):
                            at = first_x + start + layer
                            piece = slice(layer * width_y, (layer + 1) * width_y)
                            put(field, (at, slice(first_y, first_y + width_y), slice(None)), sums[piece])
                            put(edges, (at, slice(None), slice(lane_y, lane_y + width_y)), outer[:, piece])
        return carry

    lax.fori_loop(0, plane // group, sources, 0)

    for layer in range(CX + 2):
        along_x = filter_rows(lambda j: edges[layer + j])
        both = filter_rows(lambda j: pltpu.roll(along_x, (REACH - j) % LANES, 1))
        below[layer] = both[: 2 * HALO]
        above[layer] = both[2 * HALO :]


def fill(bricks, received, slots, after):
    plane = received.shape[0]
    group = 8 if plane % 8 == 0 else plane
    return pl.pallas_call(
        functools.partial(fill_kernel, bricks, group, slots),
        out_shape=[
            jax.ShapeDtypeStruct((CX + 2 * HALO, CY + 2 * PAD, 2 * CZ), f32),
            jax.ShapeDtypeStruct((CX + 2, 2 * HALO, LANES), f32),
            jax.ShapeDtypeStruct((CX + 2, 2 * HALO, LANES), f32),
        ],
        in_specs=[pl.BlockSpec(), pl.BlockSpec(memory_space=pl.ANY)],
        scratch_shapes=[
            pltpu.VMEM((4 * CZ, group * slots), bf16),
            pltpu.VMEM((8 * HALO, group * slots), bf16),
            pltpu.VMEM((CX + 2 * HALO, 4 * HALO, LANES), f32),
        ],
        compiler_params=pltpu.CompilerParams(vmem_limit_bytes=VMEM_LIMIT),
    )(received, after)


def smooth_kernel(field, below, above, turned, line):
    line[...] = jnp.zeros_like(line)
    wide = CY + PAD
    for layer in range(CX + 2):
        line[PAD : PAD + CY + 2 * PAD, :] = filter_rows(lambda j: field[layer + j])
        main = filter_rows(lambda j: line[2 * PAD + j - REACH : 2 * PAD + j - REACH + wide, :])
        before = filter_rows(lambda j: line[PAD + j - REACH : 2 * PAD + j - REACH, :])
        rest = jnp.zeros((LANES - wide - PAD, 2 * CZ), f32)
        flipped = jnp.concatenate([main, rest, before], axis=0).T
        for k in range(2):
            turned[layer, k, PAD : PAD + CZ, :] = flipped[k * CZ : (k + 1) * CZ]
            turned[layer, k, PAD - 1 : PAD, :] = below[layer, k * HALO + REACH - 1 : k * HALO + REACH, :]
            turned[layer, k, PAD + CZ : PAD + CZ + 1, :] = above[layer, k * HALO + 1 : k * HALO + 2, :]


def smooth(field, below, above):
    return pl.pallas_call(
        smooth_kernel,
        out_shape=jax.ShapeDtypeStruct((CX + 2, 2, CZ + 2 * PAD, LANES), f32),
        scratch_shapes=[pltpu.VMEM((CY + 5 * PAD, 2 * CZ), f32)],
        compiler_params=pltpu.CompilerParams(vmem_limit_bytes=VMEM_LIMIT),
    )(field, below, above)


def slope_kernel(turned, from_below, from_above, place, slopes, whole, table):
    plane, _, slots = slopes.shape
    lanes = lax.broadcasted_iota(jnp.int32, (CZ, LANES), 1)
    for layer in range(CX + 2):
        for k in range(2):
            whole[layer, k] = turned[layer, k]
            at = slice(PAD - 1, PAD - 1 + HALO)
            whole[layer, k, at, :] = whole[layer, k, at, :] + from_below[layer, k * HALO : (k + 1) * HALO, :]
            at = slice(PAD + CZ - REACH, PAD + CZ - REACH + HALO)
            whole[layer, k, at, :] = whole[layer, k, at, :] + from_above[layer, k * HALO : (k + 1) * HALO, :]
    for pair in range(CX // 2):
        for k in range(2):
            halves = []
            for layer in (1 + 2 * pair, 2 + 2 * pair):
                inner = slice(PAD, PAD + CZ)
                here = whole[layer, k, inner, :]
                halves.append(
                    (
                        whole[layer + 1, k, inner, :] - whole[layer - 1, k, inner, :],
                        pltpu.roll(here, LANES - 1, 1) - pltpu.roll(here, 1, 1),
                        whole[layer, k, PAD + 1 : PAD + 1 + CZ, :] - whole[layer, k, PAD - 1 : PAD - 1 + CZ, :],
                    )
                )
            for axis in range(3):
                both = 0.5 * jnp.where(lanes < CY, halves[0][axis], pltpu.roll(halves[1][axis], CY, 1))
                for at, part in enumerate(parts_of(both, 2)):
                    start = at * CX * CY + pair * LANES
                    table[(axis * 2 + k) * CZ : (axis * 2 + k + 1) * CZ, start : start + LANES] = part

    def source(p, carry):
        row = pl.ds(p, 1)
        hot = one_hot(place[0, row, :] * CY + place[1, row, :], CX * CY)
        picked = dot_nn(table[:, : CX * CY], hot) + dot_nn(table[:, CX * CY :], hot)
        depth = lax.broadcasted_iota(jnp.int32, (CZ, slots), 0) == place[2, row, :]
        for axis in range(3):
            steep = [
                jnp.sum(
                    jnp.where(depth, picked[(axis * 2 + k) * CZ : (axis * 2 + k + 1) * CZ], 0.0),
                    axis=0,
                    keepdims=True,
                )
                for k in range(2)
            ]
            joint = stiffness * (steep[0] + steep[1])
            for k in range(2):
                slopes[p, k * 3 + axis : k * 3 + axis + 1, :] = mixing * steep[1 - k] + joint
        return carry

    lax.fori_loop(0, plane, source, 0, unroll=4)


def pick_slopes(turned, from_below, from_above, place):
    plane, slots = place.shape[1:]
    return pl.pallas_call(
        slope_kernel,
        out_shape=[
            jax.ShapeDtypeStruct((plane, 6, slots), f32),
            jax.ShapeDtypeStruct(turned.shape, f32),
        ],
        scratch_shapes=[pltpu.VMEM((6 * CZ, 2 * CX * CY), bf16)],
        compiler_params=pltpu.CompilerParams(vmem_limit_bytes=VMEM_LIMIT),
    )(turned, from_below, from_above, place)


def smoothed_kernel(whole, smoothed):
    for layer in range(CX):
        for k in range(2):
            smoothed[k, layer] = whole[layer + 1, k, PAD : PAD + CZ, :].T[:CY]


def smoothed_of(whole):
    return pl.pallas_call(
        smoothed_kernel,
        out_shape=jax.ShapeDtypeStruct((2, CX, CY, CZ), f32),
        compiler_params=pltpu.CompilerParams(vmem_limit_bytes=VMEM_LIMIT),
    )(whole)


def shifted(values, axis, step):
    count = lax.axis_size(axis)
    return lax.ppermute(values, axis, [((i + step) % count, i) for i in range(count)])


def to_rows(store, base, row):
    for tile in range(row.shape[1] // LANES):
        store[pl.ds(base + tile, 1), :] = row[:, tile * LANES : (tile + 1) * LANES]


def bond_ends(bonds, side, where, bead_rows):
    index = bonds[pl.ds(side, 1), where]
    high = index // LANES
    rows = lax.broadcasted_iota(jnp.int32, (bead_rows, index.shape[1]), 0) == high
    return rows, index - high * LANES


def select(rows, picked):
    size = rows.shape[0]
    return [
        jnp.sum(jnp.where(rows, picked[axis * size : (axis + 1) * size], 0.0), axis=0, keepdims=True)
        for axis in range(3)
    ]


def bonds_kernel(positions, bonds, after, anchor, hot, separation):
    bead_rows = positions.shape[1] // LANES
    count = bonds.shape[1]
    bond_step = chunk_of(count, 6)
    for axis in range(3):
        to_rows(anchor, axis * bead_rows, positions[axis : axis + 1, :])
    anchor_table = jnp.concatenate(parts_of(anchor[...], 3), axis=1)
    for j in range(count // bond_step):
        where = slice(j * bond_step, (j + 1) * bond_step)
        found = []
        for side in range(2):
            rows, low = bond_ends(bonds, side, where, bead_rows)
            hot_low = one_hot(low, LANES)
            hot[side, :, where] = hot_low
            found.append(select(rows, dot_nn(anchor_table, jnp.concatenate([hot_low] * 3, axis=0))))
        for axis in range(3):
            separation[axis : axis + 1, where] = found[0][axis] - found[1][axis]


def prepare_bonds(positions, bonds, after):
    beads = positions.shape[1]
    count = bonds.shape[1]
    return pl.pallas_call(
        bonds_kernel,
        out_shape=[
            jax.ShapeDtypeStruct((3 * beads // LANES, LANES), f32),
            jax.ShapeDtypeStruct((2, LANES, count), bf16),
            jax.ShapeDtypeStruct((3, count), f32),
        ],
        in_specs=[pl.BlockSpec(), pl.BlockSpec(), pl.BlockSpec(memory_space=pl.ANY)],
        compiler_params=pltpu.CompilerParams(vmem_limit_bytes=VMEM_LIMIT),
    )(positions, bonds, after)


def finish_kernel(
    species_far,
    corner_slot_far,
    corner_weight_far,
    velocities_far,
    slopes,
    bonds_far,
    anchor_far,
    hot_far,
    separation_far,
    new_positions,
    new_velocities,
    table,
    shift,
    species,
    corner_slot,
    corner_weight,
    velocities,
    bonds,
    anchor,
    hot,
    separation,
    sems,
    late_sems,
):
    plane, _, slots = slopes.shape
    blocks = slots // LANES
    highs = 2 * blocks * plane
    beads = corner_weight.shape[1]
    bead_rows = beads // LANES
    count = bonds.shape[1]
    step = chunk_of(beads, 4)
    wait = chunk_copies(
        [
            (species_far, species),
            (corner_slot_far, corner_slot),
            (corner_weight_far, corner_weight),
            (velocities_far, velocities),
        ],
        sems,
        step,
        beads // step,
    )
    late = [
        pltpu.make_async_copy(source, target, late_sems.at[at])
        for at, (source, target) in enumerate(
            [(bonds_far, bonds), (anchor_far, anchor), (hot_far, hot), (separation_far, separation)]
        )
    ]
    for copy in late:
        copy.start()

    def collect(brick, carry):
        for axis in range(3):
            for kind in range(2):
                for block in range(blocks):
                    row = pl.ds((axis * 2 * blocks + kind * blocks + block) * plane + brick, 1)
                    at = kind * 3 + axis
                    table[row, :] = slopes[brick, at : at + 1, block * LANES : (block + 1) * LANES]
        return carry

    lax.fori_loop(0, plane, collect, 0, unroll=plane <= 8)
    slope_table = jnp.concatenate(parts_of(table[...], 2), axis=1)

    def force_body(j, carry):
        wait(j)
        where = pl.ds(pl.multiple_of(j * step, step), step)
        kind = species[:, where]
        total = jnp.zeros((3 * highs, step), f32)
        for corner in range(8):
            high, low = corner_keys(kind, corner_slot, corner, where, plane, blocks)
            weight = corner_weight[pl.ds(corner, 1), where]
            rows = lax.broadcasted_iota(jnp.int32, (highs, step), 0) == high
            weights = jnp.where(rows, weight, 0.0)
            hot_low = one_hot(low, LANES)
            picked = dot_nn(slope_table, jnp.concatenate([hot_low, hot_low], axis=0))
            total = total + picked * jnp.concatenate([weights] * 3, axis=0)
        for axis in range(3):
            force = -jnp.sum(total[axis * highs : (axis + 1) * highs], axis=0, keepdims=True)
            half = velocities[pl.ds(axis, 1), where] + 0.5 * time_step * force
            to_rows(shift, axis * bead_rows + j * (step // LANES), time_step * half)
        return carry

    lax.fori_loop(0, beads // step, force_body, 0)

    for copy in late:
        copy.wait()
    bond_step = chunk_of(count, 6)
    bond_rows = 3 * bead_rows

    def sweep(repeat, carry):
        shift_table = jnp.concatenate(parts_of(shift[...], 2), axis=1)
        total = jnp.zeros((2 * bond_rows, LANES), f32)
        for j in range(count // bond_step):
            where = slice(j * bond_step, (j + 1) * bond_step)
            hots = [hot[side, :, where] for side in range(2)]
            rows = [bond_ends(bonds, side, where, bead_rows)[0] for side in range(2)]
            found = [
                select(rows[side], dot_nn(shift_table, jnp.concatenate([hots[side]] * 2, axis=0)))
                for side in range(2)
            ]
            apart = [separation[axis : axis + 1, where] for axis in range(3)]
            stretch = [apart[axis] + (found[0][axis] - found[1][axis]) for axis in range(3)]
            excess = sum(s * s for s in stretch) - bond_length * bond_length
            along = sum(s * a for s, a in zip(stretch, apart))
            factor = excess / (4.0 * jnp.maximum(along, 0.5 * bond_length * bond_length))
            moves = [parts_of(factor * apart[axis], 2) for axis in range(3)]
            for side in range(2):
                sign = 1.0 if side else -1.0
                left = jnp.concatenate(
                    [
                        jnp.where(rows[side], sign * moves[axis][part].astype(f32), 0.0).astype(bf16)
                        for part in range(2)
                        for axis in range(3)
                    ],
                    axis=0,
                )
                total = total + dot_nt(left, hots[side])
        shift[...] = shift[...] + total[:bond_rows] + total[bond_rows:]
        return carry

    lax.fori_loop(0, SWEEPS, sweep, 0)

    for axis in range(3):
        for tile in range(bead_rows):
            row = slice(axis * bead_rows + tile, axis * bead_rows + tile + 1)
            where = slice(tile * LANES, (tile + 1) * LANES)
            move = shift[row, :]
            new_positions[axis : axis + 1, where] = anchor[row, :] + move
            new_velocities[axis : axis + 1, where] = move / time_step


def finish(species, corner_slot, corner_weight, slopes, velocities, bonds, prepared):
    beads = velocities.shape[1]
    plane, _, slots = slopes.shape
    highs = 2 * (slots // LANES) * plane
    early = (species, corner_slot, corner_weight, velocities)
    late = (bonds, *prepared)
    return pl.pallas_call(
        finish_kernel,
        out_shape=[jax.ShapeDtypeStruct((3, beads), f32)] * 2,
        in_specs=[HBM] * len(early) + [pl.BlockSpec()] + [HBM] * len(late),
        scratch_shapes=[
            pltpu.VMEM((3 * highs, LANES), f32),
            pltpu.VMEM((3 * beads // LANES, LANES), f32),
            *(pltpu.VMEM(a.shape, a.dtype) for a in early + late),
            pltpu.SemaphoreType.DMA((len(early), beads // chunk_of(beads, 4))),
            pltpu.SemaphoreType.DMA((len(late),)),
        ],
        compiler_params=pltpu.CompilerParams(vmem_limit_bytes=VMEM_WIDE),
    )(*early, slopes, *late)


def on_device(positions, velocities, species, corner_slot, corner_weight, slot_cell, bond_pairs):
    slots = slot_cell.shape[2]
    bricks = Bricks(lax.axis_size("bx"), lax.axis_size("by"))
    species = species.reshape(1, -1)
    packets = deposit(bricks, species, corner_slot, corner_weight, slot_cell)
    received = lax.all_to_all(packets, ("bx", "by"), split_axis=0, concat_axis=0, tiled=True)
    prepared = prepare_bonds(positions, bond_pairs, packets)
    field, below, above = fill(bricks, received, slots, prepared[2])
    from_above = shifted(below, "bz", 1)
    from_below = shifted(above, "bz", -1)
    turned = smooth(field, below, above)
    slopes, whole = pick_slopes(turned, from_below, from_above, slot_cell)
    returned = lax.all_to_all(slopes, ("bx", "by"), split_axis=0, concat_axis=0, tiled=True)
    smoothed = smoothed_of(whole)
    moved, new_velocities = finish(
        species, corner_slot, corner_weight, returned, velocities, bond_pairs, prepared
    )
    return (moved, new_velocities, smoothed)


def solution(mesh):
    in_specs = (
        P(None, ("bx", "by", "bz")),
        P(None, ("bx", "by", "bz")),
        P(("bx", "by", "bz")),
        P(None, None, ("bx", "by", "bz")),
        P(None, ("bx", "by", "bz")),
        P(None, ("bx", "by", "bz"), None),
        P(None, ("bx", "by", "bz")),
    )
    out_specs = (
        P(None, ("bx", "by", "bz")),
        P(None, ("bx", "by", "bz")),
        P(None, "bx", "by", "bz"),
    )
    return jax.shard_map(
        on_device, mesh=mesh, in_specs=in_specs, out_specs=out_specs, check_vma=False
    )
```

```python
import functools
import math

import jax
import jax.numpy as jnp
from jax import lax
from jax.experimental import pallas as pl
from jax.experimental.pallas import tpu as pltpu
from jax.sharding import PartitionSpec as P

CX = 16
CY = 64
CZ = 64
BEADS_DEV = 4096
REACH = 3
SWEEPS = 4


spread_cells = 1.0
mixing = 10.0
stiffness = 5.0
time_step = 0.1
bond_length = 1.0


def gauss_taps():
    raw_list = [
        math.exp(-0.5 * (offset - REACH) ** 2 / spread_cells**2) for offset in range(2 * REACH + 1)
    ]
    tap_total = sum(raw_list)
    return [entry / tap_total for entry in raw_list]


LANES = 128
VMEM_LIMIT = 20 * 1024 * 1024
VMEM_WIDE = 60 * 1024 * 1024
HBM = pl.BlockSpec(memory_space=pltpu.HBM)
f32 = jnp.float32
bf16 = jnp.bfloat16


def parts_of(values, count):
    parts = []
    for _ in range(count):
        part = values.astype(bf16)
        parts.append(part)
        values = values - part.astype(f32)
    return parts


def one_hot(index, size):
    rows = lax.broadcasted_iota(jnp.int16, (size, index.shape[1]), 0)
    return jnp.where(rows == index.astype(jnp.int16), jnp.array(1, bf16), jnp.array(0, bf16))


def dot_nn(left, right):
    return lax.dot_general(left, right, (((1,), (0,)), ((), ())), preferred_element_type=f32)


def dot_nt(left, right):
    return lax.dot_general(left, right, (((1,), (1,)), ((), ())), preferred_element_type=f32)


def chunk_of(length, most):
    tiles = length // LANES
    best = max(t for t in range(1, most + 1) if tiles % t == 0)
    return best * LANES


def chunk_copies(pairs, sems, step, count):
    def copies(j):
        where = pl.ds(pl.multiple_of(j * step, step), step)
        for at, (source, target) in enumerate(pairs):
            lead = (slice(None),) * (len(source.shape) - 1)
            yield pltpu.make_async_copy(source.at[lead + (where,)], target.at[lead + (where,)], sems.at[at, j])

    def start(j, carry):
        for copy in copies(j):
            copy.start()
        return carry

    lax.fori_loop(0, count, start, 0, unroll=True)

    def wait(j):
        for copy in copies(j):
            copy.wait()

    return wait


def corner_keys(species, corner_slot, corner, where, plane, blocks):
    brick = corner_slot[0, pl.ds(corner, 1), where]
    slot = corner_slot[1, pl.ds(corner, 1), where]
    block = slot // LANES
    high = (species * blocks + block) * plane + brick
    return high, slot - block * LANES


def deposit_kernel(
    bricks,
    species_far,
    corner_slot_far,
    corner_weight_far,
    slot_cell_far,
    packets,
    sums,
    species,
    corner_slot,
    corner_weight,
    slot_cell,
    sems,
    cell_sem,
):
    plane, slots = slot_cell.shape[1:]
    blocks = slots // LANES
    highs = 2 * blocks * plane
    beads = corner_weight.shape[1]
    step = chunk_of(beads, 8)
    count_x, count_y = bricks.counts
    wait = chunk_copies(
        [(species_far, species), (corner_slot_far, corner_slot), (corner_weight_far, corner_weight)],
        sems,
        step,
        beads // step,
    )
    cell_copy = pltpu.make_async_copy(slot_cell_far, slot_cell, cell_sem)
    cell_copy.start()

    def body(j, total):
        wait(j)
        where = pl.ds(pl.multiple_of(j * step, step), step)
        kind = species[:, where]
        for corner in range(8):
            high, low = corner_keys(kind, corner_slot, corner, where, plane, blocks)
            weight = corner_weight[pl.ds(corner, 1), where]
            rows = lax.broadcasted_iota(jnp.int32, (highs, step), 0) == high
            left = [jnp.where(rows, p.astype(f32), 0.0).astype(bf16) for p in parts_of(weight, 2)]
            total = total + dot_nt(jnp.concatenate(left, axis=0), one_hot(low, LANES))
        return total

    total = lax.fori_loop(0, beads // step, body, jnp.zeros((2 * highs, LANES), f32))
    sums[...] = total[:highs] + total[highs:]
    cell_copy.wait()
    cells = (slot_cell[0] * CY + slot_cell[1]) * CZ + slot_cell[2]
    first = 2 * blocks * len(bricks.offsets)

    def hand_out(target, carry):
        for near, (step_x, step_y) in enumerate(bricks.offsets):
            brick = lax.rem(target // count_y + step_x, count_x) * count_y + lax.rem(
                lax.rem(target, count_y) + step_y, count_y
            )
            for kind in range(2):
                for block in range(blocks):
                    row = (near * 2 + kind) * blocks + block
                    packets[target, row : row + 1, :] = sums[
                        pl.ds((kind * blocks + block) * plane + brick, 1), :
                    ]
        for block in range(blocks):
            rows = slice(first + block * plane, first + (block + 1) * plane)
            packets[target, rows, :] = cells[:, block * LANES : (block + 1) * LANES].astype(f32)
        return carry

    lax.fori_loop(0, plane, hand_out, 0, unroll=plane <= 8)


def deposit(bricks, species, corner_slot, corner_weight, slot_cell):
    plane, slots = slot_cell.shape[1:]
    blocks = slots // LANES
    rows = blocks * (2 * len(bricks.offsets) + plane)
    return pl.pallas_call(
        functools.partial(deposit_kernel, bricks),
        out_shape=jax.ShapeDtypeStruct((plane, rows, LANES), f32),
        in_specs=[HBM] * 4,
        scratch_shapes=[
            pltpu.VMEM((2 * blocks * plane, LANES), f32),
            pltpu.VMEM(species.shape, species.dtype),
            pltpu.VMEM(corner_slot.shape, corner_slot.dtype),
            pltpu.VMEM(corner_weight.shape, corner_weight.dtype),
            pltpu.VMEM(slot_cell.shape, slot_cell.dtype),
            pltpu.SemaphoreType.DMA((3, species.shape[1] // chunk_of(species.shape[1], 8))),
            pltpu.SemaphoreType.DMA(()),
        ],
        compiler_params=pltpu.CompilerParams(vmem_limit_bytes=VMEM_WIDE),
    )(species, corner_slot, corner_weight, slot_cell)


HALO = REACH + 1
PAD = 8


class Bricks:
    def __init__(self, count_x, count_y):
        self.counts = (count_x, count_y)
        self.sides_x = self.sides(count_x)
        self.sides_y = self.sides(count_y)
        self.offsets = [(x, y) for y in self.sides_y for x in self.sides_x]

    @staticmethod
    def sides(count):
        found = {}
        for side in (0, 1, -1):
            found.setdefault(side % count, []).append(side)
        return found


def tap_of(distance):
    taps = gauss_taps()
    result = jnp.zeros(distance.shape, f32)
    for far in range(REACH, -1, -1):
        result = jnp.where(distance == far, taps[REACH + far], result)
    return result


def filter_rows(load):
    taps = gauss_taps()
    result = taps[REACH] * load(REACH)
    for far in range(1, REACH + 1):
        result = result + taps[REACH + far] * (load(REACH - far) + load(REACH + far))
    return result


def fill_kernel(bricks, group, slots, received, after, field, below, above, columns, edge_columns, edges):
    plane = received.shape[0]
    blocks = slots // LANES
    first_cell = 2 * blocks * len(bricks.offsets)
    count_x, count_y = bricks.counts
    mine = (lax.axis_index("bx"), lax.axis_index("by"))
    scale = CX * CY * CZ / BEADS_DEV
    edges[...] = jnp.zeros_like(edges)
    if plane > group:
        field[...] = jnp.zeros_like(field)

    def put(ref, index, value):
        if plane > group:
            value = value + ref[index]
        ref[index] = value

    def sources(g, carry):
        for near, (step_x, step_y) in enumerate(bricks.offsets):
            brick = lax.rem(mine[0] + step_x, count_x) * count_y + lax.rem(mine[1] + step_y, count_y)
            cells_xy = []
            for p in range(group):
                source = g * group + p
                cell = jnp.concatenate(
                    [received[brick, pl.ds(first_cell + block * plane + source, 1), :] for block in range(blocks)],
                    axis=1,
                ).astype(jnp.int32)
                cells_xy.append((cell // (CY * CZ), cell // CZ % CY))
                z = cell % CZ
                amounts = []
                for k in range(2):
                    row = (near * 2 + k) * blocks
                    amounts.append(
                        scale
                        * jnp.concatenate(
                            [received[source, row + block : row + block + 1, :] for block in range(blocks)], axis=1
                        )
                    )
                tap = tap_of(jnp.abs(lax.broadcasted_iota(jnp.int32, (CZ, slots), 0) - z))
                lane = slice(p * slots, (p + 1) * slots)
                for k in range(2):
                    for at, part in enumerate(parts_of(tap * amounts[k], 2)):
                        columns[at * 2 * CZ + k * CZ : at * 2 * CZ + (k + 1) * CZ, lane] = part
                row_of = lax.broadcasted_iota(jnp.int32, (4 * HALO, slots), 0)
                layer = row_of % HALO
                layer = jnp.where(row_of < 2 * HALO, layer - REACH, layer + (CZ - 1))
                amount = jnp.where((row_of // HALO) % 2 == 0, amounts[0], amounts[1])
                edge = tap_of(jnp.abs(layer - z)) * amount
                for at, part in enumerate(parts_of(edge, 2)):
                    edge_columns[at * 4 * HALO : (at + 1) * 4 * HALO, lane] = part
            for side_x in bricks.sides_x[step_x]:
                first_x, width_x, from_x = {
                    0: (HALO, CX, 0),
                    1: (HALO + CX, HALO, 0),
                    -1: (0, HALO, CX - HALO),
                }[side_x]
                for side_y in bricks.sides_y[step_y]:
                    first_y, width_y, from_y, lane_y = {
                        0: (PAD, CY, 0, 0),
                        1: (PAD + CY, PAD, 0, CY),
                        -1: (0, PAD, CY - PAD, LANES - PAD),
                    }[side_y]
                    keys = [
                        jnp.where(
                            (y >= from_y) & (y < from_y + width_y), (x - from_x) * width_y + (y - from_y), -1
                        )
                        for x, y in cells_xy
                    ]
                    layers = min(width_x, 256 // width_y)
                    rows = layers * width_y
                    for start in range(0, width_x, layers):
                        hot = jnp.concatenate(
                            [one_hot(key - start * width_y, rows) for key in keys], axis=1
                        )
                        sums = dot_nt(hot, columns[...])
                        sums = sums[:, : 2 * CZ] + sums[:, 2 * CZ :]
                        outer = dot_nt(edge_columns[...], hot)
                        outer = outer[: 4 * HALO] + outer[4 * HALO :]
                        for layer in range(layers):
                            at = first_x + start + layer
                            piece = slice(layer * width_y, (layer + 1) * width_y)
                            put(field, (at, slice(first_y, first_y + width_y), slice(None)), sums[piece])
                            put(edges, (at, slice(None), slice(lane_y, lane_y + width_y)), outer[:, piece])
        return carry

    lax.fori_loop(0, plane // group, sources, 0)

    for layer in range(CX + 2):
        along_x = filter_rows(lambda j: edges[layer + j])
        both = filter_rows(lambda j: pltpu.roll(along_x, (REACH - j) % LANES, 1))
        below[layer] = both[: 2 * HALO]
        above[layer] = both[2 * HALO :]


def fill(bricks, received, slots, after):
    plane = received.shape[0]
    group = 8 if plane % 8 == 0 else plane
    return pl.pallas_call(
        functools.partial(fill_kernel, bricks, group, slots),
        out_shape=[
            jax.ShapeDtypeStruct((CX + 2 * HALO, CY + 2 * PAD, 2 * CZ), f32),
            jax.ShapeDtypeStruct((CX + 2, 2 * HALO, LANES), f32),
            jax.ShapeDtypeStruct((CX + 2, 2 * HALO, LANES), f32),
        ],
        in_specs=[pl.BlockSpec(), pl.BlockSpec(memory_space=pl.ANY)],
        scratch_shapes=[
            pltpu.VMEM((4 * CZ, group * slots), bf16),
            pltpu.VMEM((8 * HALO, group * slots), bf16),
            pltpu.VMEM((CX + 2 * HALO, 4 * HALO, LANES), f32),
        ],
        compiler_params=pltpu.CompilerParams(vmem_limit_bytes=VMEM_LIMIT),
    )(received, after)


def smooth_kernel(field, below, above, turned, line):
    line[...] = jnp.zeros_like(line)
    wide = CY + PAD
    for layer in range(CX + 2):
        line[PAD : PAD + CY + 2 * PAD, :] = filter_rows(lambda j: field[layer + j])
        main = filter_rows(lambda j: line[2 * PAD + j - REACH : 2 * PAD + j - REACH + wide, :])
        before = filter_rows(lambda j: line[PAD + j - REACH : 2 * PAD + j - REACH, :])
        rest = jnp.zeros((LANES - wide - PAD, 2 * CZ), f32)
        flipped = jnp.concatenate([main, rest, before], axis=0).T
        for k in range(2):
            turned[layer, k, PAD : PAD + CZ, :] = flipped[k * CZ : (k + 1) * CZ]
            turned[layer, k, PAD - 1 : PAD, :] = below[layer, k * HALO + REACH - 1 : k * HALO + REACH, :]
            turned[layer, k, PAD + CZ : PAD + CZ + 1, :] = above[layer, k * HALO + 1 : k * HALO + 2, :]


def smooth(field, below, above):
    return pl.pallas_call(
        smooth_kernel,
        out_shape=jax.ShapeDtypeStruct((CX + 2, 2, CZ + 2 * PAD, LANES), f32),
        scratch_shapes=[pltpu.VMEM((CY + 5 * PAD, 2 * CZ), f32)],
        compiler_params=pltpu.CompilerParams(vmem_limit_bytes=VMEM_LIMIT),
    )(field, below, above)


def slope_kernel(turned, from_below, from_above, place, slopes, whole, table):
    plane, _, slots = slopes.shape
    lanes = lax.broadcasted_iota(jnp.int32, (CZ, LANES), 1)
    for layer in range(CX + 2):
        for k in range(2):
            whole[layer, k] = turned[layer, k]
            at = slice(PAD - 1, PAD - 1 + HALO)
            whole[layer, k, at, :] = whole[layer, k, at, :] + from_below[layer, k * HALO : (k + 1) * HALO, :]
            at = slice(PAD + CZ - REACH, PAD + CZ - REACH + HALO)
            whole[layer, k, at, :] = whole[layer, k, at, :] + from_above[layer, k * HALO : (k + 1) * HALO, :]
    for pair in range(CX // 2):
        for k in range(2):
            halves = []
            for layer in (1 + 2 * pair, 2 + 2 * pair):
                inner = slice(PAD, PAD + CZ)
                here = whole[layer, k, inner, :]
                halves.append(
                    (
                        whole[layer + 1, k, inner, :] - whole[layer - 1, k, inner, :],
                        pltpu.roll(here, LANES - 1, 1) - pltpu.roll(here, 1, 1),
                        whole[layer, k, PAD + 1 : PAD + 1 + CZ, :] - whole[layer, k, PAD - 1 : PAD - 1 + CZ, :],
                    )
                )
            for axis in range(3):
                both = 0.5 * jnp.where(lanes < CY, halves[0][axis], pltpu.roll(halves[1][axis], CY, 1))
                for at, part in enumerate(parts_of(both, 2)):
                    start = at * CX * CY + pair * LANES
                    table[(axis * 2 + k) * CZ : (axis * 2 + k + 1) * CZ, start : start + LANES] = part

    def source(p, carry):
        row = pl.ds(p, 1)
        hot = one_hot(place[0, row, :] * CY + place[1, row, :], CX * CY)
        picked = dot_nn(table[:, : CX * CY], hot) + dot_nn(table[:, CX * CY :], hot)
        depth = lax.broadcasted_iota(jnp.int32, (CZ, slots), 0) == place[2, row, :]
        for axis in range(3):
            steep = [
                jnp.sum(
                    jnp.where(depth, picked[(axis * 2 + k) * CZ : (axis * 2 + k + 1) * CZ], 0.0),
                    axis=0,
                    keepdims=True,
                )
                for k in range(2)
            ]
            joint = stiffness * (steep[0] + steep[1])
            for k in range(2):
                slopes[p, k * 3 + axis : k * 3 + axis + 1, :] = mixing * steep[1 - k] + joint
        return carry

    lax.fori_loop(0, plane, source, 0, unroll=4)


def pick_slopes(turned, from_below, from_above, place):
    plane, slots = place.shape[1:]
    return pl.pallas_call(
        slope_kernel,
        out_shape=[
            jax.ShapeDtypeStruct((plane, 6, slots), f32),
            jax.ShapeDtypeStruct(turned.shape, f32),
        ],
        scratch_shapes=[pltpu.VMEM((6 * CZ, 2 * CX * CY), bf16)],
        compiler_params=pltpu.CompilerParams(vmem_limit_bytes=VMEM_LIMIT),
    )(turned, from_below, from_above, place)


def smoothed_kernel(whole, smoothed):
    for layer in range(CX):
        for k in range(2):
            smoothed[k, layer] = whole[layer + 1, k, PAD : PAD + CZ, :].T[:CY]


def smoothed_of(whole):
    return pl.pallas_call(
        smoothed_kernel,
        out_shape=jax.ShapeDtypeStruct((2, CX, CY, CZ), f32),
        compiler_params=pltpu.CompilerParams(vmem_limit_bytes=VMEM_LIMIT),
    )(whole)


def shifted(values, axis, step):
    count = lax.axis_size(axis)
    return lax.ppermute(values, axis, [((i + step) % count, i) for i in range(count)])


def to_rows(store, base, row):
    for tile in range(row.shape[1] // LANES):
        store[pl.ds(base + tile, 1), :] = row[:, tile * LANES : (tile + 1) * LANES]


def select(rows, picked):
    size = rows.shape[0]
    return [
        jnp.sum(jnp.where(rows, picked[at * size : (at + 1) * size], 0.0), axis=0, keepdims=True)
        for at in range(picked.shape[0] // size)
    ]


def is_row(high, size):
    return lax.broadcasted_iota(jnp.int32, (size, high.shape[1]), 0) == high


def counted(flags):
    lanes = lax.broadcasted_iota(jnp.int32, (LANES, 2 * LANES), 1)
    upto = (lax.broadcasted_iota(jnp.int32, (LANES, 2 * LANES), 0) <= lanes) | (lanes >= LANES)
    counts = dot_nn(flags.astype(bf16), jnp.where(upto, 1.0, 0.0).astype(bf16))
    before = jnp.zeros((1, LANES), f32)
    rows = []
    for row in range(flags.shape[0]):
        rows.append(counts[row : row + 1, :LANES] + before)
        before = before + counts[row : row + 1, LANES:]
    return rows


def chains_kernel(positions, bonds, after, anchor, hot, high, apart, steps, placed):
    beads = positions.shape[1]
    bead_rows = beads // LANES
    count = bonds.shape[1]
    chains = beads - count
    length = beads // chains
    ends = 2 * chains
    bond_step = chunk_of(count, 6)
    for axis in range(3):
        to_rows(anchor, axis * bead_rows, positions[axis : axis + 1, :])

    total = jnp.zeros((3 * bead_rows, LANES), f32)
    for j in range(count // bond_step):
        where = slice(j * bond_step, (j + 1) * bond_step)
        index = [bonds[side : side + 1, where] for side in range(2)]
        highs = [i // LANES for i in index]
        lows = [i - h * LANES for i, h in zip(index, highs)]
        for side in range(2):
            rows = is_row(highs[side], bead_rows)
            values = (jnp.ones((1, bond_step), f32), highs[1 - side].astype(f32), lows[1 - side].astype(f32))
            left = [jnp.where(rows, value, 0.0).astype(bf16) for value in values]
            total = total + dot_nt(jnp.concatenate(left, axis=0), one_hot(lows[side], LANES))
    single = total[:bead_rows] == 1.0
    around = (total[bead_rows : 2 * bead_rows] * LANES + total[2 * bead_rows :]).astype(jnp.int32)
    around_high = around // LANES
    table = jnp.concatenate([around_high, around - around_high * LANES], axis=0).astype(f32).astype(bf16)

    flags = jnp.where(single, 1.0, 0.0)
    ranks = counted(flags)
    rank = jnp.concatenate(
        [jnp.where(flags[row : row + 1] > 0.0, ranks[row] - 1.0, -LANES) for row in range(bead_rows)], axis=1
    ).astype(jnp.int32)
    rank_high = jnp.where(rank < 0, -1, rank // LANES)
    bead = lax.broadcasted_iota(jnp.int32, (1, beads), 1)
    end_rows = -(-ends // (8 * LANES)) * 8
    rows = is_row(rank_high, end_rows)
    left = [jnp.where(rows, part.astype(f32), 0.0) for part in (bead // LANES, bead % LANES)]
    found = dot_nt(jnp.concatenate(left, axis=0).astype(bf16), one_hot(rank - rank_high * LANES, LANES))
    found = found[:end_rows] * LANES + found[end_rows:]
    first = jnp.concatenate([found[row : row + 1] for row in range(ends // LANES)], axis=1)

    def walk(m, carry):
        before, here = carry
        bead = here.astype(jnp.int32)
        bead_high = bead // LANES
        bead_low = bead - bead_high * LANES
        steps[pl.ds(m, 1), :] = bead_high.astype(f32)
        steps[pl.ds(length + m, 1), :] = bead_low.astype(f32)
        next_high, next_low = select(is_row(bead_high, bead_rows), dot_nn(table, one_hot(bead_low, LANES)))
        return here, next_high * LANES + next_low - before

    last, _ = lax.fori_loop(0, length, walk, (jnp.zeros_like(first), first))
    kept = jnp.where(first < last, 1.0, 0.0)
    flags = jnp.concatenate([kept[:, at : at + LANES] for at in range(0, ends, LANES)], axis=0)
    kept_rank = jnp.where(kept > 0.0, jnp.concatenate(counted(flags), axis=1) - 1.0, -1.0).astype(jnp.int32)
    order = dot_nt(steps[...].astype(bf16), one_hot(kept_rank, chains)).astype(jnp.int32)
    for m in range(length):
        where = slice(m * chains, (m + 1) * chains)
        high[:, where] = order[m : m + 1]
        hot[:, where] = one_hot(order[length + m : length + m + 1], LANES)

    anchor_table = jnp.concatenate(parts_of(anchor[...], 3), axis=1)
    wide = 4 * chains
    for j in range(beads // wide):
        where = slice(j * wide, (j + 1) * wide)
        rows = is_row(high[:, where], bead_rows)
        found = select(rows, dot_nn(anchor_table, jnp.concatenate([hot[:, where]] * 3, axis=0)))
        for axis in range(3):
            for at in range(4):
                placed[axis, 4 * j + at : 4 * j + at + 1, :] = found[axis][:, at * chains : (at + 1) * chains]
    for axis in range(3):
        apart[axis, : length - 1, :] = placed[axis, : length - 1, :] - placed[axis, 1:, :]
        apart[axis, length - 1 :, :] = jnp.zeros((1, chains), f32)


def order_chains(positions, bonds, after):
    beads = positions.shape[1]
    chains = beads - bonds.shape[1]
    length = beads // chains
    return pl.pallas_call(
        chains_kernel,
        out_shape=[
            jax.ShapeDtypeStruct((3 * beads // LANES, LANES), f32),
            jax.ShapeDtypeStruct((LANES, beads), bf16),
            jax.ShapeDtypeStruct((1, beads), jnp.int32),
            jax.ShapeDtypeStruct((3, length, chains), f32),
        ],
        in_specs=[pl.BlockSpec(), pl.BlockSpec(), pl.BlockSpec(memory_space=pl.ANY)],
        scratch_shapes=[pltpu.VMEM((2 * length, 2 * chains), f32), pltpu.VMEM((3, length, chains), f32)],
        compiler_params=pltpu.CompilerParams(vmem_limit_bytes=VMEM_WIDE),
    )(positions, bonds, after)


def finish_kernel(
    species_far,
    corner_slot_far,
    corner_weight_far,
    velocities_far,
    slopes,
    anchor_far,
    hot_far,
    high_far,
    apart_far,
    new_positions,
    new_velocities,
    table,
    shift,
    species,
    corner_slot,
    corner_weight,
    velocities,
    anchor,
    hot,
    high,
    apart,
    placed,
    sems,
    late_sems,
):
    plane, _, slots = slopes.shape
    blocks = slots // LANES
    highs = 2 * blocks * plane
    beads = corner_weight.shape[1]
    bead_rows = beads // LANES
    length, chains = apart.shape[1:]
    step = chunk_of(beads, 4)
    wait = chunk_copies(
        [
            (species_far, species),
            (corner_slot_far, corner_slot),
            (corner_weight_far, corner_weight),
            (velocities_far, velocities),
        ],
        sems,
        step,
        beads // step,
    )
    late = [
        pltpu.make_async_copy(source, target, late_sems.at[at])
        for at, (source, target) in enumerate(
            [(anchor_far, anchor), (hot_far, hot), (high_far, high), (apart_far, apart)]
        )
    ]
    for copy in late:
        copy.start()

    def collect(brick, carry):
        for axis in range(3):
            for kind in range(2):
                for block in range(blocks):
                    row = pl.ds((axis * 2 * blocks + kind * blocks + block) * plane + brick, 1)
                    at = kind * 3 + axis
                    table[row, :] = slopes[brick, at : at + 1, block * LANES : (block + 1) * LANES]
        return carry

    lax.fori_loop(0, plane, collect, 0, unroll=plane <= 8)
    slope_table = jnp.concatenate(parts_of(table[...], 2), axis=1)

    def force_body(j, carry):
        wait(j)
        where = pl.ds(pl.multiple_of(j * step, step), step)
        kind = species[:, where]
        total = jnp.zeros((3 * highs, step), f32)
        for corner in range(8):
            high, low = corner_keys(kind, corner_slot, corner, where, plane, blocks)
            weight = corner_weight[pl.ds(corner, 1), where]
            rows = lax.broadcasted_iota(jnp.int32, (highs, step), 0) == high
            weights = jnp.where(rows, weight, 0.0)
            hot_low = one_hot(low, LANES)
            picked = dot_nn(slope_table, jnp.concatenate([hot_low, hot_low], axis=0))
            total = total + picked * jnp.concatenate([weights] * 3, axis=0)
        for axis in range(3):
            force = -jnp.sum(total[axis * highs : (axis + 1) * highs], axis=0, keepdims=True)
            half = velocities[pl.ds(axis, 1), where] + 0.5 * time_step * force
            to_rows(shift, axis * bead_rows + j * (step // LANES), time_step * half)
        return carry

    lax.fori_loop(0, beads // step, force_body, 0)

    for copy in late:
        copy.wait()
    shift_table = jnp.concatenate(parts_of(shift[...], 2), axis=1)
    wide = 4 * chains
    for j in range(beads // wide):
        where = slice(j * wide, (j + 1) * wide)
        rows = is_row(high[:, where], bead_rows)
        found = select(rows, dot_nn(shift_table, jnp.concatenate([hot[:, where]] * 2, axis=0)))
        for axis in range(3):
            for at in range(4):
                placed[axis, 4 * j + at : 4 * j + at + 1, :] = found[axis][:, at * chains : (at + 1) * chains]
    between = [apart[axis] for axis in range(3)]
    before = [placed[axis] for axis in range(3)]
    moved = before
    for _ in range(SWEEPS):
        stretch = [between[axis] + (moved[axis] - pltpu.roll(moved[axis], length - 1, 0)) for axis in range(3)]
        excess = sum(s * s for s in stretch) - bond_length * bond_length
        along = sum(s * a for s, a in zip(stretch, between))
        factor = excess / (4.0 * jnp.maximum(along, 0.5 * bond_length * bond_length))
        pulls = [factor * between[axis] for axis in range(3)]
        moved = [moved[axis] - pulls[axis] + pltpu.roll(pulls[axis], 1, 0) for axis in range(3)]
    for axis in range(3):
        placed[axis] = moved[axis] - before[axis]
    total = jnp.zeros((6 * bead_rows, LANES), f32)
    for j in range(beads // wide):
        where = slice(j * wide, (j + 1) * wide)
        rows = is_row(high[:, where], bead_rows)
        parts = [
            parts_of(jnp.concatenate([placed[axis, 4 * j + at : 4 * j + at + 1, :] for at in range(4)], axis=1), 2)
            for axis in range(3)
        ]
        left = [
            jnp.where(rows, parts[axis][part].astype(f32), 0.0).astype(bf16) for part in range(2) for axis in range(3)
        ]
        total = total + dot_nt(jnp.concatenate(left, axis=0), hot[:, where])
    shift[...] = shift[...] + total[: 3 * bead_rows] + total[3 * bead_rows :]

    for axis in range(3):
        for tile in range(bead_rows):
            row = slice(axis * bead_rows + tile, axis * bead_rows + tile + 1)
            where = slice(tile * LANES, (tile + 1) * LANES)
            move = shift[row, :]
            new_positions[axis : axis + 1, where] = anchor[row, :] + move
            new_velocities[axis : axis + 1, where] = move / time_step


def finish(species, corner_slot, corner_weight, slopes, velocities, prepared):
    beads = velocities.shape[1]
    plane, _, slots = slopes.shape
    highs = 2 * (slots // LANES) * plane
    early = (species, corner_slot, corner_weight, velocities)
    late = tuple(prepared)
    return pl.pallas_call(
        finish_kernel,
        out_shape=[jax.ShapeDtypeStruct((3, beads), f32)] * 2,
        in_specs=[HBM] * len(early) + [pl.BlockSpec()] + [HBM] * len(late),
        scratch_shapes=[
            pltpu.VMEM((3 * highs, LANES), f32),
            pltpu.VMEM((3 * beads // LANES, LANES), f32),
            *(pltpu.VMEM(a.shape, a.dtype) for a in early + late),
            pltpu.VMEM(prepared[3].shape, f32),
            pltpu.SemaphoreType.DMA((len(early), beads // chunk_of(beads, 4))),
            pltpu.SemaphoreType.DMA((len(late),)),
        ],
        compiler_params=pltpu.CompilerParams(vmem_limit_bytes=VMEM_WIDE),
    )(*early, slopes, *late)


def on_device(positions, velocities, species, corner_slot, corner_weight, slot_cell, bond_pairs):
    slots = slot_cell.shape[2]
    bricks = Bricks(lax.axis_size("bx"), lax.axis_size("by"))
    species = species.reshape(1, -1)
    packets = deposit(bricks, species, corner_slot, corner_weight, slot_cell)
    received = lax.all_to_all(packets, ("bx", "by"), split_axis=0, concat_axis=0, tiled=True)
    prepared = order_chains(positions, bond_pairs, packets)
    field, below, above = fill(bricks, received, slots, prepared[3])
    from_above = shifted(below, "bz", 1)
    from_below = shifted(above, "bz", -1)
    turned = smooth(field, below, above)
    slopes, whole = pick_slopes(turned, from_below, from_above, slot_cell)
    returned = lax.all_to_all(slopes, ("bx", "by"), split_axis=0, concat_axis=0, tiled=True)
    smoothed = smoothed_of(whole)
    moved, new_velocities = finish(
        species, corner_slot, corner_weight, returned, velocities, prepared
    )
    return (moved, new_velocities, smoothed)


def solution(mesh):
    in_specs = (
        P(None, ("bx", "by", "bz")),
        P(None, ("bx", "by", "bz")),
        P(("bx", "by", "bz")),
        P(None, None, ("bx", "by", "bz")),
        P(None, ("bx", "by", "bz")),
        P(None, ("bx", "by", "bz"), None),
        P(None, ("bx", "by", "bz")),
    )
    out_specs = (
        P(None, ("bx", "by", "bz")),
        P(None, ("bx", "by", "bz")),
        P(None, "bx", "by", "bz"),
    )
    return jax.shard_map(
        on_device, mesh=mesh, in_specs=in_specs, out_specs=out_specs, check_vma=False
    )
```

```python
import functools
import math

import jax
import jax.numpy as jnp
from jax import lax
from jax.experimental import pallas as pl
from jax.experimental.pallas import tpu as pltpu
from jax.sharding import PartitionSpec as P

CX = 16
CY = 64
CZ = 64
BEADS_DEV = 4096
REACH = 3
SWEEPS = 4


spread_cells = 1.0
mixing = 10.0
stiffness = 5.0
time_step = 0.1
bond_length = 1.0


def gauss_taps():
    raw_list = [
        math.exp(-0.5 * (offset - REACH) ** 2 / spread_cells**2) for offset in range(2 * REACH + 1)
    ]
    tap_total = sum(raw_list)
    return [entry / tap_total for entry in raw_list]


LANES = 128
VMEM_LIMIT = 20 * 1024 * 1024
VMEM_WIDE = 60 * 1024 * 1024
HBM = pl.BlockSpec(memory_space=pltpu.HBM)
f32 = jnp.float32
bf16 = jnp.bfloat16


def parts_of(values, count):
    parts = []
    for _ in range(count):
        part = values.astype(bf16)
        parts.append(part)
        values = values - part.astype(f32)
    return parts


def one_hot(index, size):
    rows = lax.broadcasted_iota(jnp.int16, (size, index.shape[1]), 0)
    return jnp.where(rows == index.astype(jnp.int16), jnp.array(1, bf16), jnp.array(0, bf16))


def dot_nn(left, right):
    return lax.dot_general(left, right, (((1,), (0,)), ((), ())), preferred_element_type=f32)


def dot_nt(left, right):
    return lax.dot_general(left, right, (((1,), (1,)), ((), ())), preferred_element_type=f32)


def chunk_of(length, most):
    tiles = length // LANES
    best = max(t for t in range(1, most + 1) if tiles % t == 0)
    return best * LANES


def chunk_copies(pairs, sems, step, count):
    def copies(j):
        where = pl.ds(pl.multiple_of(j * step, step), step)
        for at, (source, target) in enumerate(pairs):
            lead = (slice(None),) * (len(source.shape) - 1)
            yield pltpu.make_async_copy(source.at[lead + (where,)], target.at[lead + (where,)], sems.at[at, j])

    def start(j, carry):
        for copy in copies(j):
            copy.start()
        return carry

    lax.fori_loop(0, count, start, 0, unroll=True)

    def wait(j):
        for copy in copies(j):
            copy.wait()

    return wait


def corner_keys(species, corner_slot, corner, where, plane, blocks):
    brick = corner_slot[0, pl.ds(corner, 1), where]
    slot = corner_slot[1, pl.ds(corner, 1), where]
    block = slot // LANES
    high = (species * blocks + block) * plane + brick
    return high, slot - block * LANES


def deposit_kernel(
    bricks,
    species_far,
    corner_slot_far,
    corner_weight_far,
    slot_cell_far,
    packets,
    sums,
    species,
    corner_slot,
    corner_weight,
    slot_cell,
    sems,
    cell_sem,
):
    plane, slots = slot_cell.shape[1:]
    blocks = slots // LANES
    highs = 2 * blocks * plane
    beads = corner_weight.shape[1]
    step = chunk_of(beads, 8)
    count_x, count_y = bricks.counts
    wait = chunk_copies(
        [(species_far, species), (corner_slot_far, corner_slot), (corner_weight_far, corner_weight)],
        sems,
        step,
        beads // step,
    )
    cell_copy = pltpu.make_async_copy(slot_cell_far, slot_cell, cell_sem)
    cell_copy.start()

    def body(j, total):
        wait(j)
        where = pl.ds(pl.multiple_of(j * step, step), step)
        kind = species[:, where]
        for corner in range(8):
            high, low = corner_keys(kind, corner_slot, corner, where, plane, blocks)
            weight = corner_weight[pl.ds(corner, 1), where]
            rows = lax.broadcasted_iota(jnp.int32, (highs, step), 0) == high
            left = [jnp.where(rows, p.astype(f32), 0.0).astype(bf16) for p in parts_of(weight, 2)]
            total = total + dot_nt(one_hot(low, LANES), jnp.concatenate(left, axis=0))
        return total

    total = lax.fori_loop(0, beads // step, body, jnp.zeros((LANES, 2 * highs), f32)).T
    sums[...] = total[:highs] + total[highs:]
    cell_copy.wait()
    cells = (slot_cell[0] * CY + slot_cell[1]) * CZ + slot_cell[2]
    first = 2 * blocks * len(bricks.offsets)

    def hand_out(target, carry):
        for near, (step_x, step_y) in enumerate(bricks.offsets):
            brick = lax.rem(target // count_y + step_x, count_x) * count_y + lax.rem(
                lax.rem(target, count_y) + step_y, count_y
            )
            for kind in range(2):
                for block in range(blocks):
                    row = (near * 2 + kind) * blocks + block
                    packets[target, row : row + 1, :] = sums[
                        pl.ds((kind * blocks + block) * plane + brick, 1), :
                    ]
        for block in range(blocks):
            rows = slice(first + block * plane, first + (block + 1) * plane)
            packets[target, rows, :] = cells[:, block * LANES : (block + 1) * LANES].astype(f32)
        return carry

    lax.fori_loop(0, plane, hand_out, 0, unroll=plane <= 8)


def deposit(bricks, species, corner_slot, corner_weight, slot_cell):
    plane, slots = slot_cell.shape[1:]
    blocks = slots // LANES
    rows = blocks * (2 * len(bricks.offsets) + plane)
    return pl.pallas_call(
        functools.partial(deposit_kernel, bricks),
        out_shape=jax.ShapeDtypeStruct((plane, rows, LANES), f32),
        in_specs=[HBM] * 4,
        scratch_shapes=[
            pltpu.VMEM((2 * blocks * plane, LANES), f32),
            pltpu.VMEM(species.shape, species.dtype),
            pltpu.VMEM(corner_slot.shape, corner_slot.dtype),
            pltpu.VMEM(corner_weight.shape, corner_weight.dtype),
            pltpu.VMEM(slot_cell.shape, slot_cell.dtype),
            pltpu.SemaphoreType.DMA((3, species.shape[1] // chunk_of(species.shape[1], 8))),
            pltpu.SemaphoreType.DMA(()),
        ],
        compiler_params=pltpu.CompilerParams(vmem_limit_bytes=VMEM_WIDE),
    )(species, corner_slot, corner_weight, slot_cell)


HALO = REACH + 1
PAD = 8


class Bricks:
    def __init__(self, count_x, count_y):
        self.counts = (count_x, count_y)
        self.sides_x = self.sides(count_x)
        self.sides_y = self.sides(count_y)
        self.offsets = [(x, y) for y in self.sides_y for x in self.sides_x]

    @staticmethod
    def sides(count):
        found = {}
        for side in (0, 1, -1):
            found.setdefault(side % count, []).append(side)
        return found


def tap_of(distance):
    taps = gauss_taps()
    result = jnp.zeros(distance.shape, f32)
    for far in range(REACH, -1, -1):
        result = jnp.where(distance == far, taps[REACH + far], result)
    return result


def filter_rows(load):
    taps = gauss_taps()
    result = taps[REACH] * load(REACH)
    for far in range(1, REACH + 1):
        result = result + taps[REACH + far] * (load(REACH - far) + load(REACH + far))
    return result


def fill_kernel(bricks, group, slots, received, after, field, below, above, columns, edges):
    plane = received.shape[0]
    blocks = slots // LANES
    first_cell = 2 * blocks * len(bricks.offsets)
    count_x, count_y = bricks.counts
    mine = (lax.axis_index("bx"), lax.axis_index("by"))
    scale = CX * CY * CZ / BEADS_DEV
    if plane > group:
        field[...] = jnp.zeros_like(field)

    def put(ref, index, value):
        if plane > group:
            value = value + ref[index]
        ref[index] = value

    def sources(g, carry):
        for near, (step_x, step_y) in enumerate(bricks.offsets):
            brick = lax.rem(mine[0] + step_x, count_x) * count_y + lax.rem(mine[1] + step_y, count_y)
            cells_xy = []
            for p in range(group):
                source = g * group + p
                cell = jnp.concatenate(
                    [received[brick, pl.ds(first_cell + block * plane + source, 1), :] for block in range(blocks)],
                    axis=1,
                ).astype(jnp.int32)
                cells_xy.append((cell // (CY * CZ), cell // CZ % CY))
                z = cell % CZ
                amounts = []
                for k in range(2):
                    row = (near * 2 + k) * blocks
                    amounts.append(
                        scale
                        * jnp.concatenate(
                            [received[source, row + block : row + block + 1, :] for block in range(blocks)], axis=1
                        )
                    )
                layer = lax.broadcasted_iota(jnp.int32, (CZ, slots), 0) == z
                lane = slice(p * slots, (p + 1) * slots)
                for k in range(2):
                    for at, part in enumerate(parts_of(amounts[k], 2)):
                        columns[at * 2 * CZ + k * CZ : at * 2 * CZ + (k + 1) * CZ, lane] = jnp.where(
                            layer, part.astype(f32), 0.0
                        ).astype(bf16)
            for side_x in bricks.sides_x[step_x]:
                first_x, width_x, from_x = {
                    0: (HALO, CX, 0),
                    1: (HALO + CX, HALO, 0),
                    -1: (0, HALO, CX - HALO),
                }[side_x]
                for side_y in bricks.sides_y[step_y]:
                    first_y, width_y, from_y = {
                        0: (PAD, CY, 0),
                        1: (PAD + CY, PAD, 0),
                        -1: (0, PAD, CY - PAD),
                    }[side_y]
                    keys = [
                        jnp.where(
                            (y >= from_y) & (y < from_y + width_y), (x - from_x) * width_y + (y - from_y), -1
                        )
                        for x, y in cells_xy
                    ]
                    layers = min(width_x, 256 // width_y)
                    rows = layers * width_y
                    for start in range(0, width_x, layers):
                        hot = jnp.concatenate(
                            [one_hot(key - start * width_y, rows) for key in keys], axis=1
                        )
                        sums = dot_nt(hot, columns[...])
                        sums = sums[:, : 2 * CZ] + sums[:, 2 * CZ :]
                        for layer in range(layers):
                            at = first_x + start + layer
                            piece = slice(layer * width_y, (layer + 1) * width_y)
                            put(field, (at, slice(first_y, first_y + width_y), slice(None)), sums[piece])
        return carry

    lax.fori_loop(0, plane // group, sources, 0)

    def pair_of(shape, dim):
        index = lax.broadcasted_iota(jnp.int32, shape, dim)
        return index // CZ, index % CZ

    square = (2 * CZ, 2 * CZ)
    (kind_from, z_from), (kind_to, z_to) = pair_of(square, 0), pair_of(square, 1)
    inner = parts_of(jnp.where(kind_from == kind_to, tap_of(jnp.abs(z_to - z_from)), 0.0), 2)
    shape = (4 * HALO, 2 * CZ)
    kind_from, z_from = pair_of(shape, 1)
    row_of = lax.broadcasted_iota(jnp.int32, shape, 0)
    layer = row_of % HALO
    layer = jnp.where(row_of < 2 * HALO, layer - REACH, layer + (CZ - 1))
    kind_to = row_of // HALO % 2
    outer = parts_of(jnp.where(kind_from == kind_to, tap_of(jnp.abs(layer - z_from)), 0.0), 2)
    inner_both = jnp.concatenate([inner[0], inner[0]], axis=0)
    outer_both = jnp.concatenate([outer[0], outer[0]], axis=1)
    wide = CY + 2 * PAD
    layers = 6 if (CX + 2 * HALO) % 6 == 0 else 1
    for start in range(0, CX + 2 * HALO, layers):
        parts = parts_of(field[start : start + layers].reshape(layers * wide, 2 * CZ), 2)
        both = jnp.concatenate(parts, axis=1)
        done = dot_nn(both, inner_both) + dot_nn(parts[0], inner[1])
        field[start : start + layers] = done.reshape(layers, wide, 2 * CZ)
        edge = dot_nt(outer_both, both) + dot_nt(outer[1], parts[0])
        for at in range(layers):
            row = jnp.concatenate(
                [edge[:, at * wide : (at + 1) * wide], jnp.zeros((4 * HALO, LANES - wide), f32)], axis=1
            )
            edges[start + at] = pltpu.roll(row, LANES - PAD, 1)

    for layer in range(CX + 2):
        along_x = filter_rows(lambda j: edges[layer + j])
        both = filter_rows(lambda j: pltpu.roll(along_x, (REACH - j) % LANES, 1))
        below[layer] = both[: 2 * HALO]
        above[layer] = both[2 * HALO :]


def fill(bricks, received, slots, after):
    plane = received.shape[0]
    group = 8 if plane % 8 == 0 else plane
    return pl.pallas_call(
        functools.partial(fill_kernel, bricks, group, slots),
        out_shape=[
            jax.ShapeDtypeStruct((CX + 2 * HALO, CY + 2 * PAD, 2 * CZ), f32),
            jax.ShapeDtypeStruct((CX + 2, 2 * HALO, LANES), f32),
            jax.ShapeDtypeStruct((CX + 2, 2 * HALO, LANES), f32),
        ],
        in_specs=[pl.BlockSpec(), pl.BlockSpec(memory_space=pl.ANY)],
        scratch_shapes=[
            pltpu.VMEM((4 * CZ, group * slots), bf16),
            pltpu.VMEM((CX + 2 * HALO, 4 * HALO, LANES), f32),
        ],
        compiler_params=pltpu.CompilerParams(vmem_limit_bytes=VMEM_LIMIT),
    )(received, after)


def smooth_kernel(field, below, above, turned, line):
    line[...] = jnp.zeros_like(line)
    wide = CY + PAD
    for layer in range(CX + 2):
        line[PAD : PAD + CY + 2 * PAD, :] = filter_rows(lambda j: field[layer + j])
        main = filter_rows(lambda j: line[2 * PAD + j - REACH : 2 * PAD + j - REACH + wide, :])
        before = filter_rows(lambda j: line[PAD + j - REACH : 2 * PAD + j - REACH, :])
        rest = jnp.zeros((LANES - wide - PAD, 2 * CZ), f32)
        flipped = jnp.concatenate([main, rest, before], axis=0).T
        for k in range(2):
            turned[layer, k, PAD : PAD + CZ, :] = flipped[k * CZ : (k + 1) * CZ]
            turned[layer, k, PAD - 1 : PAD, :] = below[layer, k * HALO + REACH - 1 : k * HALO + REACH, :]
            turned[layer, k, PAD + CZ : PAD + CZ + 1, :] = above[layer, k * HALO + 1 : k * HALO + 2, :]


def smooth(field, below, above):
    return pl.pallas_call(
        smooth_kernel,
        out_shape=jax.ShapeDtypeStruct((CX + 2, 2, CZ + 2 * PAD, LANES), f32),
        scratch_shapes=[pltpu.VMEM((CY + 5 * PAD, 2 * CZ), f32)],
        compiler_params=pltpu.CompilerParams(vmem_limit_bytes=VMEM_LIMIT),
    )(field, below, above)


def slope_kernel(turned, from_below, from_above, place, slopes, whole, table):
    plane, _, slots = slopes.shape
    lanes = lax.broadcasted_iota(jnp.int32, (CZ, LANES), 1)
    for layer in range(CX + 2):
        for k in range(2):
            whole[layer, k] = turned[layer, k]
            at = slice(PAD - 1, PAD - 1 + HALO)
            whole[layer, k, at, :] = whole[layer, k, at, :] + from_below[layer, k * HALO : (k + 1) * HALO, :]
            at = slice(PAD + CZ - REACH, PAD + CZ - REACH + HALO)
            whole[layer, k, at, :] = whole[layer, k, at, :] + from_above[layer, k * HALO : (k + 1) * HALO, :]
    for pair in range(CX // 2):
        for k in range(2):
            halves = []
            for layer in (1 + 2 * pair, 2 + 2 * pair):
                inner = slice(PAD, PAD + CZ)
                here = whole[layer, k, inner, :]
                halves.append(
                    (
                        whole[layer + 1, k, inner, :] - whole[layer - 1, k, inner, :],
                        pltpu.roll(here, LANES - 1, 1) - pltpu.roll(here, 1, 1),
                        whole[layer, k, PAD + 1 : PAD + 1 + CZ, :] - whole[layer, k, PAD - 1 : PAD - 1 + CZ, :],
                    )
                )
            for axis in range(3):
                both = 0.5 * jnp.where(lanes < CY, halves[0][axis], pltpu.roll(halves[1][axis], CY, 1))
                for at, part in enumerate(parts_of(both, 2)):
                    start = at * CX * CY + pair * LANES
                    table[(axis * 2 + k) * CZ : (axis * 2 + k + 1) * CZ, start : start + LANES] = part

    def source(p, carry):
        row = pl.ds(p, 1)
        hot = one_hot(place[0, row, :] * CY + place[1, row, :], CX * CY)
        picked = dot_nn(table[:, : CX * CY], hot) + dot_nn(table[:, CX * CY :], hot)
        depth = lax.broadcasted_iota(jnp.int32, (CZ, slots), 0) == place[2, row, :]
        for axis in range(3):
            steep = [
                jnp.sum(
                    jnp.where(depth, picked[(axis * 2 + k) * CZ : (axis * 2 + k + 1) * CZ], 0.0),
                    axis=0,
                    keepdims=True,
                )
                for k in range(2)
            ]
            joint = stiffness * (steep[0] + steep[1])
            for k in range(2):
                slopes[p, k * 3 + axis : k * 3 + axis + 1, :] = mixing * steep[1 - k] + joint
        return carry

    lax.fori_loop(0, plane, source, 0, unroll=8 if plane % 8 == 0 else 1)


def pick_slopes(turned, from_below, from_above, place):
    plane, slots = place.shape[1:]
    return pl.pallas_call(
        slope_kernel,
        out_shape=[
            jax.ShapeDtypeStruct((plane, 6, slots), f32),
            jax.ShapeDtypeStruct(turned.shape, f32),
        ],
        scratch_shapes=[pltpu.VMEM((6 * CZ, 2 * CX * CY), bf16)],
        compiler_params=pltpu.CompilerParams(vmem_limit_bytes=VMEM_LIMIT),
    )(turned, from_below, from_above, place)


def smoothed_kernel(whole, smoothed):
    for layer in range(CX):
        for k in range(2):
            smoothed[k, layer] = whole[layer + 1, k, PAD : PAD + CZ, :].T[:CY]


def smoothed_of(whole):
    return pl.pallas_call(
        smoothed_kernel,
        out_shape=jax.ShapeDtypeStruct((2, CX, CY, CZ), f32),
        compiler_params=pltpu.CompilerParams(vmem_limit_bytes=VMEM_LIMIT),
    )(whole)


def shifted(values, axis, step):
    count = lax.axis_size(axis)
    return lax.ppermute(values, axis, [((i + step) % count, i) for i in range(count)])


def to_rows(store, base, row):
    for tile in range(row.shape[1] // LANES):
        store[pl.ds(base + tile, 1), :] = row[:, tile * LANES : (tile + 1) * LANES]


def select(rows, picked):
    size = rows.shape[0]
    return [
        jnp.sum(jnp.where(rows, picked[at * size : (at + 1) * size], 0.0), axis=0, keepdims=True)
        for at in range(picked.shape[0] // size)
    ]


def is_row(high, size):
    return lax.broadcasted_iota(jnp.int32, (size, high.shape[1]), 0) == high


def counted(flags):
    lanes = lax.broadcasted_iota(jnp.int32, (LANES, 2 * LANES), 1)
    upto = (lax.broadcasted_iota(jnp.int32, (LANES, 2 * LANES), 0) <= lanes) | (lanes >= LANES)
    counts = dot_nn(flags.astype(bf16), jnp.where(upto, 1.0, 0.0).astype(bf16))
    before = jnp.zeros((1, LANES), f32)
    rows = []
    for row in range(flags.shape[0]):
        rows.append(counts[row : row + 1, :LANES] + before)
        before = before + counts[row : row + 1, LANES:]
    return rows


def chains_kernel(positions, bonds, after, anchor, hot, high, apart, steps, placed):
    beads = positions.shape[1]
    bead_rows = beads // LANES
    count = bonds.shape[1]
    chains = beads - count
    length = beads // chains
    ends = 2 * chains
    bond_step = chunk_of(count, 6)
    for axis in range(3):
        to_rows(anchor, axis * bead_rows, positions[axis : axis + 1, :])

    total = jnp.zeros((3 * bead_rows, LANES), f32)
    for j in range(count // bond_step):
        where = slice(j * bond_step, (j + 1) * bond_step)
        index = [bonds[side : side + 1, where] for side in range(2)]
        highs = [i // LANES for i in index]
        lows = [i - h * LANES for i, h in zip(index, highs)]
        for side in range(2):
            rows = is_row(highs[side], bead_rows)
            values = (jnp.ones((1, bond_step), f32), highs[1 - side].astype(f32), lows[1 - side].astype(f32))
            left = [jnp.where(rows, value, 0.0).astype(bf16) for value in values]
            total = total + dot_nt(jnp.concatenate(left, axis=0), one_hot(lows[side], LANES))
    single = total[:bead_rows] == 1.0
    around = (total[bead_rows : 2 * bead_rows] * LANES + total[2 * bead_rows :]).astype(jnp.int32)
    around_high = around // LANES
    table = jnp.concatenate([around_high, around - around_high * LANES], axis=0).astype(f32).astype(bf16)

    flags = jnp.where(single, 1.0, 0.0)
    ranks = counted(flags)
    rank = jnp.concatenate(
        [jnp.where(flags[row : row + 1] > 0.0, ranks[row] - 1.0, -LANES) for row in range(bead_rows)], axis=1
    ).astype(jnp.int32)
    rank_high = jnp.where(rank < 0, -1, rank // LANES)
    bead = lax.broadcasted_iota(jnp.int32, (1, beads), 1)
    end_rows = -(-ends // (8 * LANES)) * 8
    rows = is_row(rank_high, end_rows)
    left = [jnp.where(rows, part.astype(f32), 0.0) for part in (bead // LANES, bead % LANES)]
    found = dot_nt(jnp.concatenate(left, axis=0).astype(bf16), one_hot(rank - rank_high * LANES, LANES))
    found = found[:end_rows] * LANES + found[end_rows:]
    first = jnp.concatenate([found[row : row + 1] for row in range(ends // LANES)], axis=1)

    def walk(m, carry):
        before, here = carry
        bead = here.astype(jnp.int32)
        bead_high = bead // LANES
        bead_low = bead - bead_high * LANES
        steps[pl.ds(m, 1), :] = bead_high.astype(f32)
        steps[pl.ds(length + m, 1), :] = bead_low.astype(f32)
        next_high, next_low = select(is_row(bead_high, bead_rows), dot_nn(table, one_hot(bead_low, LANES)))
        return here, next_high * LANES + next_low - before

    last, _ = lax.fori_loop(0, length, walk, (jnp.zeros_like(first), first))
    kept = jnp.where(first < last, 1.0, 0.0)
    flags = jnp.concatenate([kept[:, at : at + LANES] for at in range(0, ends, LANES)], axis=0)
    kept_rank = jnp.where(kept > 0.0, jnp.concatenate(counted(flags), axis=1) - 1.0, -1.0).astype(jnp.int32)
    order = dot_nt(steps[...].astype(bf16), one_hot(kept_rank, chains)).astype(jnp.int32)
    for m in range(length):
        where = slice(m * chains, (m + 1) * chains)
        high[:, where] = order[m : m + 1]
        hot[:, where] = one_hot(order[length + m : length + m + 1], LANES)

    anchor_table = jnp.concatenate(parts_of(anchor[...], 3), axis=1)
    wide = 4 * chains
    for j in range(beads // wide):
        where = slice(j * wide, (j + 1) * wide)
        rows = is_row(high[:, where], bead_rows)
        found = select(rows, dot_nn(anchor_table, jnp.concatenate([hot[:, where]] * 3, axis=0)))
        for axis in range(3):
            for at in range(4):
                placed[axis, 4 * j + at : 4 * j + at + 1, :] = found[axis][:, at * chains : (at + 1) * chains]
    for axis in range(3):
        apart[axis, : length - 1, :] = placed[axis, : length - 1, :] - placed[axis, 1:, :]
        apart[axis, length - 1 :, :] = jnp.zeros((1, chains), f32)


def order_chains(positions, bonds, after):
    beads = positions.shape[1]
    chains = beads - bonds.shape[1]
    length = beads // chains
    return pl.pallas_call(
        chains_kernel,
        out_shape=[
            jax.ShapeDtypeStruct((3 * beads // LANES, LANES), f32),
            jax.ShapeDtypeStruct((LANES, beads), bf16),
            jax.ShapeDtypeStruct((1, beads), jnp.int32),
            jax.ShapeDtypeStruct((3, length, chains), f32),
        ],
        in_specs=[pl.BlockSpec(), pl.BlockSpec(), pl.BlockSpec(memory_space=pl.ANY)],
        scratch_shapes=[pltpu.VMEM((2 * length, 2 * chains), f32), pltpu.VMEM((3, length, chains), f32)],
        compiler_params=pltpu.CompilerParams(vmem_limit_bytes=VMEM_WIDE),
    )(positions, bonds, after)


def finish_kernel(
    species_far,
    corner_slot_far,
    corner_weight_far,
    velocities_far,
    slopes,
    anchor_far,
    hot_far,
    high_far,
    apart_far,
    new_positions,
    new_velocities,
    table,
    shift,
    species,
    corner_slot,
    corner_weight,
    velocities,
    anchor,
    hot,
    high,
    apart,
    placed,
    sems,
    late_sems,
):
    plane, _, slots = slopes.shape
    blocks = slots // LANES
    highs = 2 * blocks * plane
    beads = corner_weight.shape[1]
    bead_rows = beads // LANES
    length, chains = apart.shape[1:]
    step = chunk_of(beads, 4)
    wait = chunk_copies(
        [
            (species_far, species),
            (corner_slot_far, corner_slot),
            (corner_weight_far, corner_weight),
            (velocities_far, velocities),
        ],
        sems,
        step,
        beads // step,
    )
    late = [
        pltpu.make_async_copy(source, target, late_sems.at[at])
        for at, (source, target) in enumerate(
            [(anchor_far, anchor), (hot_far, hot), (high_far, high), (apart_far, apart)]
        )
    ]
    for copy in late:
        copy.start()

    def collect(brick, carry):
        for axis in range(3):
            for kind in range(2):
                for block in range(blocks):
                    row = pl.ds((axis * 2 * blocks + kind * blocks + block) * plane + brick, 1)
                    at = kind * 3 + axis
                    table[row, :] = slopes[brick, at : at + 1, block * LANES : (block + 1) * LANES]
        return carry

    lax.fori_loop(0, plane, collect, 0, unroll=plane <= 8)
    slope_table = jnp.concatenate(parts_of(table[...], 2), axis=1)

    def force_body(j, carry):
        wait(j)
        where = pl.ds(pl.multiple_of(j * step, step), step)
        kind = species[:, where]
        total = jnp.zeros((3 * highs, step), f32)
        for corner in range(8):
            high, low = corner_keys(kind, corner_slot, corner, where, plane, blocks)
            weight = corner_weight[pl.ds(corner, 1), where]
            rows = lax.broadcasted_iota(jnp.int32, (highs, step), 0) == high
            weights = jnp.where(rows, weight, 0.0)
            hot_low = one_hot(low, LANES)
            picked = dot_nn(slope_table, jnp.concatenate([hot_low, hot_low], axis=0))
            total = total + picked * jnp.concatenate([weights] * 3, axis=0)
        for axis in range(3):
            force = -jnp.sum(total[axis * highs : (axis + 1) * highs], axis=0, keepdims=True)
            half = velocities[pl.ds(axis, 1), where] + 0.5 * time_step * force
            to_rows(shift, axis * bead_rows + j * (step // LANES), time_step * half)
        return carry

    lax.fori_loop(0, beads // step, force_body, 0)

    for copy in late:
        copy.wait()
    shift_table = jnp.concatenate(parts_of(shift[...], 2), axis=1)
    wide = 4 * chains
    for j in range(beads // wide):
        where = slice(j * wide, (j + 1) * wide)
        rows = is_row(high[:, where], bead_rows)
        found = select(rows, dot_nn(shift_table, jnp.concatenate([hot[:, where]] * 2, axis=0)))
        for axis in range(3):
            for at in range(4):
                placed[axis, 4 * j + at : 4 * j + at + 1, :] = found[axis][:, at * chains : (at + 1) * chains]
    between = [apart[axis] for axis in range(3)]
    before = [placed[axis] for axis in range(3)]
    moved = before
    for _ in range(SWEEPS):
        stretch = [between[axis] + (moved[axis] - pltpu.roll(moved[axis], length - 1, 0)) for axis in range(3)]
        excess = sum(s * s for s in stretch) - bond_length * bond_length
        along = sum(s * a for s, a in zip(stretch, between))
        factor = excess / (4.0 * jnp.maximum(along, 0.5 * bond_length * bond_length))
        pulls = [factor * between[axis] for axis in range(3)]
        moved = [moved[axis] - pulls[axis] + pltpu.roll(pulls[axis], 1, 0) for axis in range(3)]
    for axis in range(3):
        placed[axis] = moved[axis] - before[axis]
    total = jnp.zeros((6 * bead_rows, LANES), f32)
    for j in range(beads // wide):
        where = slice(j * wide, (j + 1) * wide)
        rows = is_row(high[:, where], bead_rows)
        parts = [
            parts_of(jnp.concatenate([placed[axis, 4 * j + at : 4 * j + at + 1, :] for at in range(4)], axis=1), 2)
            for axis in range(3)
        ]
        left = [
            jnp.where(rows, parts[axis][part].astype(f32), 0.0).astype(bf16) for part in range(2) for axis in range(3)
        ]
        total = total + dot_nt(jnp.concatenate(left, axis=0), hot[:, where])
    shift[...] = shift[...] + total[: 3 * bead_rows] + total[3 * bead_rows :]

    for axis in range(3):
        for tile in range(bead_rows):
            row = slice(axis * bead_rows + tile, axis * bead_rows + tile + 1)
            where = slice(tile * LANES, (tile + 1) * LANES)
            move = shift[row, :]
            new_positions[axis : axis + 1, where] = anchor[row, :] + move
            new_velocities[axis : axis + 1, where] = move / time_step


def finish(species, corner_slot, corner_weight, slopes, velocities, prepared):
    beads = velocities.shape[1]
    plane, _, slots = slopes.shape
    highs = 2 * (slots // LANES) * plane
    early = (species, corner_slot, corner_weight, velocities)
    late = tuple(prepared)
    return pl.pallas_call(
        finish_kernel,
        out_shape=[jax.ShapeDtypeStruct((3, beads), f32)] * 2,
        in_specs=[HBM] * len(early) + [pl.BlockSpec()] + [HBM] * len(late),
        scratch_shapes=[
            pltpu.VMEM((3 * highs, LANES), f32),
            pltpu.VMEM((3 * beads // LANES, LANES), f32),
            *(pltpu.VMEM(a.shape, a.dtype) for a in early + late),
            pltpu.VMEM(prepared[3].shape, f32),
            pltpu.SemaphoreType.DMA((len(early), beads // chunk_of(beads, 4))),
            pltpu.SemaphoreType.DMA((len(late),)),
        ],
        compiler_params=pltpu.CompilerParams(vmem_limit_bytes=VMEM_WIDE),
    )(*early, slopes, *late)


def on_device(positions, velocities, species, corner_slot, corner_weight, slot_cell, bond_pairs):
    slots = slot_cell.shape[2]
    bricks = Bricks(lax.axis_size("bx"), lax.axis_size("by"))
    species = species.reshape(1, -1)
    packets = deposit(bricks, species, corner_slot, corner_weight, slot_cell)
    received = lax.all_to_all(packets, ("bx", "by"), split_axis=0, concat_axis=0, tiled=True)
    prepared = order_chains(positions, bond_pairs, packets)
    field, below, above = fill(bricks, received, slots, prepared[3])
    from_above = shifted(below, "bz", 1)
    from_below = shifted(above, "bz", -1)
    turned = smooth(field, below, above)
    slopes, whole = pick_slopes(turned, from_below, from_above, slot_cell)
    returned = lax.all_to_all(slopes, ("bx", "by"), split_axis=0, concat_axis=0, tiled=True)
    smoothed = smoothed_of(whole)
    moved, new_velocities = finish(
        species, corner_slot, corner_weight, returned, velocities, prepared
    )
    return (moved, new_velocities, smoothed)


def solution(mesh):
    in_specs = (
        P(None, ("bx", "by", "bz")),
        P(None, ("bx", "by", "bz")),
        P(("bx", "by", "bz")),
        P(None, None, ("bx", "by", "bz")),
        P(None, ("bx", "by", "bz")),
        P(None, ("bx", "by", "bz"), None),
        P(None, ("bx", "by", "bz")),
    )
    out_specs = (
        P(None, ("bx", "by", "bz")),
        P(None, ("bx", "by", "bz")),
        P(None, "bx", "by", "bz"),
    )
    return jax.shard_map(
        on_device, mesh=mesh, in_specs=in_specs, out_specs=out_specs, check_vma=False
    )
```

```python
import functools
import math

import jax
import jax.numpy as jnp
from jax import lax
from jax.experimental import pallas as pl
from jax.experimental.pallas import tpu as pltpu
from jax.sharding import PartitionSpec as P

CX = 16
CY = 64
CZ = 64
BEADS_DEV = 4096
REACH = 3
SWEEPS = 4


spread_cells = 1.0
mixing = 10.0
stiffness = 5.0
time_step = 0.1
bond_length = 1.0


def gauss_taps():
    raw_list = [
        math.exp(-0.5 * (offset - REACH) ** 2 / spread_cells**2) for offset in range(2 * REACH + 1)
    ]
    tap_total = sum(raw_list)
    return [entry / tap_total for entry in raw_list]


LANES = 128
VMEM_LIMIT = 20 * 1024 * 1024
VMEM_STAGE = 4 * 1024 * 1024
VMEM_WIDE = 60 * 1024 * 1024
HBM = pl.BlockSpec(memory_space=pltpu.HBM)
f32 = jnp.float32
bf16 = jnp.bfloat16


def parts_of(values, count):
    parts = []
    for _ in range(count):
        part = values.astype(bf16)
        parts.append(part)
        values = values - part.astype(f32)
    return parts


def one_hot(index, size):
    rows = lax.broadcasted_iota(jnp.int16, (size, index.shape[1]), 0)
    return jnp.where(rows == index.astype(jnp.int16), jnp.array(1, bf16), jnp.array(0, bf16))


def dot_nn(left, right):
    return lax.dot_general(left, right, (((1,), (0,)), ((), ())), preferred_element_type=f32)


def dot_nt(left, right):
    return lax.dot_general(left, right, (((1,), (1,)), ((), ())), preferred_element_type=f32)


def chunk_of(length, most):
    tiles = length // LANES
    best = max(t for t in range(1, most + 1) if tiles % t == 0)
    return best * LANES


def chunk_copies(pairs, sems, step, count):
    def copies(j):
        where = pl.ds(pl.multiple_of(j * step, step), step)
        for at, (source, target) in enumerate(pairs):
            lead = (slice(None),) * (len(source.shape) - 1)
            yield pltpu.make_async_copy(source.at[lead + (where,)], target.at[lead + (where,)], sems.at[at, j])

    def start(j, carry):
        for copy in copies(j):
            copy.start()
        return carry

    lax.fori_loop(0, count, start, 0, unroll=True)

    def wait(j):
        for copy in copies(j):
            copy.wait()

    return wait


def corner_keys(species, corner_slot, corner, where, plane, blocks):
    brick = corner_slot[0, pl.ds(corner, 1), where]
    slot = corner_slot[1, pl.ds(corner, 1), where]
    block = slot // LANES
    high = (species * blocks + block) * plane + brick
    return high, slot - block * LANES


def deposit_kernel(
    bricks,
    species_far,
    corner_slot_far,
    corner_weight_far,
    slot_cell_far,
    packets,
    sums,
    species,
    corner_slot,
    corner_weight,
    slot_cell,
    sems,
    cell_sem,
):
    plane, slots = slot_cell.shape[1:]
    blocks = slots // LANES
    highs = 2 * blocks * plane
    beads = corner_weight.shape[1]
    step = chunk_of(beads, 8)
    count_x, count_y = bricks.counts
    wait = chunk_copies(
        [(species_far, species), (corner_slot_far, corner_slot), (corner_weight_far, corner_weight)],
        sems,
        step,
        beads // step,
    )
    cell_copy = pltpu.make_async_copy(slot_cell_far, slot_cell, cell_sem)
    cell_copy.start()

    def body(j, total):
        wait(j)
        where = pl.ds(pl.multiple_of(j * step, step), step)
        kind = species[:, where]
        for corner in range(8):
            high, low = corner_keys(kind, corner_slot, corner, where, plane, blocks)
            weight = corner_weight[pl.ds(corner, 1), where]
            rows = lax.broadcasted_iota(jnp.int32, (highs, step), 0) == high
            left = [jnp.where(rows, p.astype(f32), 0.0).astype(bf16) for p in parts_of(weight, 2)]
            total = total + dot_nt(one_hot(low, LANES), jnp.concatenate(left, axis=0))
        return total

    total = lax.fori_loop(0, beads // step, body, jnp.zeros((LANES, 2 * highs), f32)).T
    sums[...] = total[:highs] + total[highs:]
    cell_copy.wait()
    cells = (slot_cell[0] * CY + slot_cell[1]) * CZ + slot_cell[2]
    first = 2 * blocks * len(bricks.offsets)

    def hand_out(target, carry):
        for near, (step_x, step_y) in enumerate(bricks.offsets):
            brick = lax.rem(target // count_y + step_x, count_x) * count_y + lax.rem(
                lax.rem(target, count_y) + step_y, count_y
            )
            for kind in range(2):
                for block in range(blocks):
                    row = (near * 2 + kind) * blocks + block
                    packets[target, row : row + 1, :] = sums[
                        pl.ds((kind * blocks + block) * plane + brick, 1), :
                    ]
        for block in range(blocks):
            rows = slice(first + block * plane, first + (block + 1) * plane)
            packets[target, rows, :] = cells[:, block * LANES : (block + 1) * LANES].astype(f32)
        return carry

    lax.fori_loop(0, plane, hand_out, 0, unroll=plane <= 8)


def deposit(bricks, species, corner_slot, corner_weight, slot_cell):
    plane, slots = slot_cell.shape[1:]
    blocks = slots // LANES
    rows = blocks * (2 * len(bricks.offsets) + plane)
    return pl.pallas_call(
        functools.partial(deposit_kernel, bricks),
        out_shape=jax.ShapeDtypeStruct((plane, rows, LANES), f32),
        in_specs=[HBM] * 4,
        scratch_shapes=[
            pltpu.VMEM((2 * blocks * plane, LANES), f32),
            pltpu.VMEM(species.shape, species.dtype),
            pltpu.VMEM(corner_slot.shape, corner_slot.dtype),
            pltpu.VMEM(corner_weight.shape, corner_weight.dtype),
            pltpu.VMEM(slot_cell.shape, slot_cell.dtype),
            pltpu.SemaphoreType.DMA((3, species.shape[1] // chunk_of(species.shape[1], 8))),
            pltpu.SemaphoreType.DMA(()),
        ],
        compiler_params=pltpu.CompilerParams(vmem_limit_bytes=VMEM_WIDE),
    )(species, corner_slot, corner_weight, slot_cell)


HALO = REACH + 1
PAD = 8


class Bricks:
    def __init__(self, count_x, count_y):
        self.counts = (count_x, count_y)
        self.sides_x = self.sides(count_x)
        self.sides_y = self.sides(count_y)
        self.offsets = [(x, y) for y in self.sides_y for x in self.sides_x]

    @staticmethod
    def sides(count):
        found = {}
        for side in (0, 1, -1):
            found.setdefault(side % count, []).append(side)
        return found


def tap_of(distance):
    taps = gauss_taps()
    result = jnp.zeros(distance.shape, f32)
    for far in range(REACH, -1, -1):
        result = jnp.where(distance == far, taps[REACH + far], result)
    return result


def filter_rows(load):
    taps = gauss_taps()
    result = taps[REACH] * load(REACH)
    for far in range(1, REACH + 1):
        result = result + taps[REACH + far] * (load(REACH - far) + load(REACH + far))
    return result


def fill_kernel(bricks, group, slots, received, after, field, below, above, columns, edges):
    plane = received.shape[0]
    blocks = slots // LANES
    first_cell = 2 * blocks * len(bricks.offsets)
    count_x, count_y = bricks.counts
    mine = (lax.axis_index("bx"), lax.axis_index("by"))
    scale = CX * CY * CZ / BEADS_DEV
    if plane > group:
        field[...] = jnp.zeros_like(field)

    def put(ref, index, value):
        if plane > group:
            value = value + ref[index]
        ref[index] = value

    def sources(g, carry):
        for near, (step_x, step_y) in enumerate(bricks.offsets):
            brick = lax.rem(mine[0] + step_x, count_x) * count_y + lax.rem(mine[1] + step_y, count_y)
            cells_xy = []
            for p in range(group):
                source = g * group + p
                cell = jnp.concatenate(
                    [received[brick, pl.ds(first_cell + block * plane + source, 1), :] for block in range(blocks)],
                    axis=1,
                ).astype(jnp.int32)
                cells_xy.append((cell // (CY * CZ), cell // CZ % CY))
                z = cell % CZ
                amounts = []
                for k in range(2):
                    row = (near * 2 + k) * blocks
                    amounts.append(
                        scale
                        * jnp.concatenate(
                            [received[source, row + block : row + block + 1, :] for block in range(blocks)], axis=1
                        )
                    )
                layer = lax.broadcasted_iota(jnp.int32, (CZ, slots), 0) == z
                lane = slice(p * slots, (p + 1) * slots)
                for k in range(2):
                    for at, part in enumerate(parts_of(amounts[k], 2)):
                        columns[at * 2 * CZ + k * CZ : at * 2 * CZ + (k + 1) * CZ, lane] = jnp.where(
                            layer, part.astype(f32), 0.0
                        ).astype(bf16)
            for side_x in bricks.sides_x[step_x]:
                first_x, width_x, from_x = {
                    0: (HALO, CX, 0),
                    1: (HALO + CX, HALO, 0),
                    -1: (0, HALO, CX - HALO),
                }[side_x]
                for side_y in bricks.sides_y[step_y]:
                    first_y, width_y, from_y = {
                        0: (PAD, CY, 0),
                        1: (PAD + CY, PAD, 0),
                        -1: (0, PAD, CY - PAD),
                    }[side_y]
                    keys = [
                        jnp.where(
                            (y >= from_y) & (y < from_y + width_y), (x - from_x) * width_y + (y - from_y), -1
                        )
                        for x, y in cells_xy
                    ]
                    layers = min(width_x, 256 // width_y)
                    rows = layers * width_y
                    for start in range(0, width_x, layers):
                        hot = jnp.concatenate(
                            [one_hot(key - start * width_y, rows) for key in keys], axis=1
                        )
                        sums = dot_nt(hot, columns[...])
                        sums = sums[:, : 2 * CZ] + sums[:, 2 * CZ :]
                        for layer in range(layers):
                            at = first_x + start + layer
                            piece = slice(layer * width_y, (layer + 1) * width_y)
                            put(field, (at, slice(first_y, first_y + width_y), slice(None)), sums[piece])
        return carry

    lax.fori_loop(0, plane // group, sources, 0)

    def pair_of(shape, dim):
        index = lax.broadcasted_iota(jnp.int32, shape, dim)
        return index // CZ, index % CZ

    square = (2 * CZ, 2 * CZ)
    (kind_from, z_from), (kind_to, z_to) = pair_of(square, 0), pair_of(square, 1)
    inner = parts_of(jnp.where(kind_from == kind_to, tap_of(jnp.abs(z_to - z_from)), 0.0), 2)
    shape = (4 * HALO, 2 * CZ)
    kind_from, z_from = pair_of(shape, 1)
    row_of = lax.broadcasted_iota(jnp.int32, shape, 0)
    layer = row_of % HALO
    layer = jnp.where(row_of < 2 * HALO, layer - REACH, layer + (CZ - 1))
    kind_to = row_of // HALO % 2
    outer = parts_of(jnp.where(kind_from == kind_to, tap_of(jnp.abs(layer - z_from)), 0.0), 2)
    inner_both = jnp.concatenate([inner[0], inner[0]], axis=0)
    outer_both = jnp.concatenate([outer[0], outer[0]], axis=1)
    wide = CY + 2 * PAD
    layers = 6 if (CX + 2 * HALO) % 6 == 0 else 1
    for start in range(0, CX + 2 * HALO, layers):
        parts = parts_of(field[start : start + layers].reshape(layers * wide, 2 * CZ), 2)
        both = jnp.concatenate(parts, axis=1)
        done = dot_nn(both, inner_both) + dot_nn(parts[0], inner[1])
        field[start : start + layers] = done.reshape(layers, wide, 2 * CZ)
        edge = dot_nt(outer_both, both) + dot_nt(outer[1], parts[0])
        for at in range(layers):
            row = jnp.concatenate(
                [edge[:, at * wide : (at + 1) * wide], jnp.zeros((4 * HALO, LANES - wide), f32)], axis=1
            )
            edges[start + at] = pltpu.roll(row, LANES - PAD, 1)

    for layer in range(CX + 2):
        along_x = filter_rows(lambda j: edges[layer + j])
        both = filter_rows(lambda j: pltpu.roll(along_x, (REACH - j) % LANES, 1))
        below[layer] = both[: 2 * HALO]
        above[layer] = both[2 * HALO :]


def fill(bricks, received, slots, after):
    plane = received.shape[0]
    group = 8 if plane % 8 == 0 else plane
    return pl.pallas_call(
        functools.partial(fill_kernel, bricks, group, slots),
        out_shape=[
            jax.ShapeDtypeStruct((CX + 2 * HALO, CY + 2 * PAD, 2 * CZ), f32),
            jax.ShapeDtypeStruct((CX + 2, 2 * HALO, LANES), f32),
            jax.ShapeDtypeStruct((CX + 2, 2 * HALO, LANES), f32),
        ],
        in_specs=[pl.BlockSpec(), pl.BlockSpec(memory_space=pl.ANY)],
        scratch_shapes=[
            pltpu.VMEM((4 * CZ, group * slots), bf16),
            pltpu.VMEM((CX + 2 * HALO, 4 * HALO, LANES), f32),
        ],
        compiler_params=pltpu.CompilerParams(vmem_limit_bytes=VMEM_LIMIT),
    )(received, after)


def smooth_kernel(field, below, above, turned, line):
    line[...] = jnp.zeros_like(line)
    wide = CY + PAD
    for layer in range(CX + 2):
        line[PAD : PAD + CY + 2 * PAD, :] = filter_rows(lambda j: field[layer + j])
        main = filter_rows(lambda j: line[2 * PAD + j - REACH : 2 * PAD + j - REACH + wide, :])
        before = filter_rows(lambda j: line[PAD + j - REACH : 2 * PAD + j - REACH, :])
        rest = jnp.zeros((LANES - wide - PAD, 2 * CZ), f32)
        flipped = jnp.concatenate([main, rest, before], axis=0).T
        for k in range(2):
            turned[layer, k, PAD : PAD + CZ, :] = flipped[k * CZ : (k + 1) * CZ]
            turned[layer, k, PAD - 1 : PAD, :] = below[layer, k * HALO + REACH - 1 : k * HALO + REACH, :]
            turned[layer, k, PAD + CZ : PAD + CZ + 1, :] = above[layer, k * HALO + 1 : k * HALO + 2, :]


def smooth(field, below, above):
    return pl.pallas_call(
        smooth_kernel,
        out_shape=jax.ShapeDtypeStruct((CX + 2, 2, CZ + 2 * PAD, LANES), f32),
        scratch_shapes=[pltpu.VMEM((CY + 5 * PAD, 2 * CZ), f32)],
        compiler_params=pltpu.CompilerParams(vmem_limit_bytes=VMEM_LIMIT),
    )(field, below, above)


def slope_kernel(turned, from_below, from_above, place, slopes, whole, table):
    plane, _, slots = slopes.shape
    lanes = lax.broadcasted_iota(jnp.int32, (CZ, LANES), 1)
    for layer in range(CX + 2):
        for k in range(2):
            whole[layer, k] = turned[layer, k]
            at = slice(PAD - 1, PAD - 1 + HALO)
            whole[layer, k, at, :] = whole[layer, k, at, :] + from_below[layer, k * HALO : (k + 1) * HALO, :]
            at = slice(PAD + CZ - REACH, PAD + CZ - REACH + HALO)
            whole[layer, k, at, :] = whole[layer, k, at, :] + from_above[layer, k * HALO : (k + 1) * HALO, :]
    for pair in range(CX // 2):
        for k in range(2):
            halves = []
            for layer in (1 + 2 * pair, 2 + 2 * pair):
                inner = slice(PAD, PAD + CZ)
                here = whole[layer, k, inner, :]
                halves.append(
                    (
                        whole[layer + 1, k, inner, :] - whole[layer - 1, k, inner, :],
                        pltpu.roll(here, LANES - 1, 1) - pltpu.roll(here, 1, 1),
                        whole[layer, k, PAD + 1 : PAD + 1 + CZ, :] - whole[layer, k, PAD - 1 : PAD - 1 + CZ, :],
                    )
                )
            for axis in range(3):
                both = 0.5 * jnp.where(lanes < CY, halves[0][axis], pltpu.roll(halves[1][axis], CY, 1))
                for at, part in enumerate(parts_of(both, 2)):
                    start = at * CX * CY + pair * LANES
                    table[(axis * 2 + k) * CZ : (axis * 2 + k + 1) * CZ, start : start + LANES] = part

    def source(p, carry):
        row = pl.ds(p, 1)
        hot = one_hot(place[0, row, :] * CY + place[1, row, :], CX * CY)
        picked = dot_nn(table[:, : CX * CY], hot) + dot_nn(table[:, CX * CY :], hot)
        depth = lax.broadcasted_iota(jnp.int32, (CZ, slots), 0) == place[2, row, :]
        for axis in range(3):
            steep = [
                jnp.sum(
                    jnp.where(depth, picked[(axis * 2 + k) * CZ : (axis * 2 + k + 1) * CZ], 0.0),
                    axis=0,
                    keepdims=True,
                )
                for k in range(2)
            ]
            joint = stiffness * (steep[0] + steep[1])
            for k in range(2):
                slopes[p, k * 3 + axis : k * 3 + axis + 1, :] = mixing * steep[1 - k] + joint
        return carry

    lax.fori_loop(0, plane, source, 0, unroll=8 if plane % 8 == 0 else 1)


def pick_slopes(turned, from_below, from_above, place):
    plane, slots = place.shape[1:]
    return pl.pallas_call(
        slope_kernel,
        out_shape=[
            jax.ShapeDtypeStruct((plane, 6, slots), f32),
            jax.ShapeDtypeStruct(turned.shape, f32),
        ],
        scratch_shapes=[pltpu.VMEM((6 * CZ, 2 * CX * CY), bf16)],
        compiler_params=pltpu.CompilerParams(vmem_limit_bytes=VMEM_LIMIT),
    )(turned, from_below, from_above, place)


def smoothed_kernel(whole, smoothed):
    for layer in range(CX):
        for k in range(2):
            smoothed[k, layer] = whole[layer + 1, k, PAD : PAD + CZ, :].T[:CY]


def smoothed_of(whole):
    return pl.pallas_call(
        smoothed_kernel,
        out_shape=jax.ShapeDtypeStruct((2, CX, CY, CZ), f32),
        compiler_params=pltpu.CompilerParams(vmem_limit_bytes=VMEM_LIMIT),
    )(whole)


def shifted(values, axis, step):
    count = lax.axis_size(axis)
    return lax.ppermute(values, axis, [((i + step) % count, i) for i in range(count)])


def to_rows(store, base, row):
    for tile in range(row.shape[1] // LANES):
        store[pl.ds(base + tile, 1), :] = row[:, tile * LANES : (tile + 1) * LANES]


def select(rows, picked):
    size = rows.shape[0]
    return [
        jnp.sum(jnp.where(rows, picked[at * size : (at + 1) * size], 0.0), axis=0, keepdims=True)
        for at in range(picked.shape[0] // size)
    ]


def is_row(high, size):
    return lax.broadcasted_iota(jnp.int32, (size, high.shape[1]), 0) == high


def counted(flags):
    lanes = lax.broadcasted_iota(jnp.int32, (LANES, 2 * LANES), 1)
    upto = (lax.broadcasted_iota(jnp.int32, (LANES, 2 * LANES), 0) <= lanes) | (lanes >= LANES)
    counts = dot_nn(flags.astype(bf16), jnp.where(upto, 1.0, 0.0).astype(bf16))
    before = jnp.zeros((1, LANES), f32)
    rows = []
    for row in range(flags.shape[0]):
        rows.append(counts[row : row + 1, :LANES] + before)
        before = before + counts[row : row + 1, LANES:]
    return rows


def chains_kernel(positions, bonds, after, anchor, hot, high, apart, steps, placed):
    beads = positions.shape[1]
    bead_rows = beads // LANES
    count = bonds.shape[1]
    chains = beads - count
    length = beads // chains
    ends = 2 * chains
    bond_step = chunk_of(count, 6)
    for axis in range(3):
        to_rows(anchor, axis * bead_rows, positions[axis : axis + 1, :])

    total = jnp.zeros((3 * bead_rows, LANES), f32)
    for j in range(count // bond_step):
        where = slice(j * bond_step, (j + 1) * bond_step)
        index = [bonds[side : side + 1, where] for side in range(2)]
        highs = [i // LANES for i in index]
        lows = [i - h * LANES for i, h in zip(index, highs)]
        for side in range(2):
            rows = is_row(highs[side], bead_rows)
            values = (jnp.ones((1, bond_step), f32), highs[1 - side].astype(f32), lows[1 - side].astype(f32))
            left = [jnp.where(rows, value, 0.0).astype(bf16) for value in values]
            total = total + dot_nt(jnp.concatenate(left, axis=0), one_hot(lows[side], LANES))
    single = total[:bead_rows] == 1.0
    around = (total[bead_rows : 2 * bead_rows] * LANES + total[2 * bead_rows :]).astype(jnp.int32)
    around_high = around // LANES
    table = jnp.concatenate([around_high, around - around_high * LANES], axis=0).astype(f32).astype(bf16)

    flags = jnp.where(single, 1.0, 0.0)
    ranks = counted(flags)
    rank = jnp.concatenate(
        [jnp.where(flags[row : row + 1] > 0.0, ranks[row] - 1.0, -LANES) for row in range(bead_rows)], axis=1
    ).astype(jnp.int32)
    rank_high = jnp.where(rank < 0, -1, rank // LANES)
    bead = lax.broadcasted_iota(jnp.int32, (1, beads), 1)
    end_rows = -(-ends // (8 * LANES)) * 8
    rows = is_row(rank_high, end_rows)
    left = [jnp.where(rows, part.astype(f32), 0.0) for part in (bead // LANES, bead % LANES)]
    found = dot_nt(jnp.concatenate(left, axis=0).astype(bf16), one_hot(rank - rank_high * LANES, LANES))
    found = found[:end_rows] * LANES + found[end_rows:]
    first = jnp.concatenate([found[row : row + 1] for row in range(ends // LANES)], axis=1)

    def walk(m, carry):
        before, here = carry
        bead = here.astype(jnp.int32)
        bead_high = bead // LANES
        bead_low = bead - bead_high * LANES
        steps[pl.ds(m, 1), :] = bead_high.astype(f32)
        steps[pl.ds(length + m, 1), :] = bead_low.astype(f32)
        next_high, next_low = select(is_row(bead_high, bead_rows), dot_nn(table, one_hot(bead_low, LANES)))
        return here, next_high * LANES + next_low - before

    last, _ = lax.fori_loop(0, length, walk, (jnp.zeros_like(first), first))
    kept = jnp.where(first < last, 1.0, 0.0)
    flags = jnp.concatenate([kept[:, at : at + LANES] for at in range(0, ends, LANES)], axis=0)
    kept_rank = jnp.where(kept > 0.0, jnp.concatenate(counted(flags), axis=1) - 1.0, -1.0).astype(jnp.int32)
    order = dot_nt(steps[...].astype(bf16), one_hot(kept_rank, chains)).astype(jnp.int32)
    for m in range(length):
        where = slice(m * chains, (m + 1) * chains)
        high[:, where] = order[m : m + 1]
        hot[:, where] = one_hot(order[length + m : length + m + 1], LANES)

    anchor_table = jnp.concatenate(parts_of(anchor[...], 3), axis=1)
    wide = 4 * chains
    for j in range(beads // wide):
        where = slice(j * wide, (j + 1) * wide)
        rows = is_row(high[:, where], bead_rows)
        found = select(rows, dot_nn(anchor_table, jnp.concatenate([hot[:, where]] * 3, axis=0)))
        for axis in range(3):
            for at in range(4):
                placed[axis, 4 * j + at : 4 * j + at + 1, :] = found[axis][:, at * chains : (at + 1) * chains]
    for axis in range(3):
        apart[axis, : length - 1, :] = placed[axis, : length - 1, :] - placed[axis, 1:, :]
        apart[axis, length - 1 :, :] = jnp.zeros((1, chains), f32)


def order_chains(positions, bonds, after):
    beads = positions.shape[1]
    chains = beads - bonds.shape[1]
    length = beads // chains
    return pl.pallas_call(
        chains_kernel,
        out_shape=[
            jax.ShapeDtypeStruct((3 * beads // LANES, LANES), f32),
            jax.ShapeDtypeStruct((LANES, beads), bf16),
            jax.ShapeDtypeStruct((1, beads), jnp.int32),
            jax.ShapeDtypeStruct((3, length, chains), f32),
        ],
        in_specs=[pl.BlockSpec(), pl.BlockSpec(), pl.BlockSpec(memory_space=pl.ANY)],
        scratch_shapes=[pltpu.VMEM((2 * length, 2 * chains), f32), pltpu.VMEM((3, length, chains), f32)],
        compiler_params=pltpu.CompilerParams(vmem_limit_bytes=VMEM_WIDE),
    )(positions, bonds, after)


def stage_kernel(*refs):
    count = (len(refs) - 2) // 2
    sources, targets, sems = refs[:count], refs[count + 1 : -1], refs[-1]
    copies = [
        pltpu.make_async_copy(source, target, sems.at[at]) for at, (source, target) in enumerate(zip(sources, targets))
    ]
    for copy in copies:
        copy.start()
    for copy in copies:
        copy.wait()


def stage(arrays, after):
    return pl.pallas_call(
        stage_kernel,
        out_shape=[jax.ShapeDtypeStruct(a.shape, a.dtype) for a in arrays],
        in_specs=[HBM] * len(arrays) + [pl.BlockSpec(memory_space=pl.ANY)],
        scratch_shapes=[pltpu.SemaphoreType.DMA((len(arrays),))],
        compiler_params=pltpu.CompilerParams(vmem_limit_bytes=VMEM_STAGE),
    )(*arrays, after)


def finish_kernel(
    species,
    corner_slot,
    corner_weight,
    velocities,
    anchor,
    hot,
    high,
    apart,
    slopes,
    new_positions,
    new_velocities,
    table,
    shift,
    placed,
):
    plane, _, slots = slopes.shape
    blocks = slots // LANES
    highs = 2 * blocks * plane
    beads = corner_weight.shape[1]
    bead_rows = beads // LANES
    length, chains = apart.shape[1:]
    step = chunk_of(beads, 4)

    def collect(brick, carry):
        for axis in range(3):
            for kind in range(2):
                for block in range(blocks):
                    row = pl.ds((axis * 2 * blocks + kind * blocks + block) * plane + brick, 1)
                    at = kind * 3 + axis
                    table[row, :] = slopes[brick, at : at + 1, block * LANES : (block + 1) * LANES]
        return carry

    lax.fori_loop(0, plane, collect, 0, unroll=plane <= 8)
    slope_table = jnp.concatenate(parts_of(table[...], 2), axis=1)

    def force_body(j, carry):
        where = pl.ds(pl.multiple_of(j * step, step), step)
        kind = species[:, where]
        total = jnp.zeros((3 * highs, step), f32)
        for corner in range(8):
            high, low = corner_keys(kind, corner_slot, corner, where, plane, blocks)
            weight = corner_weight[pl.ds(corner, 1), where]
            rows = lax.broadcasted_iota(jnp.int32, (highs, step), 0) == high
            weights = jnp.where(rows, weight, 0.0)
            hot_low = one_hot(low, LANES)
            picked = dot_nn(slope_table, jnp.concatenate([hot_low, hot_low], axis=0))
            total = total + picked * jnp.concatenate([weights] * 3, axis=0)
        for axis in range(3):
            force = -jnp.sum(total[axis * highs : (axis + 1) * highs], axis=0, keepdims=True)
            half = velocities[pl.ds(axis, 1), where] + 0.5 * time_step * force
            to_rows(shift, axis * bead_rows + j * (step // LANES), time_step * half)
        return carry

    lax.fori_loop(0, beads // step, force_body, 0)

    shift_table = jnp.concatenate(parts_of(shift[...], 2), axis=1)
    wide = 4 * chains
    for j in range(beads // wide):
        where = slice(j * wide, (j + 1) * wide)
        rows = is_row(high[:, where], bead_rows)
        found = select(rows, dot_nn(shift_table, jnp.concatenate([hot[:, where]] * 2, axis=0)))
        for axis in range(3):
            for at in range(4):
                placed[axis, 4 * j + at : 4 * j + at + 1, :] = found[axis][:, at * chains : (at + 1) * chains]
    between = [apart[axis] for axis in range(3)]
    before = [placed[axis] for axis in range(3)]
    moved = before
    for _ in range(SWEEPS):
        stretch = [between[axis] + (moved[axis] - pltpu.roll(moved[axis], length - 1, 0)) for axis in range(3)]
        excess = sum(s * s for s in stretch) - bond_length * bond_length
        along = sum(s * a for s, a in zip(stretch, between))
        factor = excess / (4.0 * jnp.maximum(along, 0.5 * bond_length * bond_length))
        pulls = [factor * between[axis] for axis in range(3)]
        moved = [moved[axis] - pulls[axis] + pltpu.roll(pulls[axis], 1, 0) for axis in range(3)]
    for axis in range(3):
        placed[axis] = moved[axis] - before[axis]
    total = jnp.zeros((6 * bead_rows, LANES), f32)
    for j in range(beads // wide):
        where = slice(j * wide, (j + 1) * wide)
        rows = is_row(high[:, where], bead_rows)
        parts = [
            parts_of(jnp.concatenate([placed[axis, 4 * j + at : 4 * j + at + 1, :] for at in range(4)], axis=1), 2)
            for axis in range(3)
        ]
        left = [
            jnp.where(rows, parts[axis][part].astype(f32), 0.0).astype(bf16) for part in range(2) for axis in range(3)
        ]
        total = total + dot_nt(jnp.concatenate(left, axis=0), hot[:, where])
    shift[...] = shift[...] + total[: 3 * bead_rows] + total[3 * bead_rows :]

    for axis in range(3):
        for tile in range(bead_rows):
            row = slice(axis * bead_rows + tile, axis * bead_rows + tile + 1)
            where = slice(tile * LANES, (tile + 1) * LANES)
            move = shift[row, :]
            new_positions[axis : axis + 1, where] = anchor[row, :] + move
            new_velocities[axis : axis + 1, where] = move / time_step


def finish(near, slopes):
    beads = near[3].shape[1]
    plane, _, slots = slopes.shape
    highs = 2 * (slots // LANES) * plane
    return pl.pallas_call(
        finish_kernel,
        out_shape=[jax.ShapeDtypeStruct((3, beads), f32)] * 2,
        scratch_shapes=[
            pltpu.VMEM((3 * highs, LANES), f32),
            pltpu.VMEM((3 * beads // LANES, LANES), f32),
            pltpu.VMEM(near[7].shape, f32),
        ],
        compiler_params=pltpu.CompilerParams(vmem_limit_bytes=VMEM_LIMIT),
    )(*near, slopes)


def on_device(positions, velocities, species, corner_slot, corner_weight, slot_cell, bond_pairs):
    slots = slot_cell.shape[2]
    bricks = Bricks(lax.axis_size("bx"), lax.axis_size("by"))
    species = species.reshape(1, -1)
    packets = deposit(bricks, species, corner_slot, corner_weight, slot_cell)
    received = lax.all_to_all(packets, ("bx", "by"), split_axis=0, concat_axis=0, tiled=True)
    prepared = order_chains(positions, bond_pairs, packets)
    field, below, above = fill(bricks, received, slots, prepared[3])
    from_above = shifted(below, "bz", 1)
    from_below = shifted(above, "bz", -1)
    turned = smooth(field, below, above)
    slopes, whole = pick_slopes(turned, from_below, from_above, slot_cell)
    returned = lax.all_to_all(slopes, ("bx", "by"), split_axis=0, concat_axis=0, tiled=True)
    smoothed = smoothed_of(whole)
    near = stage((species, corner_slot, corner_weight, velocities, *prepared), slopes)
    moved, new_velocities = finish(near, returned)
    return (moved, new_velocities, smoothed)


def solution(mesh):
    in_specs = (
        P(None, ("bx", "by", "bz")),
        P(None, ("bx", "by", "bz")),
        P(("bx", "by", "bz")),
        P(None, None, ("bx", "by", "bz")),
        P(None, ("bx", "by", "bz")),
        P(None, ("bx", "by", "bz"), None),
        P(None, ("bx", "by", "bz")),
    )
    out_specs = (
        P(None, ("bx", "by", "bz")),
        P(None, ("bx", "by", "bz")),
        P(None, "bx", "by", "bz"),
    )
    return jax.shard_map(
        on_device, mesh=mesh, in_specs=in_specs, out_specs=out_specs, check_vma=False
    )
```

```python
import functools
import math

import jax
import jax.numpy as jnp
from jax import lax
from jax.experimental import pallas as pl
from jax.experimental.pallas import tpu as pltpu
from jax.sharding import PartitionSpec as P

CX = 16
CY = 64
CZ = 64
BEADS_DEV = 4096
REACH = 3
SWEEPS = 4


spread_cells = 1.0
mixing = 10.0
stiffness = 5.0
time_step = 0.1
bond_length = 1.0


def gauss_taps():
    raw_list = [
        math.exp(-0.5 * (offset - REACH) ** 2 / spread_cells**2) for offset in range(2 * REACH + 1)
    ]
    tap_total = sum(raw_list)
    return [entry / tap_total for entry in raw_list]


LANES = 128
VMEM_LIMIT = 20 * 1024 * 1024
VMEM_STAGE = 4 * 1024 * 1024
VMEM_WIDE = 60 * 1024 * 1024
HBM = pl.BlockSpec(memory_space=pltpu.HBM)
f32 = jnp.float32
bf16 = jnp.bfloat16


def parts_of(values, count):
    parts = []
    for _ in range(count):
        part = values.astype(bf16)
        parts.append(part)
        values = values - part.astype(f32)
    return parts


def one_hot(index, size):
    rows = lax.broadcasted_iota(jnp.int16, (size, index.shape[1]), 0)
    return jnp.where(rows == index.astype(jnp.int16), jnp.array(1, bf16), jnp.array(0, bf16))


def dot_nn(left, right):
    return lax.dot_general(left, right, (((1,), (0,)), ((), ())), preferred_element_type=f32)


def dot_nt(left, right):
    return lax.dot_general(left, right, (((1,), (1,)), ((), ())), preferred_element_type=f32)


def chunk_of(length, most):
    tiles = length // LANES
    best = max(t for t in range(1, most + 1) if tiles % t == 0)
    return best * LANES


def chunk_copies(pairs, sems, step, count):
    def copies(j):
        where = pl.ds(pl.multiple_of(j * step, step), step)
        for at, (source, target) in enumerate(pairs):
            lead = (slice(None),) * (len(source.shape) - 1)
            yield pltpu.make_async_copy(source.at[lead + (where,)], target.at[lead + (where,)], sems.at[at, j])

    def start(j, carry):
        for copy in copies(j):
            copy.start()
        return carry

    lax.fori_loop(0, count, start, 0, unroll=True)

    def wait(j):
        for copy in copies(j):
            copy.wait()

    return wait


def corner_keys(species, corner_slot, corner, where, plane, blocks):
    brick = corner_slot[0, pl.ds(corner, 1), where]
    slot = corner_slot[1, pl.ds(corner, 1), where]
    block = slot // LANES
    high = (species * blocks + block) * plane + brick
    return high, slot - block * LANES


def deposit_kernel(
    bricks,
    species_far,
    corner_slot_far,
    corner_weight_far,
    slot_cell_far,
    packets,
    sums,
    species,
    corner_slot,
    corner_weight,
    slot_cell,
    sems,
    cell_sem,
):
    plane, slots = slot_cell.shape[1:]
    blocks = slots // LANES
    highs = 2 * blocks * plane
    beads = corner_weight.shape[1]
    step = chunk_of(beads, 32 if plane <= 8 else 8)
    count_x, count_y = bricks.counts
    wait = chunk_copies(
        [(species_far, species), (corner_slot_far, corner_slot), (corner_weight_far, corner_weight)],
        sems,
        step,
        beads // step,
    )
    cell_copy = pltpu.make_async_copy(slot_cell_far, slot_cell, cell_sem)
    cell_copy.start()

    def body(j, total):
        wait(j)
        where = pl.ds(pl.multiple_of(j * step, step), step)
        kind = species[:, where]
        for corner in range(8):
            high, low = corner_keys(kind, corner_slot, corner, where, plane, blocks)
            weight = corner_weight[pl.ds(corner, 1), where]
            rows = lax.broadcasted_iota(jnp.int32, (highs, step), 0) == high
            left = [jnp.where(rows, p.astype(f32), 0.0).astype(bf16) for p in parts_of(weight, 2)]
            total = total + dot_nt(one_hot(low, LANES), jnp.concatenate(left, axis=0))
        return total

    total = lax.fori_loop(0, beads // step, body, jnp.zeros((LANES, 2 * highs), f32)).T
    sums[...] = total[:highs] + total[highs:]
    cell_copy.wait()
    cells = (slot_cell[0] * CY + slot_cell[1]) * CZ + slot_cell[2]
    first = 2 * blocks * len(bricks.offsets)

    def hand_out(target, carry):
        for near, (step_x, step_y) in enumerate(bricks.offsets):
            brick = lax.rem(target // count_y + step_x, count_x) * count_y + lax.rem(
                lax.rem(target, count_y) + step_y, count_y
            )
            for kind in range(2):
                for block in range(blocks):
                    row = (near * 2 + kind) * blocks + block
                    packets[target, row : row + 1, :] = sums[
                        pl.ds((kind * blocks + block) * plane + brick, 1), :
                    ]
        for block in range(blocks):
            rows = slice(first + block * plane, first + (block + 1) * plane)
            packets[target, rows, :] = cells[:, block * LANES : (block + 1) * LANES].astype(f32)
        return carry

    lax.fori_loop(0, plane, hand_out, 0, unroll=plane <= 8)


def deposit(bricks, species, corner_slot, corner_weight, slot_cell):
    plane, slots = slot_cell.shape[1:]
    blocks = slots // LANES
    rows = blocks * (2 * len(bricks.offsets) + plane)
    return pl.pallas_call(
        functools.partial(deposit_kernel, bricks),
        out_shape=jax.ShapeDtypeStruct((plane, rows, LANES), f32),
        in_specs=[HBM] * 4,
        scratch_shapes=[
            pltpu.VMEM((2 * blocks * plane, LANES), f32),
            pltpu.VMEM(species.shape, species.dtype),
            pltpu.VMEM(corner_slot.shape, corner_slot.dtype),
            pltpu.VMEM(corner_weight.shape, corner_weight.dtype),
            pltpu.VMEM(slot_cell.shape, slot_cell.dtype),
            pltpu.SemaphoreType.DMA((3, species.shape[1] // chunk_of(species.shape[1], 32 if plane <= 8 else 8))),
            pltpu.SemaphoreType.DMA(()),
        ],
        compiler_params=pltpu.CompilerParams(vmem_limit_bytes=VMEM_WIDE),
    )(species, corner_slot, corner_weight, slot_cell)


HALO = REACH + 1
PAD = 8


class Bricks:
    def __init__(self, count_x, count_y):
        self.counts = (count_x, count_y)
        self.sides_x = self.sides(count_x)
        self.sides_y = self.sides(count_y)
        self.offsets = [(x, y) for y in self.sides_y for x in self.sides_x]

    @staticmethod
    def sides(count):
        found = {}
        for side in (0, 1, -1):
            found.setdefault(side % count, []).append(side)
        return found


def tap_of(distance):
    taps = gauss_taps()
    result = jnp.zeros(distance.shape, f32)
    for far in range(REACH, -1, -1):
        result = jnp.where(distance == far, taps[REACH + far], result)
    return result


def filter_rows(load):
    taps = gauss_taps()
    result = taps[REACH] * load(REACH)
    for far in range(1, REACH + 1):
        result = result + taps[REACH + far] * (load(REACH - far) + load(REACH + far))
    return result


def fill_kernel(bricks, group, slots, received, after, field, below, above, columns, edges):
    plane = received.shape[0]
    blocks = slots // LANES
    first_cell = 2 * blocks * len(bricks.offsets)
    count_x, count_y = bricks.counts
    mine = (lax.axis_index("bx"), lax.axis_index("by"))
    scale = CX * CY * CZ / BEADS_DEV
    if plane > group:
        field[...] = jnp.zeros_like(field)

    def put(ref, index, value):
        if plane > group:
            value = value + ref[index]
        ref[index] = value

    def sources(g, carry):
        for near, (step_x, step_y) in enumerate(bricks.offsets):
            brick = lax.rem(mine[0] + step_x, count_x) * count_y + lax.rem(mine[1] + step_y, count_y)
            cells_xy = []
            for p in range(group):
                source = g * group + p
                cell = jnp.concatenate(
                    [received[brick, pl.ds(first_cell + block * plane + source, 1), :] for block in range(blocks)],
                    axis=1,
                ).astype(jnp.int32)
                cells_xy.append((cell // (CY * CZ), cell // CZ % CY))
                z = cell % CZ
                amounts = []
                for k in range(2):
                    row = (near * 2 + k) * blocks
                    amounts.append(
                        scale
                        * jnp.concatenate(
                            [received[source, row + block : row + block + 1, :] for block in range(blocks)], axis=1
                        )
                    )
                layer = lax.broadcasted_iota(jnp.int32, (CZ, slots), 0) == z
                lane = slice(p * slots, (p + 1) * slots)
                for k in range(2):
                    for at, part in enumerate(parts_of(amounts[k], 2)):
                        columns[at * 2 * CZ + k * CZ : at * 2 * CZ + (k + 1) * CZ, lane] = jnp.where(
                            layer, part.astype(f32), 0.0
                        ).astype(bf16)
            for side_x in bricks.sides_x[step_x]:
                first_x, width_x, from_x = {
                    0: (HALO, CX, 0),
                    1: (HALO + CX, HALO, 0),
                    -1: (0, HALO, CX - HALO),
                }[side_x]
                for side_y in bricks.sides_y[step_y]:
                    first_y, width_y, from_y = {
                        0: (PAD, CY, 0),
                        1: (PAD + CY, PAD, 0),
                        -1: (0, PAD, CY - PAD),
                    }[side_y]
                    keys = [
                        jnp.where(
                            (y >= from_y) & (y < from_y + width_y), (x - from_x) * width_y + (y - from_y), -1
                        )
                        for x, y in cells_xy
                    ]
                    layers = min(width_x, 256 // width_y)
                    rows = layers * width_y
                    for start in range(0, width_x, layers):
                        hot = jnp.concatenate(
                            [one_hot(key - start * width_y, rows) for key in keys], axis=1
                        )
                        sums = dot_nt(hot, columns[...])
                        sums = sums[:, : 2 * CZ] + sums[:, 2 * CZ :]
                        for layer in range(layers):
                            at = first_x + start + layer
                            piece = slice(layer * width_y, (layer + 1) * width_y)
                            put(field, (at, slice(first_y, first_y + width_y), slice(None)), sums[piece])
        return carry

    lax.fori_loop(0, plane // group, sources, 0)

    def pair_of(shape, dim):
        index = lax.broadcasted_iota(jnp.int32, shape, dim)
        return index // CZ, index % CZ

    square = (2 * CZ, 2 * CZ)
    (kind_from, z_from), (kind_to, z_to) = pair_of(square, 0), pair_of(square, 1)
    inner = parts_of(jnp.where(kind_from == kind_to, tap_of(jnp.abs(z_to - z_from)), 0.0), 2)
    shape = (4 * HALO, 2 * CZ)
    kind_from, z_from = pair_of(shape, 1)
    row_of = lax.broadcasted_iota(jnp.int32, shape, 0)
    layer = row_of % HALO
    layer = jnp.where(row_of < 2 * HALO, layer - REACH, layer + (CZ - 1))
    kind_to = row_of // HALO % 2
    outer = parts_of(jnp.where(kind_from == kind_to, tap_of(jnp.abs(layer - z_from)), 0.0), 2)
    inner_both = jnp.concatenate([inner[0], inner[0]], axis=0)
    outer_both = jnp.concatenate([outer[0], outer[0]], axis=1)
    wide = CY + 2 * PAD
    layers = 6 if (CX + 2 * HALO) % 6 == 0 else 1
    for start in range(0, CX + 2 * HALO, layers):
        parts = parts_of(field[start : start + layers].reshape(layers * wide, 2 * CZ), 2)
        both = jnp.concatenate(parts, axis=1)
        done = dot_nn(both, inner_both) + dot_nn(parts[0], inner[1])
        field[start : start + layers] = done.reshape(layers, wide, 2 * CZ)
        edge = dot_nt(outer_both, both) + dot_nt(outer[1], parts[0])
        for at in range(layers):
            row = jnp.concatenate(
                [edge[:, at * wide : (at + 1) * wide], jnp.zeros((4 * HALO, LANES - wide), f32)], axis=1
            )
            edges[start + at] = pltpu.roll(row, LANES - PAD, 1)

    for layer in range(CX + 2):
        along_x = filter_rows(lambda j: edges[layer + j])
        both = filter_rows(lambda j: pltpu.roll(along_x, (REACH - j) % LANES, 1))
        below[layer] = both[: 2 * HALO]
        above[layer] = both[2 * HALO :]


def fill(bricks, received, slots, after):
    plane = received.shape[0]
    group = 8 if plane % 8 == 0 else plane
    return pl.pallas_call(
        functools.partial(fill_kernel, bricks, group, slots),
        out_shape=[
            jax.ShapeDtypeStruct((CX + 2 * HALO, CY + 2 * PAD, 2 * CZ), f32),
            jax.ShapeDtypeStruct((CX + 2, 2 * HALO, LANES), f32),
            jax.ShapeDtypeStruct((CX + 2, 2 * HALO, LANES), f32),
        ],
        in_specs=[pl.BlockSpec(), pl.BlockSpec(memory_space=pl.ANY)],
        scratch_shapes=[
            pltpu.VMEM((4 * CZ, group * slots), bf16),
            pltpu.VMEM((CX + 2 * HALO, 4 * HALO, LANES), f32),
        ],
        compiler_params=pltpu.CompilerParams(vmem_limit_bytes=VMEM_LIMIT),
    )(received, after)


def smooth_kernel(field, below, above, turned, line):
    line[...] = jnp.zeros_like(line)
    wide = CY + PAD
    for layer in range(CX + 2):
        line[PAD : PAD + CY + 2 * PAD, :] = filter_rows(lambda j: field[layer + j])
        main = filter_rows(lambda j: line[2 * PAD + j - REACH : 2 * PAD + j - REACH + wide, :])
        before = filter_rows(lambda j: line[PAD + j - REACH : 2 * PAD + j - REACH, :])
        rest = jnp.zeros((LANES - wide - PAD, 2 * CZ), f32)
        flipped = jnp.concatenate([main, rest, before], axis=0).T
        for k in range(2):
            turned[layer, k, PAD : PAD + CZ, :] = flipped[k * CZ : (k + 1) * CZ]
            turned[layer, k, PAD - 1 : PAD, :] = below[layer, k * HALO + REACH - 1 : k * HALO + REACH, :]
            turned[layer, k, PAD + CZ : PAD + CZ + 1, :] = above[layer, k * HALO + 1 : k * HALO + 2, :]


def smooth(field, below, above):
    return pl.pallas_call(
        smooth_kernel,
        out_shape=jax.ShapeDtypeStruct((CX + 2, 2, CZ + 2 * PAD, LANES), f32),
        scratch_shapes=[pltpu.VMEM((CY + 5 * PAD, 2 * CZ), f32)],
        compiler_params=pltpu.CompilerParams(vmem_limit_bytes=VMEM_LIMIT),
    )(field, below, above)


def slope_kernel(turned, from_below, from_above, place, slopes, whole, table):
    plane, _, slots = slopes.shape
    lanes = lax.broadcasted_iota(jnp.int32, (CZ, LANES), 1)
    for layer in range(CX + 2):
        for k in range(2):
            whole[layer, k] = turned[layer, k]
            at = slice(PAD - 1, PAD - 1 + HALO)
            whole[layer, k, at, :] = whole[layer, k, at, :] + from_below[layer, k * HALO : (k + 1) * HALO, :]
            at = slice(PAD + CZ - REACH, PAD + CZ - REACH + HALO)
            whole[layer, k, at, :] = whole[layer, k, at, :] + from_above[layer, k * HALO : (k + 1) * HALO, :]
    for pair in range(CX // 2):
        for k in range(2):
            halves = []
            for layer in (1 + 2 * pair, 2 + 2 * pair):
                inner = slice(PAD, PAD + CZ)
                here = whole[layer, k, inner, :]
                halves.append(
                    (
                        whole[layer + 1, k, inner, :] - whole[layer - 1, k, inner, :],
                        pltpu.roll(here, LANES - 1, 1) - pltpu.roll(here, 1, 1),
                        whole[layer, k, PAD + 1 : PAD + 1 + CZ, :] - whole[layer, k, PAD - 1 : PAD - 1 + CZ, :],
                    )
                )
            for axis in range(3):
                both = 0.5 * jnp.where(lanes < CY, halves[0][axis], pltpu.roll(halves[1][axis], CY, 1))
                for at, part in enumerate(parts_of(both, 2)):
                    start = at * CX * CY + pair * LANES
                    table[(axis * 2 + k) * CZ : (axis * 2 + k + 1) * CZ, start : start + LANES] = part

    def source(p, carry):
        row = pl.ds(p, 1)
        hot = one_hot(place[0, row, :] * CY + place[1, row, :], CX * CY)
        picked = dot_nn(table[:, : CX * CY], hot) + dot_nn(table[:, CX * CY :], hot)
        depth = lax.broadcasted_iota(jnp.int32, (CZ, slots), 0) == place[2, row, :]
        for axis in range(3):
            steep = [
                jnp.sum(
                    jnp.where(depth, picked[(axis * 2 + k) * CZ : (axis * 2 + k + 1) * CZ], 0.0),
                    axis=0,
                    keepdims=True,
                )
                for k in range(2)
            ]
            joint = stiffness * (steep[0] + steep[1])
            for k in range(2):
                slopes[p, k * 3 + axis : k * 3 + axis + 1, :] = mixing * steep[1 - k] + joint
        return carry

    lax.fori_loop(0, plane, source, 0, unroll=8 if plane % 8 == 0 else 1)


def pick_slopes(turned, from_below, from_above, place):
    plane, slots = place.shape[1:]
    return pl.pallas_call(
        slope_kernel,
        out_shape=[
            jax.ShapeDtypeStruct((plane, 6, slots), f32),
            jax.ShapeDtypeStruct(turned.shape, f32),
        ],
        scratch_shapes=[pltpu.VMEM((6 * CZ, 2 * CX * CY), bf16)],
        compiler_params=pltpu.CompilerParams(vmem_limit_bytes=VMEM_LIMIT),
    )(turned, from_below, from_above, place)


def smoothed_kernel(whole, smoothed):
    for layer in range(CX):
        for k in range(2):
            smoothed[k, layer] = whole[layer + 1, k, PAD : PAD + CZ, :].T[:CY]


def smoothed_of(whole):
    return pl.pallas_call(
        smoothed_kernel,
        out_shape=jax.ShapeDtypeStruct((2, CX, CY, CZ), f32),
        compiler_params=pltpu.CompilerParams(vmem_limit_bytes=VMEM_LIMIT),
    )(whole)


def shifted(values, axis, step):
    count = lax.axis_size(axis)
    return lax.ppermute(values, axis, [((i + step) % count, i) for i in range(count)])


def to_rows(store, base, row):
    for tile in range(row.shape[1] // LANES):
        store[pl.ds(base + tile, 1), :] = row[:, tile * LANES : (tile + 1) * LANES]


def select(rows, picked):
    size = rows.shape[0]
    return [
        jnp.sum(jnp.where(rows, picked[at * size : (at + 1) * size], 0.0), axis=0, keepdims=True)
        for at in range(picked.shape[0] // size)
    ]


def is_row(high, size):
    return lax.broadcasted_iota(jnp.int32, (size, high.shape[1]), 0) == high


def counted(flags):
    lanes = lax.broadcasted_iota(jnp.int32, (LANES, 2 * LANES), 1)
    upto = (lax.broadcasted_iota(jnp.int32, (LANES, 2 * LANES), 0) <= lanes) | (lanes >= LANES)
    counts = dot_nn(flags.astype(bf16), jnp.where(upto, 1.0, 0.0).astype(bf16))
    before = jnp.zeros((1, LANES), f32)
    rows = []
    for row in range(flags.shape[0]):
        rows.append(counts[row : row + 1, :LANES] + before)
        before = before + counts[row : row + 1, LANES:]
    return rows


def chains_kernel(positions, bonds, after, anchor, hot, high, apart, steps, placed):
    beads = positions.shape[1]
    bead_rows = beads // LANES
    count = bonds.shape[1]
    chains = beads - count
    length = beads // chains
    ends = 2 * chains
    bond_step = chunk_of(count, 6)
    for axis in range(3):
        to_rows(anchor, axis * bead_rows, positions[axis : axis + 1, :])

    total = jnp.zeros((3 * bead_rows, LANES), f32)
    for j in range(count // bond_step):
        where = slice(j * bond_step, (j + 1) * bond_step)
        index = [bonds[side : side + 1, where] for side in range(2)]
        highs = [i // LANES for i in index]
        lows = [i - h * LANES for i, h in zip(index, highs)]
        for side in range(2):
            rows = is_row(highs[side], bead_rows)
            values = (jnp.ones((1, bond_step), f32), highs[1 - side].astype(f32), lows[1 - side].astype(f32))
            left = [jnp.where(rows, value, 0.0).astype(bf16) for value in values]
            total = total + dot_nt(jnp.concatenate(left, axis=0), one_hot(lows[side], LANES))
    single = total[:bead_rows] == 1.0
    around = (total[bead_rows : 2 * bead_rows] * LANES + total[2 * bead_rows :]).astype(jnp.int32)
    around_high = around // LANES
    table = jnp.concatenate([around_high, around - around_high * LANES], axis=0).astype(f32).astype(bf16)

    flags = jnp.where(single, 1.0, 0.0)
    ranks = counted(flags)
    rank = jnp.concatenate(
        [jnp.where(flags[row : row + 1] > 0.0, ranks[row] - 1.0, -LANES) for row in range(bead_rows)], axis=1
    ).astype(jnp.int32)
    rank_high = jnp.where(rank < 0, -1, rank // LANES)
    bead = lax.broadcasted_iota(jnp.int32, (1, beads), 1)
    end_rows = -(-ends // (8 * LANES)) * 8
    rows = is_row(rank_high, end_rows)
    left = [jnp.where(rows, part.astype(f32), 0.0) for part in (bead // LANES, bead % LANES)]
    found = dot_nt(jnp.concatenate(left, axis=0).astype(bf16), one_hot(rank - rank_high * LANES, LANES))
    found = found[:end_rows] * LANES + found[end_rows:]
    first = jnp.concatenate([found[row : row + 1] for row in range(ends // LANES)], axis=1)

    def walk(m, carry):
        before, here = carry
        bead = here.astype(jnp.int32)
        bead_high = bead // LANES
        bead_low = bead - bead_high * LANES
        steps[pl.ds(m, 1), :] = bead_high.astype(f32)
        steps[pl.ds(length + m, 1), :] = bead_low.astype(f32)
        next_high, next_low = select(is_row(bead_high, bead_rows), dot_nn(table, one_hot(bead_low, LANES)))
        return here, next_high * LANES + next_low - before

    last, _ = lax.fori_loop(0, length, walk, (jnp.zeros_like(first), first))
    kept = jnp.where(first < last, 1.0, 0.0)
    flags = jnp.concatenate([kept[:, at : at + LANES] for at in range(0, ends, LANES)], axis=0)
    kept_rank = jnp.where(kept > 0.0, jnp.concatenate(counted(flags), axis=1) - 1.0, -1.0).astype(jnp.int32)
    order = dot_nt(steps[...].astype(bf16), one_hot(kept_rank, chains)).astype(jnp.int32)
    for m in range(length):
        where = slice(m * chains, (m + 1) * chains)
        high[:, where] = order[m : m + 1]
        hot[:, where] = one_hot(order[length + m : length + m + 1], LANES)

    anchor_table = jnp.concatenate(parts_of(anchor[...], 3), axis=1)
    wide = 4 * chains
    for j in range(beads // wide):
        where = slice(j * wide, (j + 1) * wide)
        rows = is_row(high[:, where], bead_rows)
        found = select(rows, dot_nn(anchor_table, jnp.concatenate([hot[:, where]] * 3, axis=0)))
        for axis in range(3):
            for at in range(4):
                placed[axis, 4 * j + at : 4 * j + at + 1, :] = found[axis][:, at * chains : (at + 1) * chains]
    for axis in range(3):
        apart[axis, : length - 1, :] = placed[axis, : length - 1, :] - placed[axis, 1:, :]
        apart[axis, length - 1 :, :] = jnp.zeros((1, chains), f32)


def order_chains(positions, bonds, after):
    beads = positions.shape[1]
    chains = beads - bonds.shape[1]
    length = beads // chains
    return pl.pallas_call(
        chains_kernel,
        out_shape=[
            jax.ShapeDtypeStruct((3 * beads // LANES, LANES), f32),
            jax.ShapeDtypeStruct((LANES, beads), bf16),
            jax.ShapeDtypeStruct((1, beads), jnp.int32),
            jax.ShapeDtypeStruct((3, length, chains), f32),
        ],
        in_specs=[pl.BlockSpec(), pl.BlockSpec(), pl.BlockSpec(memory_space=pl.ANY)],
        scratch_shapes=[pltpu.VMEM((2 * length, 2 * chains), f32), pltpu.VMEM((3, length, chains), f32)],
        compiler_params=pltpu.CompilerParams(vmem_limit_bytes=VMEM_WIDE),
    )(positions, bonds, after)


def stage_kernel(*refs):
    count = (len(refs) - 2) // 2
    sources, targets, sems = refs[:count], refs[count + 1 : -1], refs[-1]
    copies = [
        pltpu.make_async_copy(source, target, sems.at[at]) for at, (source, target) in enumerate(zip(sources, targets))
    ]
    for copy in copies:
        copy.start()
    for copy in copies:
        copy.wait()


def stage(arrays, after):
    return pl.pallas_call(
        stage_kernel,
        out_shape=[jax.ShapeDtypeStruct(a.shape, a.dtype) for a in arrays],
        in_specs=[HBM] * len(arrays) + [pl.BlockSpec(memory_space=pl.ANY)],
        scratch_shapes=[pltpu.SemaphoreType.DMA((len(arrays),))],
        compiler_params=pltpu.CompilerParams(vmem_limit_bytes=VMEM_STAGE),
    )(*arrays, after)


def finish_kernel(
    species,
    corner_slot,
    corner_weight,
    velocities,
    anchor,
    hot,
    high,
    apart,
    slopes,
    new_positions,
    new_velocities,
    table,
    shift,
    placed,
):
    plane, _, slots = slopes.shape
    blocks = slots // LANES
    highs = 2 * blocks * plane
    beads = corner_weight.shape[1]
    bead_rows = beads // LANES
    length, chains = apart.shape[1:]
    step = chunk_of(beads, 8)

    def collect(brick, carry):
        for axis in range(3):
            for kind in range(2):
                for block in range(blocks):
                    row = pl.ds((axis * 2 * blocks + kind * blocks + block) * plane + brick, 1)
                    at = kind * 3 + axis
                    table[row, :] = slopes[brick, at : at + 1, block * LANES : (block + 1) * LANES]
        return carry

    lax.fori_loop(0, plane, collect, 0, unroll=plane <= 8)
    slope_table = jnp.concatenate(parts_of(table[...], 2), axis=1)

    def force_body(j, carry):
        where = pl.ds(pl.multiple_of(j * step, step), step)
        kind = species[:, where]
        total = jnp.zeros((3 * highs, step), f32)
        for corner in range(8):
            high, low = corner_keys(kind, corner_slot, corner, where, plane, blocks)
            weight = corner_weight[pl.ds(corner, 1), where]
            rows = lax.broadcasted_iota(jnp.int32, (highs, step), 0) == high
            weights = jnp.where(rows, weight, 0.0)
            hot_low = one_hot(low, LANES)
            picked = dot_nn(slope_table, jnp.concatenate([hot_low, hot_low], axis=0))
            total = total + picked * jnp.concatenate([weights] * 3, axis=0)
        for axis in range(3):
            force = -jnp.sum(total[axis * highs : (axis + 1) * highs], axis=0, keepdims=True)
            half = velocities[pl.ds(axis, 1), where] + 0.5 * time_step * force
            to_rows(shift, axis * bead_rows + j * (step // LANES), time_step * half)
        return carry

    lax.fori_loop(0, beads // step, force_body, 0, unroll=beads // step if plane <= 8 else 1)

    shift_table = jnp.concatenate(parts_of(shift[...], 2), axis=1)
    wide = 4 * chains
    for j in range(beads // wide):
        where = slice(j * wide, (j + 1) * wide)
        rows = is_row(high[:, where], bead_rows)
        found = select(rows, dot_nn(shift_table, jnp.concatenate([hot[:, where]] * 2, axis=0)))
        for axis in range(3):
            for at in range(4):
                placed[axis, 4 * j + at : 4 * j + at + 1, :] = found[axis][:, at * chains : (at + 1) * chains]
    between = [apart[axis] for axis in range(3)]
    before = [placed[axis] for axis in range(3)]
    moved = before
    for _ in range(SWEEPS):
        stretch = [between[axis] + (moved[axis] - pltpu.roll(moved[axis], length - 1, 0)) for axis in range(3)]
        excess = sum(s * s for s in stretch) - bond_length * bond_length
        along = sum(s * a for s, a in zip(stretch, between))
        factor = excess / (4.0 * jnp.maximum(along, 0.5 * bond_length * bond_length))
        pulls = [factor * between[axis] for axis in range(3)]
        moved = [moved[axis] - pulls[axis] + pltpu.roll(pulls[axis], 1, 0) for axis in range(3)]
    for axis in range(3):
        placed[axis] = moved[axis] - before[axis]
    total = jnp.zeros((6 * bead_rows, LANES), f32)
    for j in range(beads // wide):
        where = slice(j * wide, (j + 1) * wide)
        rows = is_row(high[:, where], bead_rows)
        parts = [
            parts_of(jnp.concatenate([placed[axis, 4 * j + at : 4 * j + at + 1, :] for at in range(4)], axis=1), 2)
            for axis in range(3)
        ]
        left = [
            jnp.where(rows, parts[axis][part].astype(f32), 0.0).astype(bf16) for part in range(2) for axis in range(3)
        ]
        total = total + dot_nt(jnp.concatenate(left, axis=0), hot[:, where])
    shift[...] = shift[...] + total[: 3 * bead_rows] + total[3 * bead_rows :]

    for axis in range(3):
        for tile in range(bead_rows):
            row = slice(axis * bead_rows + tile, axis * bead_rows + tile + 1)
            where = slice(tile * LANES, (tile + 1) * LANES)
            move = shift[row, :]
            new_positions[axis : axis + 1, where] = anchor[row, :] + move
            new_velocities[axis : axis + 1, where] = move / time_step


def finish(near, slopes):
    beads = near[3].shape[1]
    plane, _, slots = slopes.shape
    highs = 2 * (slots // LANES) * plane
    return pl.pallas_call(
        finish_kernel,
        out_shape=[jax.ShapeDtypeStruct((3, beads), f32)] * 2,
        scratch_shapes=[
            pltpu.VMEM((3 * highs, LANES), f32),
            pltpu.VMEM((3 * beads // LANES, LANES), f32),
            pltpu.VMEM(near[7].shape, f32),
        ],
        compiler_params=pltpu.CompilerParams(vmem_limit_bytes=VMEM_LIMIT),
    )(*near, slopes)


def on_device(positions, velocities, species, corner_slot, corner_weight, slot_cell, bond_pairs):
    slots = slot_cell.shape[2]
    bricks = Bricks(lax.axis_size("bx"), lax.axis_size("by"))
    species = species.reshape(1, -1)
    packets = deposit(bricks, species, corner_slot, corner_weight, slot_cell)
    received = lax.all_to_all(packets, ("bx", "by"), split_axis=0, concat_axis=0, tiled=True)
    prepared = order_chains(positions, bond_pairs, packets)
    field, below, above = fill(bricks, received, slots, prepared[3])
    from_above = shifted(below, "bz", 1)
    from_below = shifted(above, "bz", -1)
    turned = smooth(field, below, above)
    slopes, whole = pick_slopes(turned, from_below, from_above, slot_cell)
    returned = lax.all_to_all(slopes, ("bx", "by"), split_axis=0, concat_axis=0, tiled=True)
    smoothed = smoothed_of(whole)
    near = stage((species, corner_slot, corner_weight, velocities, *prepared), slopes)
    moved, new_velocities = finish(near, returned)
    return (moved, new_velocities, smoothed)


def solution(mesh):
    in_specs = (
        P(None, ("bx", "by", "bz")),
        P(None, ("bx", "by", "bz")),
        P(("bx", "by", "bz")),
        P(None, None, ("bx", "by", "bz")),
        P(None, ("bx", "by", "bz")),
        P(None, ("bx", "by", "bz"), None),
        P(None, ("bx", "by", "bz")),
    )
    out_specs = (
        P(None, ("bx", "by", "bz")),
        P(None, ("bx", "by", "bz")),
        P(None, "bx", "by", "bz"),
    )
    return jax.shard_map(
        on_device, mesh=mesh, in_specs=in_specs, out_specs=out_specs, check_vma=False
    )
```
